32 devices in a mesh: dp: 8 (over z, x), tensor: 4 (over y, core).
Axes of the slice: x: 2, y: 2, z: 4, core: 2. Of those that a mesh axis runs over, the one named last changes fastest.
Arguments:
- tokens: bfloat16 [16384, 512], P(('dp', 'tensor')), may hold values from -6 to 6
- routes: int32 [16384, 8], P('dp'), may hold values from 0 to 23, all different within a row; in each aligned block of 2048 rows (0 to 2047, 2048 to 4095, ...) at most 1024 rows name the same one
- cotangent: bfloat16 [16384, 512], P(('dp', 'tensor')), may hold values from -12 to 12
- ln1_gain: bfloat16 [512], P(('dp', 'tensor')), may hold values from 0.5 to 1.5
- ln1_bias: bfloat16 [512], P(('dp', 'tensor')), may hold values from -0.625 to 0.625
- w_key: bfloat16 [512, 64], P(('dp', 'tensor')), may hold values from -0.25 to 0.25
- w_value: bfloat16 [512, 64], P(('dp', 'tensor')), may hold values from -0.25 to 0.25
- w_router: bfloat16 [512, 24], P(('dp', 'tensor')), may hold values from -0.125 to 0.125
- w_query: bfloat16 [24, 512, 64], P('tensor', 'dp'), may hold values from -0.375 to 0.375
- w_out: bfloat16 [24, 64, 512], P('tensor', None, 'dp'), may hold values from -16 to 16
- ln2_gain: bfloat16 [512], P(('dp', 'tensor')), may hold values from 0.5 to 1.5
- ln2_bias: bfloat16 [512], P(('dp', 'tensor')), may hold values from -0.625 to 0.625
- w_up: bfloat16 [512, 2048], P('dp', 'tensor'), may hold values from -0.25 to 0.25
- b_up: bfloat16 [2048], P(('dp', 'tensor')), may hold values from -0.625 to 0.625
- w_down: bfloat16 [2048, 512], P('tensor', 'dp'), may hold values from -0.1875 to 0.1875
- b_down: bfloat16 [512], P(('dp', 'tensor')), may hold values from -0.625 to 0.625
Outputs:
- output: bfloat16 [16384, 512], P(('dp', 'tensor'))
- grad_tokens: float32 [16384, 512], P(('dp', 'tensor'))
- grad_ln1_gain: float32 [512], P(('dp', 'tensor'))
- grad_ln1_bias: float32 [512], P(('dp', 'tensor'))
- grad_w_key: float32 [512, 64], P(('dp', 'tensor'))
- grad_w_value: float32 [512, 64], P(('dp', 'tensor'))
- grad_w_router: float32 [512, 24], P(('dp', 'tensor'))
- grad_w_query: float32 [24, 512, 64], P('tensor', 'dp')
- grad_w_out: float32 [24, 64, 512], P('tensor', None, 'dp')
- grad_ln2_gain: float32 [512], P(('dp', 'tensor'))
- grad_ln2_bias: float32 [512], P(('dp', 'tensor'))
- grad_w_up: float32 [512, 2048], P('dp', 'tensor')
- grad_b_up: float32 [2048], P(('dp', 'tensor'))
- grad_w_down: float32 [2048, 512], P('tensor', 'dp')
- grad_b_down: float32 [512], P(('dp', 'tensor'))
The draws below stay inside these ranges and needn't reach their ends.
Inputs may be any that keep to these rules, and one draw needn't show every extreme that they name: `routes`: each row names 8 different experts. Among the 2048 rows of one sequence no expert is named by more than 1024 rows, and in every draw some expert is named by exactly 1024 rows of some sequence.
All inputs are finite; a program needn't handle non-finite values.
Results may differ from the reference program's by a relative error of at most 0.019.
Values may be sent and summed in bfloat16 or wider, within the bound.
No kernel may reach another device: no remote copies, remote signals or barrier semaphores. Data moves between devices by JAX's collectives and lax.ppermute only.
A program may use at most 128 MiB of HBM per device.

```python
import math
import jax
import jax.numpy as jnp
import numpy as np
from jax import lax

D = 512
HEAD = 64
EXPERTS = 24
TOPK = 8
FF = 2048
SEQ = 2048
ROWBLK = 512
CAP = 1024
TOKENS = 16384
N_DP = 8


def strengthened(values, stream_key, source, target, shards_of, factor):
    def block_of(axis_at):
        return (jnp.arange(values.shape[axis_at]) // (values.shape[axis_at] // shards_of)).reshape((-1,) + (1,) * (values.ndim - 1 - axis_at))

    first = jax.random.permutation(stream_key, shards_of)[block_of(target)]
    far = (block_of(target) + shards_of // 2) % shards_of
    return jnp.where((block_of(source) == first) | (block_of(source) == far), factor * values, values)


def steps_of(stream_key, dims, shards, low, largest):
    level = 1.0
    for axis_at, parts in shards:
        draws = jax.random.uniform(jax.random.fold_in(jax.random.fold_in(stream_key, 6), axis_at), (parts,), jnp.float32, low / len(shards), largest / len(shards))
        level = level * jnp.repeat(jnp.exp(draws), dims[axis_at] // parts).reshape((-1,) + (1,) * (len(dims) - 1 - axis_at))
    return level


def routed_block(stream_key, own, number, rows, number_of, top, limit, skew):
    sequence = jax.random.permutation(stream_key, number_of)
    crowded, usual = portions_of(number_of, rows * top, limit, skew, True), portions_of(number_of, rows * top, limit, skew, False)
    places = jnp.arange(number_of)

    def named(lengths, offset_by):
        used = int((lengths > 0).sum())
        fixed = max(1, used // 4)
        moved = fixed + (places - fixed + offset_by * (used - fixed)) % max(1, number_of - fixed)
        return jnp.zeros((number_of,), jnp.int32).at[sequence[jnp.where(places < fixed, places, moved)]].set(jnp.asarray(lengths, jnp.int32))

    lengths = jnp.where(number % 4 == 0, named(crowded, number // 4), named(usual, number - number // 4 - 1))
    mixed = jax.random.permutation(jax.random.fold_in(own, 3), number_of)
    source_of, receiver = mixed[0:number_of // 2 * 2:2], mixed[1:number_of // 2 * 2:2]
    margin = jnp.minimum(lengths[source_of] - 1, limit - lengths[receiver]) // 2
    margin = jnp.where((source_of == sequence[0]) | (receiver == sequence[0]) | (lengths[receiver] == 0), 0, jnp.maximum(margin, 0))
    moved = jax.random.randint(jax.random.fold_in(own, 4), (number_of // 2,), 0, 1 << 20) % (margin + 1)
    lengths = lengths.at[source_of].add(-moved).at[receiver].add(moved)
    labels = jnp.searchsorted(jnp.cumsum(lengths), jnp.arange(rows * top), side="right").astype(jnp.int32)
    listing = labels.reshape(top, rows).T
    listing = listing[jax.random.permutation(jax.random.fold_in(own, 1), rows)]
    offset_by = jax.random.randint(jax.random.fold_in(own, 2), (rows, 1), 0, top)
    return jnp.take_along_axis(listing, (jnp.arange(top)[None, :] + offset_by) % top, axis=1)


def portions_of(count, total, most, slope, full):
    portions = [(1 << 20) // math.isqrt(rank ** slope) + 1 for rank in range(1, count + 1)]
    largest = most if full else min(most, max(-(-total // count), total * portions[0] // sum(portions)))
    least = 1 if total - largest >= count - 1 else 0
    given, spare = [largest] + [least] * (count - 1), total - largest - least * (count - 1)
    while spare > 0:
        movable = [i for i in range(1, count) if given[i] < largest] or [i for i in range(1, count) if given[i] < most]
        whole, remaining = sum([portions[i] for i in movable]), spare
        for i in movable:
            more = min(most - given[i], max(1, remaining * portions[i] // whole), spare)
            given[i] = given[i] + more
            spare = spare - more
    return np.array(given)


def scatter_about(stream_key, shape, deviation, reach, cuts=(), kind=jnp.bfloat16):
    level = steps_of(stream_key, shape, cuts, -0.22, 0.18) if cuts else 1.0
    drawn = jax.random.normal(stream_key, shape, jnp.float32) * deviation * level
    return jnp.minimum(jnp.maximum(drawn, -reach), reach).astype(kind)


def noise_with(key, dims, width, bound, cuts, heavy, kind=jnp.bfloat16):
    drawn = width * jax.random.normal(key, dims, jnp.float32)
    if cuts:
        drawn = drawn * steps_of(key, dims, cuts, -0.22, 0.18)
    return jnp.clip(strengthened(drawn, jax.random.fold_in(key, 3), *heavy), -bound, bound).astype(kind)


def setup_inputs(seed: int = 0) -> dict:
    keys = jax.random.split(jax.random.key(seed), 17)
    tokens = scatter_about(keys[0], (TOKENS, D), 1.0, 6.0, ((0, 32),))
    routes_keys = jax.random.split(jax.random.fold_in(keys[1], 1), TOKENS // SEQ)
    routes_turns = jax.random.permutation(jax.random.fold_in(keys[1], 3), TOKENS // SEQ)
    routes = jax.vmap(lambda own, number: routed_block(jax.random.fold_in(keys[1], 2), own, number, SEQ, EXPERTS, TOPK, CAP, 1))(routes_keys, routes_turns).reshape((TOKENS, TOPK))
    cotangent = noise_with(keys[2], (TOKENS, D), 1.0, 12.0, ((0, 32),), (0, 1, 32, 2.75))
    ln1_gain = jnp.clip(1.0 + 0.1 * jax.random.normal(keys[3], (D,), jnp.float32), 0.5, 1.5).astype(jnp.bfloat16)
    ln1_bias = scatter_about(keys[4], (D,), 0.1, 0.625, ((0, 32),))
    w_key = scatter_about(keys[5], (D, HEAD), D ** -0.5, 0.25, ((0, 32),))
    w_value = scatter_about(keys[6], (D, HEAD), D ** -0.5, 0.25, ((0, 32),))
    w_router = scatter_about(keys[7], (D, EXPERTS), (4 * D) ** -0.5, 0.125, ((0, 32),))
    w_query = scatter_about(keys[8], (EXPERTS, D, HEAD), (4 * D // 9) ** -0.5, 0.375, ((0, 4), (1, 8)))
    w_out = scatter_about(keys[9], (EXPERTS, HEAD, D), 3.0, 16.0, ((0, 4), (2, 8)))
    ln2_gain = jnp.clip(1.0 + 0.1 * jax.random.normal(keys[10], (D,), jnp.float32), 0.5, 1.5).astype(jnp.bfloat16)
    ln2_bias = scatter_about(keys[11], (D,), 0.1, 0.625, ((0, 32),))
    w_up = scatter_about(keys[12], (D, FF), D ** -0.5, 0.25, ((0, 8), (1, 4)))
    b_up = scatter_about(keys[13], (FF,), 0.1, 0.625, ((0, 32),))
    w_down = scatter_about(keys[14], (FF, D), (FF // 2) ** -0.5, 0.1875, ((0, 4), (1, 8)))
    b_down = scatter_about(keys[15], (D,), 0.1, 0.625, ((0, 32),))
    return dict(tokens=tokens, routes=routes, cotangent=cotangent, ln1_gain=ln1_gain, ln1_bias=ln1_bias, w_key=w_key, w_value=w_value, w_router=w_router, w_query=w_query, w_out=w_out, ln2_gain=ln2_gain, ln2_bias=ln2_bias, w_up=w_up, b_up=b_up, w_down=w_down, b_down=b_down)


@jax.custom_vjp
def low(v):
    return lax.optimization_barrier(v.astype(jnp.bfloat16)).astype(jnp.float32)

@jax.custom_vjp
def low_back(v):
    return v

def low_keep(v):
    return (low(v), None)

def low_pass(kept, grad):
    return (grad,)

def back_keep(v):
    return (v, None)

def back_low(kept, grad):
    return (low(grad),)
low.defvjp(low_keep, low_pass)
low_back.defvjp(back_keep, back_low)

def rounded_both(operand):
    return low_back(low(operand))

def matmul(left, right):
    return jnp.dot(left, right, precision=lax.Precision.HIGHEST)

def layer_norm(operand, gain, offset):
    average = lax.optimization_barrier(jnp.mean(operand, axis=-1, keepdims=True))
    centered = operand - average
    variance = lax.optimization_barrier(jnp.mean(centered * centered, axis=-1, keepdims=True))
    return centered * lax.rsqrt(variance + 1e-05) * gain + offset

def slot_table(route_rows):
    expert_range = jnp.arange(EXPERTS, dtype=jnp.int32)
    picked = route_rows[:, :, None] == expert_range[None, None, :]
    member = jnp.any(picked, axis=1).astype(jnp.int32)
    running = jnp.cumsum(member, axis=0).astype(jnp.int32)
    slot_range = jnp.arange(CAP, dtype=jnp.int32)
    token_of = jax.vmap(lambda column: jnp.searchsorted(column, slot_range, side='right'))(running.T).astype(jnp.int32)
    filled = slot_range[None, :] < running[-1][:, None]
    return (picked.astype(jnp.float32), jnp.minimum(token_of, SEQ - 1), filled)

def attend_block(query_rows, position_rows, key_rows, value_rows):
    scores = low_back(matmul(query_rows, key_rows.T) * 0.125)
    allowed = jnp.arange(SEQ, dtype=jnp.int32)[None, :] <= position_rows[:, None]
    scores = jnp.where(allowed, scores, -1e+30)
    weights = low(jax.nn.softmax(scores, axis=-1))
    return matmul(weights, value_rows)

def forward_sequence(layer_input, route_rows, params):
    ln1_gain, ln1_bias, w_key, w_value, w_router, w_query, w_out, ln2_gain, ln2_bias, w_up, b_up, w_down, b_down = params
    picked, token_of, filled = slot_table(route_rows)
    normed = low(layer_norm(layer_input, ln1_gain, ln1_bias))
    key_rows = rounded_both(matmul(normed, w_key))
    value_rows = rounded_both(matmul(normed, w_value))
    queries = rounded_both(jnp.einsum('td,edh->teh', normed, w_query, precision=lax.Precision.HIGHEST))
    logits = matmul(normed, w_router)
    chosen = lax.optimization_barrier(jnp.sum(picked * logits[:, None, :], axis=-1))
    gate_rows = jax.nn.softmax(chosen, axis=-1)
    token_gate = lax.optimization_barrier(jnp.sum(gate_rows[:, :, None] * picked, axis=1))
    expert_col = jnp.arange(EXPERTS, dtype=jnp.int32)[:, None]
    slot_query = queries[token_of, expert_col]
    slot_gate = token_gate[token_of, expert_col] * filled.astype(jnp.float32)
    block_count = EXPERTS * CAP // ROWBLK
    checked = jax.checkpoint(attend_block)
    head_out = lax.map(lambda pieces: checked(pieces[0], pieces[1], key_rows, value_rows), (slot_query.reshape(block_count, ROWBLK, HEAD), token_of.reshape(block_count, ROWBLK)))
    head_out = low_back(head_out.reshape(EXPERTS, CAP, HEAD))
    weighted = low(slot_gate[:, :, None] * head_out)
    mixed_rows = jnp.zeros((SEQ, EXPERTS, HEAD), jnp.float32).at[token_of, expert_col].add(weighted)
    attention = low_back(matmul(mixed_rows.reshape(SEQ, EXPERTS * HEAD), w_out.reshape(EXPERTS * HEAD, D)))
    middle = layer_input + attention
    normed_two = low(layer_norm(middle, ln2_gain, ln2_bias))
    preact = low_back(matmul(normed_two, w_up) + b_up)
    hidden = low(jax.nn.silu(preact))
    return middle + matmul(hidden, w_down) + b_down

def reference(tokens, routes, cotangent, ln1_gain, ln1_bias, w_key, w_value, w_router, w_query, w_out, ln2_gain, ln2_bias, w_up, b_up, w_down, b_down):
    params = tuple((weight.astype(jnp.float32) for weight in (ln1_gain, ln1_bias, w_key, w_value, w_router, w_query, w_out, ln2_gain, ln2_bias, w_up, b_up, w_down, b_down)))
    sequences = (tokens.astype(jnp.float32).reshape(N_DP, SEQ, D), routes.reshape(N_DP, SEQ, TOPK), cotangent.astype(jnp.float32).reshape(N_DP, SEQ, D))

    def one_sequence(running_grads, pieces):
        input_rows, route_rows, grad_rows = pieces
        result, pull_back = jax.vjp(lambda operand, weights: forward_sequence(operand, route_rows, weights), input_rows, params)
        grad_input, grad_weights = pull_back(grad_rows)
        running_grads = jax.tree.map(lambda first_term, second_term: first_term + second_term, running_grads, grad_weights)
        return (running_grads, (result.astype(jnp.bfloat16), grad_input))
    start_grads = jax.tree.map(jnp.zeros_like, params)
    totals, (results, input_grads) = lax.scan(one_sequence, start_grads, sequences)
    return (results.reshape(TOKENS, D), input_grads.reshape(TOKENS, D), totals[0], totals[1], totals[2], totals[3], totals[4], totals[5], totals[6], totals[7], totals[8], totals[9], totals[10], totals[11], totals[12])
```

```python
import jax
import jax.numpy as jnp
from jax import lax
from jax.experimental import pallas as pl
from jax.experimental.pallas import tpu as pltpu
from jax.sharding import PartitionSpec as P

F32 = jnp.float32
BF16 = jnp.bfloat16
HEAD = 64
LANES = 128
HALF = 256
ROWS = 64
TINY = 16
CHUNK = 32
VMEM_MAX = 60 * 1024 * 1024

PLACES_A = ((0, 0, 0), (0, 0, 1), (1, 0, 0), (1, 0, 1))
PLACES_XA = tuple((y, 1, s) for y, _, s in PLACES_A)
PLACES_B = ((0, 0, 2), (0, 0, 3), (0, 1, 2), (0, 1, 3))
PLACES_YB = tuple((1, x, s) for _, x, s in PLACES_B)
LAYOUT = tuple(
    tuple((2 * y + core, 2 * s + x) for y, x, s in places)
    for core in (0, 1)
    for places in (PLACES_A, PLACES_XA, PLACES_B, PLACES_YB)
)
SLOT_AT, IN_AT, OUT_AT, POS_AT = 0, 4, 12, 20


def nn(left, right):
    return lax.dot_general(left, right, (((1,), (0,)), ((), ())), preferred_element_type=F32)


def nt(left, right):
    return lax.dot_general(left, right, (((1,), (1,)), ((), ())), preferred_element_type=F32)


def norm_parts(rows):
    average = jnp.mean(rows, axis=-1, keepdims=True)
    centered = rows - average
    inverse = lax.rsqrt(jnp.mean(centered * centered, axis=-1, keepdims=True) + 1e-05)
    return centered * inverse, inverse


def norm_backward(incoming, scaled, inverse, gain):
    weighted = incoming * gain
    return inverse * (
        weighted
        - jnp.mean(weighted, axis=-1, keepdims=True)
        - scaled * jnp.mean(weighted * scaled, axis=-1, keepdims=True)
    )


def any_spec():
    return pl.BlockSpec(memory_space=pl.ANY)


def smem_spec():
    return pl.BlockSpec(memory_space=pltpu.SMEM)


def params():
    return pltpu.CompilerParams(vmem_limit_bytes=VMEM_MAX)


def shaped(shape, kind):
    return jax.ShapeDtypeStruct(shape, kind)


def pack_kernel(
    wq, wo, wup, wdown, wk, wv, wr, g1, b1, g2, b2, bdown, bup, first_ref, second_ref, wide, square
):
    experts = wq.shape[0]
    group = experts * HEAD
    hidden = wup.shape[1]
    first_ref[...] = jnp.zeros_like(first_ref)
    for j in range(experts):
        first_ref[0:ROWS, j * HEAD : (j + 1) * HEAD] = wq[j]
    square[...] = jnp.zeros_like(square)
    for i, vector in enumerate((g1, b1, g2, b2, bdown)):
        square[24 + i : 25 + i, 0:TINY] = vector[...].astype(F32)
    columns = square[...].T
    first_ref[ROWS : ROWS + TINY, 0:HEAD] = wk[...]
    first_ref[ROWS : ROWS + TINY, HEAD : 2 * HEAD] = wv[...]
    first_ref[ROWS : ROWS + TINY, LANES : 2 * LANES] = columns[0:TINY, :].astype(BF16)
    first_ref[ROWS : ROWS + TINY, LANES : LANES + wr.shape[1]] = wr[...]
    first_ref[ROWS : ROWS + 1, 2 * LANES : 2 * LANES + HEAD] = bup[...]
    wide[...] = jnp.zeros_like(wide)
    for j in range(experts):
        wide[j * HEAD : (j + 1) * HEAD, 0:ROWS] = wo[j].astype(F32)
    second_ref[:, 0:group] = wide[0:group, :].T[0:ROWS].astype(BF16)
    second_ref[:, group : group + hidden] = wup[...]
    wide[0:hidden, 0:ROWS] = wdown[...].astype(F32)
    second_ref[:, group + hidden :] = wide[0:hidden, :].T[0:ROWS].astype(BF16)


def pack(wq, wo, wup, wdown, wk, wv, wr, vectors, bup):
    group, hidden = wq.shape[0] * HEAD, wup.shape[1]
    return pl.pallas_call(
        pack_kernel,
        out_shape=(
            shaped((ROWS + TINY, group), BF16),
            shaped((ROWS, group + 2 * hidden), BF16),
        ),
        scratch_shapes=[
            pltpu.VMEM((max(group, hidden), LANES), F32),
            pltpu.VMEM((LANES, LANES), F32),
        ],
        compiler_params=params(),
    )(wq, wo, wup, wdown, wk, wv, wr, *[v.reshape(1, -1) for v in vectors], bup.reshape(1, -1))


def sum_four(kept, one, two, three):
    return kept.astype(F32) + one.astype(F32) + two.astype(F32) + three.astype(F32)


def unpack_first_kernel(kept, one, two, three, gq, gk, gv, gr, v1, v2, v3, v4, v5, gb, total):
    total[...] = sum_four(kept[0], one[...], two[...], three[...])
    for j in range(gq.shape[0]):
        gq[j] = total[0:ROWS, j * HEAD : (j + 1) * HEAD]
    gk[...] = total[ROWS : ROWS + TINY, 0:HEAD]
    gv[...] = total[ROWS : ROWS + TINY, HEAD : 2 * HEAD]
    gr[...] = total[ROWS : ROWS + TINY, LANES : LANES + gr.shape[1]]
    square = jnp.concatenate(
        [total[ROWS : ROWS + TINY, LANES : 2 * LANES], jnp.zeros((LANES - TINY, LANES), F32)], axis=0
    ).T
    for i, out in enumerate((v1, v2, v3, v4, v5)):
        out[...] = square[24 + i : 25 + i, 0:TINY]
    gb[...] = total[ROWS : ROWS + 1, 2 * LANES : 2 * LANES + HEAD]


def unpack_first(kept, one, two, three, experts, routed):
    outs = pl.pallas_call(
        unpack_first_kernel,
        out_shape=(
            shaped((experts, ROWS, HEAD), F32),
            shaped((TINY, HEAD), F32),
            shaped((TINY, HEAD), F32),
            shaped((TINY, routed), F32),
            *[shaped((1, TINY), F32) for _ in range(5)],
            shaped((1, HEAD), F32),
        ),
        scratch_shapes=[pltpu.VMEM(kept.shape[1:], F32)],
        compiler_params=params(),
    )(kept, one, two, three)
    return outs[0], outs[1], outs[2], outs[3], [v.reshape(-1) for v in outs[4:9]], outs[9].reshape(-1)


def unpack_second_kernel(kept, one, two, three, go, gup, gdown, total, wide):
    experts = go.shape[0]
    group, hidden = experts * HEAD, gup.shape[1]
    total[...] = sum_four(kept[0], one[...], two[...], three[...])
    gup[...] = total[:, group : group + hidden]
    wide[...] = jnp.zeros_like(wide)
    wide[0:ROWS, 0:group] = total[:, 0:group]
    turned = wide[:, 0:group].T
    for j in range(experts):
        go[j] = turned[j * HEAD : (j + 1) * HEAD, 0:ROWS]
    wide[0:ROWS, 0:hidden] = total[:, group + hidden :]
    gdown[...] = wide[:, 0:hidden].T[:, 0:ROWS]


def unpack_second(kept, one, two, three, experts, hidden):
    group = experts * HEAD
    return pl.pallas_call(
        unpack_second_kernel,
        out_shape=(
            shaped((experts, HEAD, ROWS), F32),
            shaped((ROWS, hidden), F32),
            shaped((hidden, ROWS), F32),
        ),
        scratch_shapes=[
            pltpu.VMEM(kept.shape[1:], F32),
            pltpu.VMEM((LANES, max(group, hidden)), F32),
        ],
        compiler_params=params(),
    )(kept, one, two, three)


def axis_moves(dp):
    turns = [
        [(d, (d + 2 * step) % dp) for d in range(dp)] for step in range(1, dp // 2)
    ]
    return turns, [(d, d ^ 1) for d in range(dp)]


CORE = [(0, 1), (1, 0), (2, 3), (3, 2)]
ACROSS = [(0, 2), (2, 0), (1, 3), (3, 1)]
CROSSED = [(0, 3), (3, 0), (1, 2), (2, 1)]


def over_core(x):
    return lax.ppermute(x, "tensor", CORE)


def over_y(x):
    return lax.ppermute(x, "tensor", ACROSS)


def crossed(x):
    return lax.ppermute(x, "tensor", CROSSED)


def gather_blocks(own, dp):
    turns, swap = axis_moves(dp)

    def over_x(x):
        return lax.ppermute(x, "dp", swap)

    own = own[None]
    one, two, three = [lax.ppermute(own, "dp", turn) for turn in turns]
    first = jnp.concatenate([own, one, over_y(own), over_y(one)], axis=0)
    second = jnp.concatenate([two, three, over_x(two), over_x(three)], axis=0)
    mine = [first, over_x(first), second, over_y(second)]
    return mine + [over_core(x) for x in mine]


def add_low(*terms):
    total = terms[0].astype(F32)
    for term in terms[1:]:
        total = total + term.astype(F32)
    return total.astype(BF16)


def reduce_blocks(keep_a, keep_b, send_a, send_b, dp):
    turns, swap = axis_moves(dp)

    def over_x(x):
        return lax.ppermute(x, "dp", swap)

    got_a, got_b = over_core(send_a), over_core(send_b)
    next_a = over_y(add_low(keep_a[1], got_a[1]))
    next_b = over_x(add_low(keep_b[1], got_b[1]))
    last_a = over_x(add_low(keep_a[0, 1], got_a[0, 1], next_a[1]))
    last_b = over_y(add_low(keep_b[0, 1], got_b[0, 1], next_b[1]))
    done_a = add_low(keep_a[0, 0], got_a[0, 0], next_a[0], last_a)
    done_b = add_low(keep_b[0, 0], got_b[0, 0], next_b[0], last_b)
    return (
        done_a,
        lax.ppermute(done_a[1], "dp", turns[0]),
        lax.ppermute(done_b[0], "dp", turns[1]),
        lax.ppermute(done_b[1], "dp", turns[2]),
    )


def block_copies(table, pieces, row_from, rows, stride, target, sems):
    copies = []
    for a, (piece, places) in enumerate(zip(pieces, LAYOUT)):
        for i, (slot, place) in enumerate(places):
            source = piece.at[i, pl.ds(row_from, rows), :]
            block = table[IN_AT + place]
            if stride is None:
                into = target.at[slot, pl.ds(pl.multiple_of(block * rows, rows), rows), :]
            else:
                row = (block * stride + table[SLOT_AT + slot]) * rows
                into = target.at[pl.ds(pl.multiple_of(row, rows), rows), :]
            copies.append(pltpu.make_async_copy(source, into, sems.at[a, i]))
    return copies


def first_kernel(table, low_tok, high_tok, routes, *refs):
    pieces, (normed_ref, kv_ref, gates_ref, small, vectors, up_bias, sems) = refs[:8], refs[8:]
    copies = block_copies(table, pieces, ROWS, TINY, 4, small, sems)
    for copy in copies:
        copy.start()
    tokens = jnp.concatenate([low_tok[0:HALF, :], high_tok[...]], axis=0).astype(F32)
    scaled, _ = norm_parts(tokens)
    for copy in copies:
        copy.wait()
    turned = small[:, LANES : 2 * LANES].astype(F32).T
    vectors[...] = turned[24:32, :]
    for i in range(32):
        up_bias[i // 8 : i // 8 + 1, (i % 8) * HEAD : (i % 8 + 1) * HEAD] = small[
            TINY * i : TINY * i + 1, 2 * LANES : 2 * LANES + HEAD
        ].astype(F32)
    normed = (scaled * vectors[0:1, :] + vectors[1:2, :]).astype(BF16)
    normed_ref[...] = normed
    kv_ref[...] = nn(normed, small[:, 0:LANES]).astype(BF16)
    logits = nn(normed, small[:, LANES : 2 * LANES])
    lane = lax.broadcasted_iota(jnp.int32, logits.shape, 1)
    ways = routes.shape[1]
    chosen = [lane == routes[:, k : k + 1] for k in range(ways)]
    member = chosen[0]
    for k in range(1, ways):
        member = member | chosen[k]
    logits = jnp.where(member, logits, -jnp.inf)
    exponent = jnp.exp(logits - jnp.max(logits, axis=-1, keepdims=True))
    shares = exponent / jnp.sum(exponent, axis=-1, keepdims=True)
    gates = jnp.zeros_like(shares)
    for k in range(ways):
        gate = jnp.sum(jnp.where(chosen[k], shares, 0.0), axis=-1, keepdims=True)
        gates = jnp.where(lane == k, gate, gates)
    gates_ref[...] = gates


def first_stage(table, tokens, tokens_high, routes, pieces):
    rows, width = tokens.shape
    return pl.pallas_call(
        first_kernel,
        in_specs=[smem_spec()] + [pl.BlockSpec(memory_space=pltpu.VMEM)] * 3 + [any_spec()] * 8,
        out_shape=(
            shaped((rows, width), BF16),
            shaped((rows, LANES), BF16),
            shaped((rows, LANES), F32),
            shaped((width, pieces[0].shape[2]), BF16),
            shaped((8, width), F32),
            shaped((8, width), F32),
        ),
        scratch_shapes=[pltpu.SemaphoreType.DMA((8, 4))],
        compiler_params=params(),
    )(table, tokens, tokens_high, routes, *pieces)


def half_routes(routes, k, at, half):
    return jnp.broadcast_to(routes[at, k : k + 1], half.shape) - half


def query_kernel(table, normed, routes, *refs):
    pieces, (chosen, weight, queries, sems) = refs[:8], refs[8:]
    experts = weight.shape[2] // HEAD
    copies = block_copies(table, pieces, 0, ROWS, None, weight, sems)
    for copy in copies:
        copy.start()
    for copy in copies:
        copy.wait()
    for slot in range(4):
        queries[slot] = nn(normed[...], weight[slot]).astype(BF16)
    ways = routes.shape[1]
    half = (lax.broadcasted_iota(jnp.int32, (CHUNK, LANES), 1) >= HEAD).astype(jnp.int32)

    def step(c, _):
        at = pl.ds(pl.multiple_of(c * CHUNK, CHUNK), CHUNK)
        wanted = [half_routes(routes, k, at, half) for k in range(ways)]
        picked = [jnp.zeros((CHUNK, LANES), F32)] * ways
        for slot in range(4):
            for pair in range(experts // 2):
                value = queries[slot, at, pair * LANES : (pair + 1) * LANES].astype(F32)
                base = experts * table[SLOT_AT + slot] + 2 * pair
                for k in range(ways):
                    picked[k] = jnp.where(wanted[k] == base, value, picked[k])
        for k in range(ways):
            chosen[k, at, :] = picked[k].astype(BF16)
        return 0

    lax.fori_loop(0, normed.shape[0] // CHUNK, step, 0)


def query_stage(table, normed, routes, pieces):
    rows, width = normed.shape
    group = pieces[0].shape[2]
    return pl.pallas_call(
        query_kernel,
        in_specs=[smem_spec()] + [pl.BlockSpec(memory_space=pltpu.VMEM)] * 2 + [any_spec()] * 8,
        out_shape=(
            shaped((routes.shape[1], rows, LANES), BF16),
            shaped((4, width, group), BF16),
        ),
        scratch_shapes=[
            pltpu.VMEM((4, rows, group), BF16),
            pltpu.SemaphoreType.DMA((8, 4)),
        ],
        compiler_params=params(),
    )(table, normed, routes, *pieces)


def place_pair(table, pieces, key_scr, value_scr, ones):
    lower = lax.broadcasted_iota(jnp.int32, (HALF, LANES), 1) < HEAD
    for p, piece in enumerate(pieces):
        for h in range(2):
            both = piece[h * HALF : (h + 1) * HALF, :].astype(F32)
            turned = pltpu.roll(both, HEAD, 1)
            at = pl.ds(pl.multiple_of(table[POS_AT + 2 * p + h] * HALF, HALF), HALF)
            key_scr[at, :] = (jnp.where(lower, both, turned) * 0.125).astype(BF16)
            value_scr[at, 0:LANES] = jnp.where(lower, turned, both).astype(BF16)
            if ones:
                value_scr[at, LANES : 2 * LANES] = jnp.ones((HALF, LANES), BF16)


def causal_mask():
    shape = (HALF, HALF)
    return lax.broadcasted_iota(jnp.int32, shape, 1) <= lax.broadcasted_iota(jnp.int32, shape, 0)


def attend_kernel(table, query, kv0, kv1, kv2, kv3, out_ref, total_ref, keys, values, scores, tops, sums):
    block = pl.program_id(0)
    ways = query.shape[0]

    @pl.when(block == 0)
    def _():
        place_pair(table, (kv0, kv1, kv2, kv3), keys, values, True)

    last = table[POS_AT + block]
    tops[...] = jnp.full_like(tops, -jnp.inf)

    def score(at, masked):
        rows = pl.ds(pl.multiple_of(at * HALF, HALF), HALF)
        keys_here = keys[rows, :]
        for k in range(ways):
            here = nt(query[k], keys_here)
            if masked:
                here = jnp.where(causal_mask(), here, -1e30)
            scores[at, k] = here
            tops[k] = jnp.maximum(tops[k], jnp.maximum(here[:, 0:LANES], here[:, LANES:]))

    lax.fori_loop(0, last, lambda at, _: (score(at, False), 0)[1], 0)
    score(last, True)
    for k in range(ways):
        tops[k] = jnp.broadcast_to(jnp.max(tops[k], axis=-1, keepdims=True), (HALF, LANES))
    sums[...] = jnp.zeros_like(sums)

    def weigh(at, _):
        rows = pl.ds(pl.multiple_of(at * HALF, HALF), HALF)
        values_here = values[rows, :]
        for k in range(ways):
            top = tops[k]
            here = scores[at, k]
            weights = jnp.concatenate(
                [jnp.exp(here[:, 0:LANES] - top), jnp.exp(here[:, LANES:] - top)], axis=1
            ).astype(BF16)
            sums[k] += nn(weights, values_here)
        return 0

    lax.fori_loop(0, last + 1, weigh, 0)
    for k in range(ways):
        whole = sums[k]
        out_ref[k] = whole[:, 0:LANES] / whole[:, LANES:]
        total_ref[k] = tops[k] + jnp.log(whole[:, LANES:])


def attend_stage(table, query, pairs, seq):
    ways, rows, _ = query.shape
    kv_spec = pl.BlockSpec((rows, LANES), lambda b: (0, 0))
    spec = pl.BlockSpec((ways, HALF, LANES), lambda b: (0, b, 0))
    return pl.pallas_call(
        attend_kernel,
        grid=(rows // HALF,),
        in_specs=[smem_spec(), spec] + [kv_spec] * 4,
        out_specs=(spec, spec),
        out_shape=(shaped((ways, rows, LANES), F32), shaped((ways, rows, LANES), F32)),
        scratch_shapes=[
            pltpu.VMEM((seq, LANES), BF16),
            pltpu.VMEM((seq, 2 * LANES), BF16),
            pltpu.VMEM((seq // HALF, ways, HALF, HALF), F32),
            pltpu.VMEM((ways, HALF, LANES), F32),
            pltpu.VMEM((ways, HALF, 2 * LANES), F32),
        ],
        compiler_params=params(),
    )(table, query, *pairs)


def attend_back_kernel(
    table, query, grad, totals, inner, kv0, kv1, kv2, kv3, grad_query, *refs
):
    outs, (keys, values, key_sum, value_sum, query_sum, query_t, grad_t, probs, scored) = refs[:4], refs[4:]
    block = pl.program_id(0)
    ways = query.shape[0]

    @pl.when(block == 0)
    def _():
        place_pair(table, (kv0, kv1, kv2, kv3), keys, values, False)
        key_sum[...] = jnp.zeros_like(key_sum)
        value_sum[...] = jnp.zeros_like(value_sum)

    last = table[POS_AT + block]
    query_sum[...] = jnp.zeros_like(query_sum)
    for k in range(ways):
        query_t[:, k * HALF : (k + 1) * HALF] = query[k].T
        grad_t[:, k * HALF : (k + 1) * HALF] = grad[k].T

    def step(at, masked):
        rows = pl.ds(pl.multiple_of(at * HALF, HALF), HALF)
        keys_here = keys[rows, :]
        values_here = values[rows, :]
        for k in range(ways):
            score = nt(query[k], keys_here)
            total, mean = totals[k], inner[k]
            prob = jnp.concatenate(
                [jnp.exp(score[:, 0:LANES] - total), jnp.exp(score[:, LANES:] - total)], axis=1
            )
            if masked:
                prob = jnp.where(causal_mask(), prob, 0.0)
            grad_prob = nt(grad[k], values_here)
            grad_score = prob * (grad_prob - jnp.concatenate([mean, mean], axis=1))
            probs[k * HALF : (k + 1) * HALF, :] = prob.astype(BF16)
            scored[k * HALF : (k + 1) * HALF, :] = grad_score.astype(BF16)
        query_sum[...] += nn(scored[...], keys_here)
        key_sum[at] += nn(query_t[...], scored[...])
        value_sum[at] += nn(grad_t[...], probs[...])

    lax.fori_loop(0, last, lambda at, _: (step(at, False), 0)[1], 0)
    step(last, True)
    for k in range(ways):
        grad_query[k] = query_sum[k * HALF : (k + 1) * HALF, :].astype(BF16)

    @pl.when(block == pl.num_programs(0) - 1)
    def _():
        for p, out in enumerate(outs):
            for h in range(2):
                at = table[POS_AT + 2 * p + h]
                key_part, value_part = key_sum[at], value_sum[at]
                out[h, 0:HEAD, :] = ((key_part[0:HEAD] + key_part[HEAD:]) * 0.125).astype(BF16)
                out[h, HEAD:, :] = (value_part[0:HEAD] + value_part[HEAD:]).astype(BF16)


def attend_back_stage(table, query, grad, totals, inner, pairs, seq):
    ways, rows, _ = query.shape
    kv_spec = pl.BlockSpec((rows, LANES), lambda b: (0, 0))
    spec = pl.BlockSpec((ways, HALF, LANES), lambda b: (0, b, 0))
    pair_spec = pl.BlockSpec((2, LANES, HALF), lambda b: (0, 0, 0))
    return pl.pallas_call(
        attend_back_kernel,
        grid=(rows // HALF,),
        in_specs=[smem_spec()] + [spec] * 4 + [kv_spec] * 4,
        out_specs=(spec,) + (pair_spec,) * 4,
        out_shape=(shaped((ways, rows, LANES), BF16),) + (shaped((2, LANES, HALF), BF16),) * 4,
        scratch_shapes=[
            pltpu.VMEM((seq, LANES), BF16),
            pltpu.VMEM((seq, LANES), BF16),
            pltpu.VMEM((seq // HALF, LANES, HALF), F32),
            pltpu.VMEM((seq // HALF, LANES, HALF), F32),
            pltpu.VMEM((ways * HALF, LANES), F32),
            pltpu.VMEM((LANES, ways * HALF), BF16),
            pltpu.VMEM((LANES, ways * HALF), BF16),
            pltpu.VMEM((ways * HALF, HALF), BF16),
            pltpu.VMEM((ways * HALF, HALF), BF16),
        ],
        compiler_params=params(),
    )(table, query, grad, totals, inner, *pairs)


def put_blocks(table, grads, outs, slot, rows, row_to, column_to, slot_stride):
    keep_a, keep_b, send_a, send_b = outs
    y, core = slot // 2, slot % 2
    wide = grads.shape[1]
    for s in range(4):
        for x in range(2):
            at = table[OUT_AT + 2 * s + x]
            if slot_stride:
                at = at * slot_stride + table[SLOT_AT + slot]
            block = grads[pl.ds(pl.multiple_of(at * rows, rows), rows), :]
            if s < 2:
                out, place = (send_a if core else keep_a), (y, x, s)
            else:
                out, place = (send_b if core else keep_b), (x, y, s - 2)
            out[place[0], place[1], place[2], row_to : row_to + rows, column_to : column_to + wide] = block


def middle_kernel(table, low_tok, high_tok, low_cot, high_cot, heads, gates, routes, vectors, up_bias, *refs):
    pieces = refs[:8]
    output, grad_mid, grad_ref, inner, grad_gate, sums, bias_grad = refs[8:15]
    blocks = refs[15:19]
    weight, mixed, back, big, hid_scr, pre_scr, sems = refs[19:]
    ways, rows, _ = heads.shape
    width = low_tok.shape[1]
    group = mixed.shape[2]
    hidden = hid_scr.shape[1]
    experts = group // HEAD
    copies = block_copies(table, pieces, 0, ROWS, None, weight, sems)
    for copy in copies:
        copy.start()
    half = (lax.broadcasted_iota(jnp.int32, (CHUNK, LANES), 1) >= HEAD).astype(jnp.int32)
    lane = lax.broadcasted_iota(jnp.int32, (CHUNK, LANES), 1)

    def expand(c, _):
        at = pl.ds(pl.multiple_of(c * CHUNK, CHUNK), CHUNK)
        wanted = [half_routes(routes, k, at, half) for k in range(ways)]
        weighted = [
            (heads[k, at, :] * gates[at, k : k + 1]).astype(BF16).astype(F32) for k in range(ways)
        ]
        for slot in range(4):
            for pair in range(experts // 2):
                base = experts * table[SLOT_AT + slot] + 2 * pair
                value = jnp.zeros((CHUNK, LANES), F32)
                for k in range(ways):
                    value = jnp.where(wanted[k] == base, weighted[k], value)
                mixed[slot, at, pair * LANES : (pair + 1) * LANES] = value.astype(BF16)
        return 0

    lax.fori_loop(0, rows // CHUNK, expand, 0)
    for copy in copies:
        copy.wait()
    middle = jnp.concatenate([low_tok[0:HALF, :], high_tok[...]], axis=0).astype(F32)
    for slot in range(4):
        middle = middle + nt(mixed[slot], weight[slot, :, 0:group])
    scaled, inverse = norm_parts(middle)
    gain = vectors[2:3, :]
    normed = (scaled * gain + vectors[3:4, :]).astype(BF16)
    normed_t = normed.T
    cot = jnp.concatenate([low_cot[0:HALF, :], high_cot[...]], axis=0)
    cot_t = cot.T
    result = middle + vectors[4:5, :]
    grad_normed = jnp.zeros((rows, width), F32)
    up_at, down_at = group, group + hidden
    for slot in range(4):
        bias = up_bias[pl.ds(table[SLOT_AT + slot], 1), :]
        preact = nn(normed, weight[slot, :, up_at:down_at]) + bias
        share = jax.nn.sigmoid(preact)
        active = (preact * share).astype(BF16)
        hid_scr[...] = active
        slope = share * (1.0 + preact * (1.0 - share))
        grad_pre = (nn(cot, weight[slot, :, down_at:]) * slope).astype(BF16)
        pre_scr[...] = grad_pre
        bias_grad[pl.ds(table[SLOT_AT + slot], 1), :] = jnp.sum(
            grad_pre.astype(F32), axis=0, keepdims=True
        )
        result = result + nt(hid_scr[...], weight[slot, :, down_at:])
        grad_normed = grad_normed + nt(pre_scr[...], weight[slot, :, up_at:down_at])
        big[...] = nn(normed_t, pre_scr[...]).astype(BF16)
        put_blocks(table, big, blocks, slot, ROWS, 0, up_at, 0)
        big[...] = nn(cot_t, hid_scr[...]).astype(BF16)
        put_blocks(table, big, blocks, slot, ROWS, 0, down_at, 0)
    output[...] = result.astype(BF16)
    cot_wide = cot.astype(F32)
    sums[...] = jnp.zeros_like(sums)
    sums[2:3, :] = jnp.sum(grad_normed * scaled, axis=0, keepdims=True)
    sums[3:4, :] = jnp.sum(grad_normed, axis=0, keepdims=True)
    sums[4:5, :] = jnp.sum(cot_wide, axis=0, keepdims=True)
    grad_middle = cot_wide + norm_backward(grad_normed, scaled, inverse, gain)
    grad_mid[...] = grad_middle
    grad_attn = grad_middle.astype(BF16)
    grad_attn_t = grad_attn.T
    for slot in range(4):
        big[:, 0:group] = nn(grad_attn_t, mixed[slot]).astype(BF16)
        put_blocks(table, big.at[:, 0:group], blocks, slot, ROWS, 0, 0, 0)
        back[slot] = nn(grad_attn, weight[slot, :, 0:group])

    def select(c, _):
        at = pl.ds(pl.multiple_of(c * CHUNK, CHUNK), CHUNK)
        wanted = [half_routes(routes, k, at, half) for k in range(ways)]
        picked = [jnp.zeros((CHUNK, LANES), F32)] * ways
        for slot in range(4):
            for pair in range(experts // 2):
                value = back[slot, at, pair * LANES : (pair + 1) * LANES]
                base = experts * table[SLOT_AT + slot] + 2 * pair
                for k in range(ways):
                    picked[k] = jnp.where(wanted[k] == base, value, picked[k])
        gate_grads = jnp.zeros((CHUNK, LANES), F32)
        for k in range(ways):
            head = heads[k, at, :]
            gate_grad = jnp.sum(picked[k] * head, axis=-1, keepdims=True)
            gate_grads = jnp.where(lane == k, gate_grad, gate_grads)
            low = (picked[k] * gates[at, k : k + 1]).astype(BF16)
            grad_ref[k, at, :] = low
            inner[k, at, :] = jnp.broadcast_to(
                jnp.sum(low.astype(F32) * head, axis=-1, keepdims=True), (CHUNK, LANES)
            )
        grad_gate[at, :] = gate_grads
        return 0

    lax.fori_loop(0, rows // CHUNK, select, 0)


def middle_stage(table, tokens, tokens_high, cot, cot_high, heads, gates, routes, vectors, up_bias, pieces):
    rows, width = tokens.shape
    ways = heads.shape[0]
    packed = pieces[0].shape[2]
    hidden = up_bias.shape[1]
    group = packed - 2 * hidden
    block = shaped((2, 2, 2, ROWS, packed), BF16)
    vmem = pl.BlockSpec(memory_space=pltpu.VMEM)
    return pl.pallas_call(
        middle_kernel,
        in_specs=[smem_spec()] + [vmem] * 9 + [any_spec()] * 8,
        out_shape=(
            shaped((rows, width), BF16),
            shaped((rows, width), F32),
            shaped((ways, rows, LANES), BF16),
            shaped((ways, rows, LANES), F32),
            shaped((rows, LANES), F32),
            shaped((8, width), F32),
            shaped((8, hidden), F32),
            block,
            block,
            block,
            block,
        ),
        scratch_shapes=[
            pltpu.VMEM((4, width, packed), BF16),
            pltpu.VMEM((4, rows, group), BF16),
            pltpu.VMEM((4, rows, group), F32),
            pltpu.VMEM((width, hidden), BF16),
            pltpu.VMEM((rows, hidden), BF16),
            pltpu.VMEM((rows, hidden), BF16),
            pltpu.SemaphoreType.DMA((8, 4)),
        ],
        compiler_params=params(),
    )(table, tokens, tokens_high, cot, cot_high, heads, gates, routes, vectors, up_bias, *pieces)


def last_kernel(
    table, low_tok, high_tok, grad_mid, grad_query, normed, routes, gates, grad_gate, weight, small,
    vectors, sums, bias_grad, p0, p1, p2, p3, low_out, high_out, *refs
):
    blocks, (spread, pair_grad, big, tiny, wide, extra) = refs[:4], refs[4:]
    ways, rows, _ = grad_query.shape
    group = spread.shape[2]
    experts = group // HEAD
    half = (lax.broadcasted_iota(jnp.int32, (CHUNK, LANES), 1) >= HEAD).astype(jnp.int32)

    def expand(c, _):
        at = pl.ds(pl.multiple_of(c * CHUNK, CHUNK), CHUNK)
        wanted = [half_routes(routes, k, at, half) for k in range(ways)]
        held = [grad_query[k, at, :].astype(F32) for k in range(ways)]
        for slot in range(4):
            for pair in range(experts // 2):
                base = experts * table[SLOT_AT + slot] + 2 * pair
                value = jnp.zeros((CHUNK, LANES), F32)
                for k in range(ways):
                    value = jnp.where(wanted[k] == base, held[k], value)
                spread[slot, at, pair * LANES : (pair + 1) * LANES] = value.astype(BF16)
        return 0

    lax.fori_loop(0, rows // CHUNK, expand, 0)
    for h in range(2):
        total = sum_four(p0[h], p1[h], p2[h], p3[h])
        pair_grad[h * HALF : (h + 1) * HALF, :] = total.T.astype(BF16)
    gate = gates[...]
    gate_grad = grad_gate[...]
    chosen_grad = gate * (gate_grad - jnp.sum(gate * gate_grad, axis=-1, keepdims=True))
    lane = lax.broadcasted_iota(jnp.int32, (rows, LANES), 1)
    logit_grad = jnp.zeros((rows, LANES), F32)
    for k in range(ways):
        logit_grad = jnp.where(lane == routes[:, k : k + 1], chosen_grad[:, k : k + 1], logit_grad)
    logit_low = logit_grad.astype(BF16)
    normed_t = normed[...].T
    grad_normed = nt(pair_grad[...], small[:, 0:LANES]) + nt(logit_low, small[:, LANES : 2 * LANES])
    for slot in range(4):
        grad_normed = grad_normed + nt(spread[slot], weight[slot])
        big[...] = nn(normed_t, spread[slot]).astype(BF16)
        put_blocks(table, big, blocks, slot, ROWS, 0, 0, 0)
    tokens = jnp.concatenate([low_tok[0:HALF, :], high_tok[...]], axis=0).astype(F32)
    scaled, inverse = norm_parts(tokens)
    back = grad_mid[...] + norm_backward(grad_normed, scaled, inverse, vectors[0:1, :])
    low_out[...] = back[0:HALF]
    high_out[...] = back[HALF:].astype(BF16)
    wide[...] = jnp.zeros_like(wide)
    wide[24:32, :] = sums[...]
    wide[24:25, :] = jnp.sum(grad_normed * scaled, axis=0, keepdims=True)
    wide[25:26, :] = jnp.sum(grad_normed, axis=0, keepdims=True)
    tiny[:, 0:LANES] = nn(normed_t, pair_grad[...]).astype(BF16)
    tiny[:, LANES : 2 * LANES] = (nn(normed_t, logit_low) + wide[...].T).astype(BF16)
    extra[...] = jnp.zeros_like(extra)
    for i in range(32):
        extra[TINY * i : TINY * i + 1, 0:HEAD] = bias_grad[i // 8 : i // 8 + 1, (i % 8) * HEAD : (i % 8 + 1) * HEAD]
    tiny[:, 2 * LANES : 3 * LANES] = extra[...].astype(BF16)
    for slot in range(4):
        put_blocks(table, tiny, blocks, slot, TINY, ROWS, 0, 4)


def last_stage(
    table, tokens, tokens_high, grad_mid, grad_query, normed, routes, gates, grad_gate, weight, small,
    vectors, sums, bias_grad, pair_parts
):
    rows, width = tokens.shape
    group = weight.shape[2]
    block = shaped((2, 2, 2, ROWS + TINY, group), BF16)
    vmem = pl.BlockSpec(memory_space=pltpu.VMEM)
    return pl.pallas_call(
        last_kernel,
        in_specs=[smem_spec()] + [vmem] * 17,
        out_shape=(shaped((HALF, width), F32), shaped((rows - HALF, width), BF16), block, block, block, block),
        scratch_shapes=[
            pltpu.VMEM((4, rows, group), BF16),
            pltpu.VMEM((rows, LANES), BF16),
            pltpu.VMEM((width, group), BF16),
            pltpu.VMEM((width, 3 * LANES), BF16),
            pltpu.VMEM((LANES, width), F32),
            pltpu.VMEM((width, LANES), F32),
        ],
        compiler_params=params(),
    )(
        table, tokens, tokens_high, grad_mid, grad_query, normed, routes, gates, grad_gate, weight, small,
        vectors, sums, bias_grad, *pair_parts
    )


def gather_plain(x, axis, dim):
    return lax.all_gather(x, axis, axis=dim, tiled=True)


def general_pieces(wq, wo, wup, wdown, wk, wv, wr, vectors, bup):
    every = ("dp", "tensor")
    width = wup.shape[0] * lax.axis_size("dp")
    group = wq.shape[0] * HEAD

    def whole(rows):
        return lax.all_gather(gather_plain(rows, "dp", 0), "tensor", axis=0)

    queries = whole(wq.transpose(1, 0, 2).reshape(-1, group))
    second = whole(
        jnp.concatenate([wo.transpose(2, 0, 1).reshape(-1, group), wup, wdown.T], axis=1)
    )
    wide = [gather_plain(w, every, 0) for w in (wk, wv, wr)]
    columns = [gather_plain(v, every, 0)[:, None] for v in vectors]
    bias = jnp.pad(gather_plain(bup, every, 0).reshape(-1, 1, HEAD), ((0, 0), (0, TINY - 1), (0, 0)))
    left = jnp.concatenate(wide + columns, axis=1)
    small = jnp.concatenate(
        [jnp.pad(left, ((0, 0), (0, 2 * LANES - left.shape[1]))), bias.reshape(width, HEAD)], axis=1
    )
    small = jnp.pad(small, ((0, 0), (0, group - small.shape[1])))

    def block_one(slot, place):
        row = (4 * place + slot) * TINY
        return jnp.concatenate([queries[slot, place * ROWS : (place + 1) * ROWS], small[row : row + TINY]])

    first = [jnp.stack([block_one(*at) for at in places]) for places in LAYOUT]
    later = [
        jnp.stack([second[slot, place * ROWS : (place + 1) * ROWS] for slot, place in places])
        for places in LAYOUT
    ]
    return first, later


def general_sum(blocks):
    keep_a, keep_b, send_a, send_b = blocks
    slots = []
    for slot in range(4):
        y, core = slot // 2, slot % 2
        part_a, part_b = (send_a, send_b) if core else (keep_a, keep_b)
        slots.append(
            jnp.stack(
                [(part_a[y, x, s] if s < 2 else part_b[x, y, s - 2]) for s in range(4) for x in range(2)]
            )
        )
    return lax.psum(jnp.stack(slots), ("dp", "tensor")).astype(F32)


def general_grads(first, later, experts, hidden, routed):
    group = experts * HEAD
    d, t = lax.axis_index("dp"), lax.axis_index("tensor")
    dp = lax.axis_size("dp")
    width = 8 * ROWS
    first, later = general_sum(first), general_sum(later)
    mine = lax.dynamic_index_in_dim(first[:, :, 0:ROWS].reshape(4, width, group), t, 0, False)
    small = first[:, :, ROWS:].transpose(1, 0, 2, 3).reshape(width, group)
    rest = lax.dynamic_index_in_dim(later.reshape(4, width, -1), t, 0, False)
    rows = width // dp

    def own(x, length, index):
        return lax.dynamic_slice_in_dim(x, index * length, length, 0)

    query = own(mine, rows, d).reshape(rows, experts, HEAD).transpose(1, 0, 2)
    rest = own(rest, rows, d)
    index = d * 4 + t
    tiny = own(small, rows // 4, index)
    bias = small.reshape(32, TINY, group)[:, 0, 2 * LANES : 2 * LANES + HEAD].reshape(-1)
    return (
        query,
        tiny[:, 0:HEAD],
        tiny[:, HEAD : 2 * HEAD],
        tiny[:, LANES : LANES + routed],
        [tiny[:, LANES + 24 + i] for i in range(5)],
        own(bias, bias.shape[0] // (4 * dp), index),
        rest[:, 0:group].reshape(rows, experts, HEAD).transpose(1, 2, 0),
        rest[:, group : group + hidden],
        rest[:, group + hidden :].T,
    )


def per_device(
    tokens,
    routes,
    cotangent,
    ln1_gain,
    ln1_bias,
    w_key,
    w_value,
    w_router,
    w_query,
    w_out,
    ln2_gain,
    ln2_bias,
    w_up,
    b_up,
    w_down,
    b_down,
):
    dp = lax.axis_size("dp")
    tuned = dp == 8
    d, t = lax.axis_index("dp"), lax.axis_index("tensor")
    seq = routes.shape[0]
    blocks = seq // HALF
    slots = [(t ^ s) if tuned else jnp.int32(s) for s in range(4)]
    z, x = d // 2, d % 2
    if tuned:
        into = [((z + 4 - s) % 4) * 2 + (x ^ o) for s in range(4) for o in range(2)]
        out = [((z + s) % 4) * 2 + (x ^ o) for s in range(4) for o in range(2)]
    else:
        into = out = [jnp.int32(place) for place in range(8)]
    ranks = [t, t ^ 1, t ^ 2, t ^ 3]
    positions = [p for r in ranks for p in (2 * r, blocks - 1 - 2 * r)]
    table = jnp.stack([v.astype(jnp.int32) for v in slots + into + out + positions])
    own_routes = jnp.concatenate(
        [lax.dynamic_slice_in_dim(routes, p * HALF, HALF, 0) for p in positions[0:2]], axis=0
    )
    vectors_in = (ln1_gain, ln1_bias, ln2_gain, ln2_bias, b_down)

    tokens_high = crossed(tokens[HALF:])
    if tuned:
        first, second = pack(w_query, w_out, w_up, w_down, w_key, w_value, w_router, vectors_in, b_up)
        first_pieces = gather_blocks(first, dp)
        second_pieces = gather_blocks(second, dp)
    else:
        first_pieces, second_pieces = general_pieces(
            w_query, w_out, w_up, w_down, w_key, w_value, w_router, vectors_in, b_up
        )
    cot_high = crossed(cotangent[HALF:])

    normed, pair, gates, small, vectors, up_bias = first_stage(
        table, tokens, tokens_high, own_routes, first_pieces
    )
    pair_y = over_y(pair)
    pairs = (pair, over_core(pair), pair_y, over_core(pair_y))
    query, query_weight = query_stage(table, normed, own_routes, first_pieces)
    heads, totals = attend_stage(table, query, pairs, seq)
    (output, grad_mid, grad_heads, inner, grad_gate, sums, bias_grad, *later_blocks) = middle_stage(
        table, tokens, tokens_high, cotangent, cot_high, heads, gates, own_routes, vectors, up_bias, second_pieces
    )
    grad_query, part0, part1, part2, part3 = attend_back_stage(
        table, query, grad_heads, totals, inner, pairs, seq
    )
    pair_parts = (part0, over_core(part1), over_y(part2), crossed(part3))
    low_rows, high_rows, *first_blocks = last_stage(
        table, tokens, tokens_high, grad_mid, grad_query, normed, own_routes, gates, grad_gate,
        query_weight, small, vectors, sums, bias_grad, pair_parts,
    )
    experts, hidden, routed = w_query.shape[0], w_up.shape[1], w_router.shape[1]
    if tuned:
        later = reduce_blocks(*later_blocks, dp)
        out_grad, up_grad, down_grad = unpack_second(*later, experts, hidden)
        early = reduce_blocks(*first_blocks, dp)
        query_grad, key_grad, value_grad, router_grad, small_grads, up_bias_grad = unpack_first(
            *early, experts, routed
        )
    else:
        (
            query_grad, key_grad, value_grad, router_grad, small_grads, up_bias_grad,
            out_grad, up_grad, down_grad,
        ) = general_grads(first_blocks, later_blocks, experts, hidden, routed)
    result = jnp.concatenate([output[:HALF], crossed(output[HALF:])], axis=0)
    grad_tokens = jnp.concatenate([low_rows, crossed(high_rows).astype(F32)], axis=0)
    return (
        result,
        grad_tokens,
        small_grads[0],
        small_grads[1],
        key_grad,
        value_grad,
        router_grad,
        query_grad,
        out_grad,
        small_grads[2],
        small_grads[3],
        up_grad,
        up_bias_grad,
        down_grad,
        small_grads[4],
    )


def solution(mesh):
    rows = P(("dp", "tensor"), None)
    vector = P(("dp", "tensor"))
    in_specs = (
        rows,
        P("dp", None),
        rows,
        vector,
        vector,
        rows,
        rows,
        rows,
        P("tensor", "dp", None),
        P("tensor", None, "dp"),
        vector,
        vector,
        P("dp", "tensor"),
        vector,
        P("tensor", "dp"),
        vector,
    )
    out_specs = (
        rows,
        rows,
        vector,
        vector,
        rows,
        rows,
        rows,
        P("tensor", "dp", None),
        P("tensor", None, "dp"),
        vector,
        vector,
        P("dp", "tensor"),
        vector,
        P("tensor", "dp"),
        vector,
    )
    return jax.shard_map(
        per_device, mesh=mesh, in_specs=in_specs, out_specs=out_specs, check_vma=False
    )
```

```python
import jax
import jax.numpy as jnp
from jax import lax
from jax.experimental import pallas as pl
from jax.experimental.pallas import tpu as pltpu
from jax.sharding import PartitionSpec as P

F32 = jnp.float32
BF16 = jnp.bfloat16
HEAD = 64
LANES = 128
HALF = 256
ROWS = 64
TINY = 16
CHUNK = 32
VMEM_MAX = 60 * 1024 * 1024

PLACES_A = ((0, 0, 0), (0, 0, 1), (1, 0, 0), (1, 0, 1))
PLACES_XA = tuple((y, 1, s) for y, _, s in PLACES_A)
PLACES_B = ((0, 0, 2), (0, 0, 3), (0, 1, 2), (0, 1, 3))
PLACES_YB = tuple((1, x, s) for _, x, s in PLACES_B)
LAYOUT = tuple(
    tuple((2 * y + core, 2 * s + x) for y, x, s in places)
    for core in (0, 1)
    for places in (PLACES_A, PLACES_XA, PLACES_B, PLACES_YB)
)
SLOT_AT, IN_AT, OUT_AT, POS_AT = 0, 4, 12, 20


def nn(left, right):
    return lax.dot_general(left, right, (((1,), (0,)), ((), ())), preferred_element_type=F32)


def nt(left, right):
    return lax.dot_general(left, right, (((1,), (1,)), ((), ())), preferred_element_type=F32)


def norm_parts(rows):
    average = jnp.mean(rows, axis=-1, keepdims=True)
    centered = rows - average
    inverse = lax.rsqrt(jnp.mean(centered * centered, axis=-1, keepdims=True) + 1e-05)
    return centered * inverse, inverse


def norm_backward(incoming, scaled, inverse, gain):
    weighted = incoming * gain
    return inverse * (
        weighted
        - jnp.mean(weighted, axis=-1, keepdims=True)
        - scaled * jnp.mean(weighted * scaled, axis=-1, keepdims=True)
    )


def any_spec():
    return pl.BlockSpec(memory_space=pl.ANY)


def smem_spec():
    return pl.BlockSpec(memory_space=pltpu.SMEM)


def params():
    return pltpu.CompilerParams(vmem_limit_bytes=VMEM_MAX)


def cost(microseconds):
    return pl.CostEstimate(flops=0, bytes_accessed=int(microseconds * 3.69e5), transcendentals=0)


def after(value, *earlier):
    return lax.optimization_barrier((value, *earlier))[0]


def shaped(shape, kind):
    return jax.ShapeDtypeStruct(shape, kind)


def pack_kernel(
    wq, wo, wup, wdown, wk, wv, wr, tok, cot, g1, b1, g2, b2, bdown, bup, first_ref, second_ref, cross_ref, wide, square
):
    cross_ref[0:HALF, :] = tok[HALF:, :]
    cross_ref[HALF:, :] = cot[HALF:, :]
    experts = wq.shape[0]
    group = experts * HEAD
    hidden = wup.shape[1]
    first_ref[...] = jnp.zeros_like(first_ref)
    for j in range(experts):
        first_ref[0:ROWS, j * HEAD : (j + 1) * HEAD] = wq[j]
    square[...] = jnp.zeros_like(square)
    for i, vector in enumerate((g1, b1, g2, b2, bdown)):
        square[24 + i : 25 + i, 0:TINY] = vector[...].astype(F32)
    columns = square[...].T
    first_ref[ROWS : ROWS + TINY, 0:HEAD] = wk[...]
    first_ref[ROWS : ROWS + TINY, HEAD : 2 * HEAD] = wv[...]
    first_ref[ROWS : ROWS + TINY, LANES : 2 * LANES] = columns[0:TINY, :].astype(BF16)
    first_ref[ROWS : ROWS + TINY, LANES : LANES + wr.shape[1]] = wr[...]
    first_ref[ROWS : ROWS + 1, 2 * LANES : 2 * LANES + HEAD] = bup[...]
    wide[...] = jnp.zeros_like(wide)
    for j in range(experts):
        wide[j * HEAD : (j + 1) * HEAD, 0:ROWS] = wo[j].astype(F32)
    second_ref[:, 0:group] = wide[...].T[0:ROWS].astype(BF16)
    second_ref[:, group : group + hidden] = wup[...]
    second_ref[:, group + hidden :] = wdown[...]


def pack(wq, wo, wup, wdown, wk, wv, wr, tok, cot, vectors, bup):
    group, hidden = wq.shape[0] * HEAD, wup.shape[1]
    return pl.pallas_call(
        pack_kernel,
        cost_estimate=cost(2),
        out_shape=(
            shaped((ROWS + TINY, group), BF16),
            shaped((ROWS, group + 2 * hidden), BF16),
            shaped(tok.shape, BF16),
        ),
        scratch_shapes=[
            pltpu.VMEM((group, LANES), F32),
            pltpu.VMEM((LANES, LANES), F32),
        ],
        compiler_params=params(),
    )(wq, wo, wup, wdown, wk, wv, wr, tok, cot, *[v.reshape(1, -1) for v in vectors], bup.reshape(1, -1))


def sum_four(kept, one, two, three):
    return kept.astype(F32) + one.astype(F32) + two.astype(F32) + three.astype(F32)


def unpack_first_kernel(kept, one, two, three, gq, gk, gv, gr, v1, v2, v3, v4, v5, gb, total):
    total[...] = sum_four(kept[0], one[...], two[...], three[...])
    for j in range(gq.shape[0]):
        gq[j] = total[0:ROWS, j * HEAD : (j + 1) * HEAD]
    gk[...] = total[ROWS : ROWS + TINY, 0:HEAD]
    gv[...] = total[ROWS : ROWS + TINY, HEAD : 2 * HEAD]
    gr[...] = total[ROWS : ROWS + TINY, LANES : LANES + gr.shape[1]]
    square = jnp.concatenate(
        [total[ROWS : ROWS + TINY, LANES : 2 * LANES], jnp.zeros((LANES - TINY, LANES), F32)], axis=0
    ).T
    for i, out in enumerate((v1, v2, v3, v4, v5)):
        out[...] = square[24 + i : 25 + i, 0:TINY]
    gb[...] = total[ROWS : ROWS + 1, 2 * LANES : 2 * LANES + HEAD]


def unpack_first(kept, one, two, three, experts, routed):
    outs = pl.pallas_call(
        unpack_first_kernel,
        cost_estimate=cost(2),
        out_shape=(
            shaped((experts, ROWS, HEAD), F32),
            shaped((TINY, HEAD), F32),
            shaped((TINY, HEAD), F32),
            shaped((TINY, routed), F32),
            *[shaped((1, TINY), F32) for _ in range(5)],
            shaped((1, HEAD), F32),
        ),
        scratch_shapes=[pltpu.VMEM(kept.shape[1:], F32)],
        compiler_params=params(),
    )(kept, one, two, three)
    return outs[0], outs[1], outs[2], outs[3], [v.reshape(-1) for v in outs[4:9]], outs[9].reshape(-1)


def unpack_second_kernel(kept, one, two, three, go, gup, gdown, total, wide):
    experts = go.shape[0]
    group, hidden = experts * HEAD, gup.shape[1]
    total[...] = sum_four(kept[0], one[...], two[...], three[...])
    gup[...] = total[:, group : group + hidden]
    wide[...] = jnp.zeros_like(wide)
    wide[0:ROWS, :] = total[:, 0:group]
    turned = wide[...].T
    for j in range(experts):
        go[j] = turned[j * HEAD : (j + 1) * HEAD, 0:ROWS]
    gdown[...] = total[:, group + hidden :]


def unpack_second(kept, one, two, three, experts, hidden):
    group = experts * HEAD
    return pl.pallas_call(
        unpack_second_kernel,
        cost_estimate=cost(2),
        out_shape=(
            shaped((experts, HEAD, ROWS), F32),
            shaped((ROWS, hidden), F32),
            shaped((ROWS, hidden), F32),
        ),
        scratch_shapes=[
            pltpu.VMEM(kept.shape[1:], F32),
            pltpu.VMEM((LANES, group), F32),
        ],
        compiler_params=params(),
    )(kept, one, two, three)


def axis_moves(dp):
    turns = [
        [(d, (d + 2 * step) % dp) for d in range(dp)] for step in range(1, dp // 2)
    ]
    return turns, [(d, d ^ 1) for d in range(dp)]


CORE = [(0, 1), (1, 0), (2, 3), (3, 2)]
ACROSS = [(0, 2), (2, 0), (1, 3), (3, 1)]
CROSSED = [(0, 3), (3, 0), (1, 2), (2, 1)]


def over_core(x):
    return lax.ppermute(x, "tensor", CORE)


def over_y(x):
    return lax.ppermute(x, "tensor", ACROSS)


def crossed(x):
    return lax.ppermute(x, "tensor", CROSSED)


def add_low(*terms):
    total = terms[0].astype(F32)
    for term in terms[1:]:
        total = total + term.astype(F32)
    return total.astype(BF16)


def block_copies(table, pieces, row_from, rows, stride, target, sems):
    copies = []
    for a, (piece, places) in enumerate(zip(pieces, LAYOUT)):
        for i, (slot, place) in enumerate(places):
            source = piece.at[i, pl.ds(row_from, rows), :]
            block = table[IN_AT + place]
            if stride is None:
                into = target.at[slot, pl.ds(pl.multiple_of(block * rows, rows), rows), :]
            else:
                row = (block * stride + table[SLOT_AT + slot]) * rows
                into = target.at[pl.ds(pl.multiple_of(row, rows), rows), :]
            copies.append(pltpu.make_async_copy(source, into, sems.at[a, i]))
    return copies


def first_kernel(table, low_tok, cross, routes, *refs):
    pieces, (normed_ref, kv_ref, gates_ref, small, vectors, up_bias, sems) = refs[:8], refs[8:]
    copies = block_copies(table, pieces, ROWS, TINY, 4, small, sems)
    for copy in copies:
        copy.start()
    tokens = jnp.concatenate([low_tok[0:HALF, :], cross[0:HALF, :]], axis=0).astype(F32)
    scaled, _ = norm_parts(tokens)
    for copy in copies:
        copy.wait()
    turned = small[:, LANES : 2 * LANES].astype(F32).T
    vectors[...] = turned[24:32, :]
    for i in range(32):
        up_bias[i // 8 : i // 8 + 1, (i % 8) * HEAD : (i % 8 + 1) * HEAD] = small[
            TINY * i : TINY * i + 1, 2 * LANES : 2 * LANES + HEAD
        ].astype(F32)
    normed = (scaled * vectors[0:1, :] + vectors[1:2, :]).astype(BF16)
    normed_ref[...] = normed
    kv_ref[...] = nn(normed, small[:, 0:LANES]).astype(BF16)
    logits = nn(normed, small[:, LANES : 2 * LANES])
    lane = lax.broadcasted_iota(jnp.int32, logits.shape, 1)
    ways = routes.shape[1]
    chosen = [lane == routes[:, k : k + 1] for k in range(ways)]
    member = chosen[0]
    for k in range(1, ways):
        member = member | chosen[k]
    logits = jnp.where(member, logits, -jnp.inf)
    exponent = jnp.exp(logits - jnp.max(logits, axis=-1, keepdims=True))
    shares = exponent / jnp.sum(exponent, axis=-1, keepdims=True)
    gates = jnp.zeros_like(shares)
    for k in range(ways):
        gate = jnp.sum(jnp.where(chosen[k], shares, 0.0), axis=-1, keepdims=True)
        gates = jnp.where(lane == k, gate, gates)
    gates_ref[...] = gates


def first_stage(table, tokens, cross, routes, pieces):
    rows, width = tokens.shape
    return pl.pallas_call(
        first_kernel,
        cost_estimate=cost(5),
        in_specs=[smem_spec()] + [pl.BlockSpec(memory_space=pltpu.VMEM)] * 3 + [any_spec()] * 8,
        out_shape=(
            shaped((rows, width), BF16),
            shaped((rows, LANES), BF16),
            shaped((rows, LANES), F32),
            shaped((width, pieces[0].shape[2]), BF16),
            shaped((8, width), F32),
            shaped((8, width), F32),
        ),
        scratch_shapes=[pltpu.SemaphoreType.DMA((8, 4))],
        compiler_params=params(),
    )(table, tokens, cross, routes, *pieces)


def half_routes(routes, k, at, half):
    return jnp.broadcast_to(routes[at, k : k + 1], half.shape) - half


def query_kernel(table, normed, routes, *refs):
    pieces, (chosen, weight, queries, sems) = refs[:8], refs[8:]
    experts = weight.shape[2] // HEAD
    copies = block_copies(table, pieces, 0, ROWS, None, weight, sems)
    for copy in copies:
        copy.start()
    for copy in copies:
        copy.wait()
    for slot in range(4):
        queries[slot] = nn(normed[...], weight[slot]).astype(BF16)
    ways = routes.shape[1]
    half = (lax.broadcasted_iota(jnp.int32, (CHUNK, LANES), 1) >= HEAD).astype(jnp.int32)

    def step(c, _):
        at = pl.ds(pl.multiple_of(c * CHUNK, CHUNK), CHUNK)
        wanted = [half_routes(routes, k, at, half) for k in range(ways)]
        picked = [jnp.zeros((CHUNK, LANES), F32)] * ways
        for slot in range(4):
            for pair in range(experts // 2):
                value = queries[slot, at, pair * LANES : (pair + 1) * LANES].astype(F32)
                base = experts * table[SLOT_AT + slot] + 2 * pair
                for k in range(ways):
                    picked[k] = jnp.where(wanted[k] == base, value, picked[k])
        for k in range(ways):
            chosen[k, at, :] = picked[k].astype(BF16)
        return 0

    lax.fori_loop(0, normed.shape[0] // CHUNK, step, 0)


def query_stage(table, normed, routes, pieces):
    rows, width = normed.shape
    group = pieces[0].shape[2]
    return pl.pallas_call(
        query_kernel,
        cost_estimate=cost(8),
        in_specs=[smem_spec()] + [pl.BlockSpec(memory_space=pltpu.VMEM)] * 2 + [any_spec()] * 8,
        out_shape=(
            shaped((routes.shape[1], rows, LANES), BF16),
            shaped((4, width, group), BF16),
        ),
        scratch_shapes=[
            pltpu.VMEM((4, rows, group), BF16),
            pltpu.SemaphoreType.DMA((8, 4)),
        ],
        compiler_params=params(),
    )(table, normed, routes, *pieces)


def place_pair(table, pieces, key_scr, value_scr, ones):
    lower = lax.broadcasted_iota(jnp.int32, (HALF, LANES), 1) < HEAD
    for p, piece in enumerate(pieces):
        for h in range(2):
            both = piece[h * HALF : (h + 1) * HALF, :].astype(F32)
            turned = pltpu.roll(both, HEAD, 1)
            at = pl.ds(pl.multiple_of(table[POS_AT + 2 * p + h] * HALF, HALF), HALF)
            key_scr[at, :] = (jnp.where(lower, both, turned) * 0.125).astype(BF16)
            value_scr[at, 0:LANES] = jnp.where(lower, turned, both).astype(BF16)
            if ones:
                value_scr[at, LANES : 2 * LANES] = jnp.ones((HALF, LANES), BF16)


def causal_mask():
    shape = (HALF, HALF)
    return lax.broadcasted_iota(jnp.int32, shape, 1) <= lax.broadcasted_iota(jnp.int32, shape, 0)


def attend_kernel(table, query, kv0, kv1, kv2, kv3, out_ref, total_ref, keys, values, scores, tops, sums):
    block = pl.program_id(0)
    ways = query.shape[0]

    @pl.when(block == 0)
    def _():
        place_pair(table, (kv0, kv1, kv2, kv3), keys, values, True)

    last = table[POS_AT + block]
    tops[...] = jnp.full_like(tops, -jnp.inf)

    def score(at, masked):
        rows = pl.ds(pl.multiple_of(at * HALF, HALF), HALF)
        keys_here = keys[rows, :]
        for k in range(ways):
            here = nt(query[k], keys_here)
            if masked:
                here = jnp.where(causal_mask(), here, -1e30)
            scores[at, k] = here
            tops[k] = jnp.maximum(tops[k], jnp.maximum(here[:, 0:LANES], here[:, LANES:]))

    lax.fori_loop(0, last, lambda at, _: (score(at, False), 0)[1], 0)
    score(last, True)
    for k in range(ways):
        tops[k] = jnp.broadcast_to(jnp.max(tops[k], axis=-1, keepdims=True), (HALF, LANES))
    sums[...] = jnp.zeros_like(sums)

    def weigh(at, _):
        rows = pl.ds(pl.multiple_of(at * HALF, HALF), HALF)
        values_here = values[rows, :]
        for k in range(ways):
            top = tops[k]
            here = scores[at, k]
            weights = jnp.concatenate(
                [jnp.exp(here[:, 0:LANES] - top), jnp.exp(here[:, LANES:] - top)], axis=1
            ).astype(BF16)
            sums[k] += nn(weights, values_here)
        return 0

    lax.fori_loop(0, last + 1, weigh, 0)
    for k in range(ways):
        whole = sums[k]
        out_ref[k] = whole[:, 0:LANES] / whole[:, LANES:]
        total_ref[k] = tops[k] + jnp.log(whole[:, LANES:])


def attend_stage(table, query, pairs, seq):
    ways, rows, _ = query.shape
    kv_spec = pl.BlockSpec((rows, LANES), lambda b: (0, 0))
    spec = pl.BlockSpec((ways, HALF, LANES), lambda b: (0, b, 0))
    return pl.pallas_call(
        attend_kernel,
        cost_estimate=cost(12),
        grid=(rows // HALF,),
        in_specs=[smem_spec(), spec] + [kv_spec] * 4,
        out_specs=(spec, spec),
        out_shape=(shaped((ways, rows, LANES), F32), shaped((ways, rows, LANES), F32)),
        scratch_shapes=[
            pltpu.VMEM((seq, LANES), BF16),
            pltpu.VMEM((seq, 2 * LANES), BF16),
            pltpu.VMEM((seq // HALF, ways, HALF, HALF), F32),
            pltpu.VMEM((ways, HALF, LANES), F32),
            pltpu.VMEM((ways, HALF, 2 * LANES), F32),
        ],
        compiler_params=params(),
    )(table, query, *pairs)


def attend_back_kernel(
    table, query, grad, totals, inner, kv0, kv1, kv2, kv3, grad_query, *refs
):
    outs, (keys, values, key_sum, value_sum, query_sum, query_t, grad_t, probs, scored) = refs[:4], refs[4:]
    block = pl.program_id(0)
    ways = query.shape[0]

    @pl.when(block == 0)
    def _():
        place_pair(table, (kv0, kv1, kv2, kv3), keys, values, False)
        key_sum[...] = jnp.zeros_like(key_sum)
        value_sum[...] = jnp.zeros_like(value_sum)

    last = table[POS_AT + block]
    query_sum[...] = jnp.zeros_like(query_sum)
    for k in range(ways):
        query_t[:, k * HALF : (k + 1) * HALF] = query[k].T
        grad_t[:, k * HALF : (k + 1) * HALF] = grad[k].T

    def step(at, masked):
        rows = pl.ds(pl.multiple_of(at * HALF, HALF), HALF)
        keys_here = keys[rows, :]
        values_here = values[rows, :]
        for k in range(ways):
            score = nt(query[k], keys_here)
            total, mean = totals[k], inner[k]
            prob = jnp.concatenate(
                [jnp.exp(score[:, 0:LANES] - total), jnp.exp(score[:, LANES:] - total)], axis=1
            )
            if masked:
                prob = jnp.where(causal_mask(), prob, 0.0)
            grad_prob = nt(grad[k], values_here)
            grad_score = prob * (grad_prob - jnp.concatenate([mean, mean], axis=1))
            probs[k * HALF : (k + 1) * HALF, :] = prob.astype(BF16)
            scored[k * HALF : (k + 1) * HALF, :] = grad_score.astype(BF16)
        query_sum[...] += nn(scored[...], keys_here)
        key_sum[at] += nn(query_t[...], scored[...])
        value_sum[at] += nn(grad_t[...], probs[...])

    lax.fori_loop(0, last, lambda at, _: (step(at, False), 0)[1], 0)
    step(last, True)
    for k in range(ways):
        grad_query[k] = query_sum[k * HALF : (k + 1) * HALF, :].astype(BF16)

    @pl.when(block == pl.num_programs(0) - 1)
    def _():
        for p, out in enumerate(outs):
            for h in range(2):
                at = table[POS_AT + 2 * p + h]
                key_part, value_part = key_sum[at], value_sum[at]
                out[h, 0:HEAD, :] = ((key_part[0:HEAD] + key_part[HEAD:]) * 0.125).astype(BF16)
                out[h, HEAD:, :] = (value_part[0:HEAD] + value_part[HEAD:]).astype(BF16)


def attend_back_stage(table, query, grad, totals, inner, pairs, seq):
    ways, rows, _ = query.shape
    kv_spec = pl.BlockSpec((rows, LANES), lambda b: (0, 0))
    spec = pl.BlockSpec((ways, HALF, LANES), lambda b: (0, b, 0))
    pair_spec = pl.BlockSpec((2, LANES, HALF), lambda b: (0, 0, 0))
    return pl.pallas_call(
        attend_back_kernel,
        cost_estimate=cost(16),
        grid=(rows // HALF,),
        in_specs=[smem_spec()] + [spec] * 4 + [kv_spec] * 4,
        out_specs=(spec,) + (pair_spec,) * 4,
        out_shape=(shaped((ways, rows, LANES), BF16),) + (shaped((2, LANES, HALF), BF16),) * 4,
        scratch_shapes=[
            pltpu.VMEM((seq, LANES), BF16),
            pltpu.VMEM((seq, LANES), BF16),
            pltpu.VMEM((seq // HALF, LANES, HALF), F32),
            pltpu.VMEM((seq // HALF, LANES, HALF), F32),
            pltpu.VMEM((ways * HALF, LANES), F32),
            pltpu.VMEM((LANES, ways * HALF), BF16),
            pltpu.VMEM((LANES, ways * HALF), BF16),
            pltpu.VMEM((ways * HALF, HALF), BF16),
            pltpu.VMEM((ways * HALF, HALF), BF16),
        ],
        compiler_params=params(),
    )(table, query, grad, totals, inner, *pairs)


def put_blocks(table, grads, outs, slot, rows, row_to, column_to, slot_stride):
    keep_a, keep_b, send_a, send_b = outs
    y, core = slot // 2, slot % 2
    wide = grads.shape[1]
    for s in range(4):
        for x in range(2):
            at = table[OUT_AT + 2 * s + x]
            if slot_stride:
                at = at * slot_stride + table[SLOT_AT + slot]
            block = grads[pl.ds(pl.multiple_of(at * rows, rows), rows), :]
            if s < 2:
                out, place = (send_a if core else keep_a), (y, x, s)
            else:
                out, place = (send_b if core else keep_b), (x, y, s - 2)
            out[place[0], place[1], place[2], row_to : row_to + rows, column_to : column_to + wide] = block


def middle_kernel(table, low_tok, low_cot, cross, heads, gates, routes, vectors, up_bias, *refs):
    pieces = refs[:8]
    output, grad_mid, back, sums, bias_grad = refs[8:13]
    blocks = refs[13:17]
    weight, mixed, big, hid_scr, pre_scr, sems = refs[17:]
    ways, rows, _ = heads.shape
    width = low_tok.shape[1]
    group = mixed.shape[2]
    hidden = hid_scr.shape[1]
    experts = group // HEAD
    copies = block_copies(table, pieces, 0, ROWS, None, weight, sems)
    for copy in copies:
        copy.start()
    half = (lax.broadcasted_iota(jnp.int32, (CHUNK, LANES), 1) >= HEAD).astype(jnp.int32)

    def expand(c, _):
        at = pl.ds(pl.multiple_of(c * CHUNK, CHUNK), CHUNK)
        wanted = [half_routes(routes, k, at, half) for k in range(ways)]
        weighted = [
            (heads[k, at, :] * gates[at, k : k + 1]).astype(BF16).astype(F32) for k in range(ways)
        ]
        for slot in range(4):
            for pair in range(experts // 2):
                base = experts * table[SLOT_AT + slot] + 2 * pair
                value = jnp.zeros((CHUNK, LANES), F32)
                for k in range(ways):
                    value = jnp.where(wanted[k] == base, weighted[k], value)
                mixed[slot, at, pair * LANES : (pair + 1) * LANES] = value.astype(BF16)
        return 0

    lax.fori_loop(0, rows // CHUNK, expand, 0)
    for copy in copies:
        copy.wait()
    middle = jnp.concatenate([low_tok[0:HALF, :], cross[0:HALF, :]], axis=0).astype(F32)
    for slot in range(4):
        middle = middle + nt(mixed[slot], weight[slot, :, 0:group])
    scaled, inverse = norm_parts(middle)
    gain = vectors[2:3, :]
    normed = (scaled * gain + vectors[3:4, :]).astype(BF16)
    normed_t = normed.T
    cot = jnp.concatenate([low_cot[0:HALF, :], cross[HALF:, :]], axis=0)
    cot_t = cot.T
    result = middle + vectors[4:5, :]
    grad_normed = jnp.zeros((rows, width), F32)
    up_at, down_at = group, group + hidden
    for slot in range(4):
        bias = up_bias[pl.ds(table[SLOT_AT + slot], 1), :]
        preact = nn(normed, weight[slot, :, up_at:down_at]) + bias
        share = jax.nn.sigmoid(preact)
        active = (preact * share).astype(BF16)
        hid_scr[...] = active
        slope = share * (1.0 + preact * (1.0 - share))
        grad_pre = (nn(cot, weight[slot, :, down_at:]) * slope).astype(BF16)
        pre_scr[...] = grad_pre
        bias_grad[pl.ds(table[SLOT_AT + slot], 1), :] = jnp.sum(
            grad_pre.astype(F32), axis=0, keepdims=True
        )
        result = result + nt(hid_scr[...], weight[slot, :, down_at:])
        grad_normed = grad_normed + nt(pre_scr[...], weight[slot, :, up_at:down_at])
        big[...] = nn(normed_t, pre_scr[...]).astype(BF16)
        put_blocks(table, big, blocks, slot, ROWS, 0, up_at, 0)
        big[...] = nn(cot_t, hid_scr[...]).astype(BF16)
        put_blocks(table, big, blocks, slot, ROWS, 0, down_at, 0)
    output[...] = result.astype(BF16)
    cot_wide = cot.astype(F32)
    sums[...] = jnp.zeros_like(sums)
    sums[2:3, :] = jnp.sum(grad_normed * scaled, axis=0, keepdims=True)
    sums[3:4, :] = jnp.sum(grad_normed, axis=0, keepdims=True)
    sums[4:5, :] = jnp.sum(cot_wide, axis=0, keepdims=True)
    grad_middle = cot_wide + norm_backward(grad_normed, scaled, inverse, gain)
    grad_mid[...] = grad_middle
    grad_attn = grad_middle.astype(BF16)
    grad_attn_t = grad_attn.T
    for slot in range(4):
        big[:, 0:group] = nn(grad_attn_t, mixed[slot]).astype(BF16)
        put_blocks(table, big.at[:, 0:group], blocks, slot, ROWS, 0, 0, 0)
        back[slot] = nn(grad_attn, weight[slot, :, 0:group]).astype(BF16)


def select_kernel(table, back, heads, gates, routes, grad_ref, inner, grad_gate):
    ways, rows, _ = heads.shape
    experts = back.shape[2] // HEAD
    half = (lax.broadcasted_iota(jnp.int32, (CHUNK, LANES), 1) >= HEAD).astype(jnp.int32)
    lane = lax.broadcasted_iota(jnp.int32, (CHUNK, LANES), 1)

    def select(c, _):
        at = pl.ds(pl.multiple_of(c * CHUNK, CHUNK), CHUNK)
        wanted = [half_routes(routes, k, at, half) for k in range(ways)]
        picked = [jnp.zeros((CHUNK, LANES), F32)] * ways
        for slot in range(4):
            for pair in range(experts // 2):
                value = back[slot, at, pair * LANES : (pair + 1) * LANES].astype(F32)
                base = experts * table[SLOT_AT + slot] + 2 * pair
                for k in range(ways):
                    picked[k] = jnp.where(wanted[k] == base, value, picked[k])
        gate_grads = jnp.zeros((CHUNK, LANES), F32)
        ones = jnp.ones((LANES, LANES), BF16)
        for k in range(ways):
            gate = jnp.broadcast_to(gates[at, k : k + 1], (CHUNK, LANES))
            gate_grad = nn((picked[k] * heads[k, at, :]).astype(BF16), ones)
            gate_grads = jnp.where(lane == k, gate_grad, gate_grads)
            grad_ref[k, at, :] = (picked[k] * gate).astype(BF16)
            inner[k, at, :] = gate_grad * gate
        grad_gate[at, :] = gate_grads
        return 0

    lax.fori_loop(0, rows // CHUNK, select, 0)


def select_stage(table, back, heads, gates, routes):
    ways, rows, _ = heads.shape
    vmem = pl.BlockSpec(memory_space=pltpu.VMEM)
    return pl.pallas_call(
        select_kernel,
        cost_estimate=cost(8),
        in_specs=[smem_spec()] + [vmem] * 4,
        out_shape=(
            shaped((ways, rows, LANES), BF16),
            shaped((ways, rows, LANES), F32),
            shaped((rows, LANES), F32),
        ),
        compiler_params=params(),
    )(table, back, heads, gates, routes)


def middle_stage(table, tokens, cot, cross, heads, gates, routes, vectors, up_bias, pieces):
    rows, width = tokens.shape
    packed = pieces[0].shape[2]
    hidden = up_bias.shape[1]
    group = packed - 2 * hidden
    block = shaped((2, 2, 2, ROWS, packed), BF16)
    vmem = pl.BlockSpec(memory_space=pltpu.VMEM)
    return pl.pallas_call(
        middle_kernel,
        cost_estimate=cost(36),
        in_specs=[smem_spec()] + [vmem] * 8 + [any_spec()] * 8,
        out_shape=(
            shaped((rows, width), BF16),
            shaped((rows, width), F32),
            shaped((4, rows, group), BF16),
            shaped((8, width), F32),
            shaped((8, hidden), F32),
            block,
            block,
            block,
            block,
        ),
        scratch_shapes=[
            pltpu.VMEM((4, width, packed), BF16),
            pltpu.VMEM((4, rows, group), BF16),
            pltpu.VMEM((width, hidden), BF16),
            pltpu.VMEM((rows, hidden), BF16),
            pltpu.VMEM((rows, hidden), BF16),
            pltpu.SemaphoreType.DMA((8, 4)),
        ],
        compiler_params=params(),
    )(table, tokens, cot, cross, heads, gates, routes, vectors, up_bias, *pieces)


def last_kernel(
    table, low_tok, cross, grad_mid, grad_query, normed, routes, gates, grad_gate, weight, small,
    vectors, sums, bias_grad, p0, p1, p2, p3, low_out, high_out, *refs
):
    blocks, (spread, pair_grad, big, tiny, wide, extra) = refs[:4], refs[4:]
    ways, rows, _ = grad_query.shape
    group = spread.shape[2]
    experts = group // HEAD
    half = (lax.broadcasted_iota(jnp.int32, (CHUNK, LANES), 1) >= HEAD).astype(jnp.int32)

    def expand(c, _):
        at = pl.ds(pl.multiple_of(c * CHUNK, CHUNK), CHUNK)
        wanted = [half_routes(routes, k, at, half) for k in range(ways)]
        held = [grad_query[k, at, :].astype(F32) for k in range(ways)]
        for slot in range(4):
            for pair in range(experts // 2):
                base = experts * table[SLOT_AT + slot] + 2 * pair
                value = jnp.zeros((CHUNK, LANES), F32)
                for k in range(ways):
                    value = jnp.where(wanted[k] == base, held[k], value)
                spread[slot, at, pair * LANES : (pair + 1) * LANES] = value.astype(BF16)
        return 0

    lax.fori_loop(0, rows // CHUNK, expand, 0)
    for h in range(2):
        total = sum_four(p0[h], p1[h], p2[h], p3[h])
        pair_grad[h * HALF : (h + 1) * HALF, :] = total.T.astype(BF16)
    gate = gates[...]
    gate_grad = grad_gate[...]
    chosen_grad = gate * (gate_grad - jnp.sum(gate * gate_grad, axis=-1, keepdims=True))
    lane = lax.broadcasted_iota(jnp.int32, (rows, LANES), 1)
    logit_grad = jnp.zeros((rows, LANES), F32)
    for k in range(ways):
        logit_grad = jnp.where(lane == routes[:, k : k + 1], chosen_grad[:, k : k + 1], logit_grad)
    logit_low = logit_grad.astype(BF16)
    normed_t = normed[...].T
    grad_normed = nt(pair_grad[...], small[:, 0:LANES]) + nt(logit_low, small[:, LANES : 2 * LANES])
    for slot in range(4):
        grad_normed = grad_normed + nt(spread[slot], weight[slot])
        big[...] = nn(normed_t, spread[slot]).astype(BF16)
        put_blocks(table, big, blocks, slot, ROWS, 0, 0, 0)
    tokens = jnp.concatenate([low_tok[0:HALF, :], cross[0:HALF, :]], axis=0).astype(F32)
    scaled, inverse = norm_parts(tokens)
    back = grad_mid[...] + norm_backward(grad_normed, scaled, inverse, vectors[0:1, :])
    low_out[...] = back[0:HALF]
    high_out[...] = back[HALF:].astype(BF16)
    wide[...] = jnp.zeros_like(wide)
    wide[24:32, :] = sums[...]
    wide[24:25, :] = jnp.sum(grad_normed * scaled, axis=0, keepdims=True)
    wide[25:26, :] = jnp.sum(grad_normed, axis=0, keepdims=True)
    tiny[:, 0:LANES] = nn(normed_t, pair_grad[...]).astype(BF16)
    tiny[:, LANES : 2 * LANES] = (nn(normed_t, logit_low) + wide[...].T).astype(BF16)
    extra[...] = jnp.zeros_like(extra)
    for i in range(32):
        extra[TINY * i : TINY * i + 1, 0:HEAD] = bias_grad[i // 8 : i // 8 + 1, (i % 8) * HEAD : (i % 8 + 1) * HEAD]
    tiny[:, 2 * LANES : 3 * LANES] = extra[...].astype(BF16)
    for slot in range(4):
        put_blocks(table, tiny, blocks, slot, TINY, ROWS, 0, 4)


def last_stage(
    table, tokens, cross, grad_mid, grad_query, normed, routes, gates, grad_gate, weight, small,
    vectors, sums, bias_grad, pair_parts
):
    rows, width = tokens.shape
    group = weight.shape[2]
    block = shaped((2, 2, 2, ROWS + TINY, group), BF16)
    vmem = pl.BlockSpec(memory_space=pltpu.VMEM)
    return pl.pallas_call(
        last_kernel,
        cost_estimate=cost(12),
        in_specs=[smem_spec()] + [vmem] * 17,
        out_shape=(shaped((HALF, width), F32), shaped((rows - HALF, width), BF16), block, block, block, block),
        scratch_shapes=[
            pltpu.VMEM((4, rows, group), BF16),
            pltpu.VMEM((rows, LANES), BF16),
            pltpu.VMEM((width, group), BF16),
            pltpu.VMEM((width, 3 * LANES), BF16),
            pltpu.VMEM((LANES, width), F32),
            pltpu.VMEM((width, LANES), F32),
        ],
        compiler_params=params(),
    )(
        table, tokens, cross, grad_mid, grad_query, normed, routes, gates, grad_gate, weight, small,
        vectors, sums, bias_grad, *pair_parts
    )


def gather_plain(x, axis, dim):
    return lax.all_gather(x, axis, axis=dim, tiled=True)


def general_pieces(wq, wo, wup, wdown, wk, wv, wr, vectors, bup):
    every = ("dp", "tensor")
    width = wup.shape[0] * lax.axis_size("dp")
    group = wq.shape[0] * HEAD

    def whole(rows):
        return lax.all_gather(gather_plain(rows, "dp", 0), "tensor", axis=0)

    queries = whole(wq.transpose(1, 0, 2).reshape(-1, group))
    second = whole(
        jnp.concatenate([wo.transpose(2, 0, 1).reshape(-1, group), wup, wdown.T], axis=1)
    )
    wide = [gather_plain(w, every, 0) for w in (wk, wv, wr)]
    columns = [gather_plain(v, every, 0)[:, None] for v in vectors]
    bias = jnp.pad(gather_plain(bup, every, 0).reshape(-1, 1, HEAD), ((0, 0), (0, TINY - 1), (0, 0)))
    left = jnp.concatenate(wide + columns, axis=1)
    small = jnp.concatenate(
        [jnp.pad(left, ((0, 0), (0, 2 * LANES - left.shape[1]))), bias.reshape(width, HEAD)], axis=1
    )
    small = jnp.pad(small, ((0, 0), (0, group - small.shape[1])))

    def block_one(slot, place):
        row = (4 * place + slot) * TINY
        return jnp.concatenate([queries[slot, place * ROWS : (place + 1) * ROWS], small[row : row + TINY]])

    first = [jnp.stack([block_one(*at) for at in places]) for places in LAYOUT]
    later = [
        jnp.stack([second[slot, place * ROWS : (place + 1) * ROWS] for slot, place in places])
        for places in LAYOUT
    ]
    return first, later


def general_sum(blocks):
    keep_a, keep_b, send_a, send_b = blocks
    slots = []
    for slot in range(4):
        y, core = slot // 2, slot % 2
        part_a, part_b = (send_a, send_b) if core else (keep_a, keep_b)
        slots.append(
            jnp.stack(
                [(part_a[y, x, s] if s < 2 else part_b[x, y, s - 2]) for s in range(4) for x in range(2)]
            )
        )
    return lax.psum(jnp.stack(slots), ("dp", "tensor")).astype(F32)


def general_grads(first, later, experts, hidden, routed):
    group = experts * HEAD
    d, t = lax.axis_index("dp"), lax.axis_index("tensor")
    dp = lax.axis_size("dp")
    width = 8 * ROWS
    first, later = general_sum(first), general_sum(later)
    mine = lax.dynamic_index_in_dim(first[:, :, 0:ROWS].reshape(4, width, group), t, 0, False)
    small = first[:, :, ROWS:].transpose(1, 0, 2, 3).reshape(width, group)
    rest = lax.dynamic_index_in_dim(later.reshape(4, width, -1), t, 0, False)
    rows = width // dp

    def own(x, length, index):
        return lax.dynamic_slice_in_dim(x, index * length, length, 0)

    query = own(mine, rows, d).reshape(rows, experts, HEAD).transpose(1, 0, 2)
    rest = own(rest, rows, d)
    index = d * 4 + t
    tiny = own(small, rows // 4, index)
    bias = small.reshape(32, TINY, group)[:, 0, 2 * LANES : 2 * LANES + HEAD].reshape(-1)
    return (
        query,
        tiny[:, 0:HEAD],
        tiny[:, HEAD : 2 * HEAD],
        tiny[:, LANES : LANES + routed],
        [tiny[:, LANES + 24 + i] for i in range(5)],
        own(bias, bias.shape[0] // (4 * dp), index),
        rest[:, 0:group].reshape(rows, experts, HEAD).transpose(1, 2, 0),
        rest[:, group : group + hidden],
        rest[:, group + hidden :].T,
    )


def per_device(
    tokens,
    routes,
    cotangent,
    ln1_gain,
    ln1_bias,
    w_key,
    w_value,
    w_router,
    w_query,
    w_out,
    ln2_gain,
    ln2_bias,
    w_up,
    b_up,
    w_down,
    b_down,
):
    dp = lax.axis_size("dp")
    tuned = dp == 8
    d, t = lax.axis_index("dp"), lax.axis_index("tensor")
    seq = routes.shape[0]
    blocks = seq // HALF
    slots = [(t ^ s) if tuned else jnp.int32(s) for s in range(4)]
    z, x = d // 2, d % 2
    if tuned:
        into = [((z + 4 - s) % 4) * 2 + (x ^ o) for s in range(4) for o in range(2)]
        out = [((z + s) % 4) * 2 + (x ^ o) for s in range(4) for o in range(2)]
    else:
        into = out = [jnp.int32(place) for place in range(8)]
    ranks = [t, t ^ 1, t ^ 2, t ^ 3]
    positions = [p for r in ranks for p in (2 * r, blocks - 1 - 2 * r)]
    table = jnp.stack([v.astype(jnp.int32) for v in slots + into + out + positions])
    own_routes = jnp.concatenate(
        [lax.dynamic_slice_in_dim(routes, p * HALF, HALF, 0) for p in positions[0:2]], axis=0
    )
    vectors_in = (ln1_gain, ln1_bias, ln2_gain, ln2_bias, b_down)

    experts, hidden, routed = w_query.shape[0], w_up.shape[1], w_router.shape[1]
    turns, swap = axis_moves(dp)

    def over_x(x):
        return lax.ppermute(x, "dp", swap)

    def over_z(x, step):
        return lax.ppermute(x, "dp", turns[step - 1])

    def over_zx(x, step):
        return lax.ppermute(x, "dp", [(source, target ^ 1) for source, target in turns[step - 1]])

    if tuned:
        first, second, cross = pack(
            w_query, w_out, w_up, w_down.T, w_key, w_value, w_router, tokens, cotangent, vectors_in, b_up
        )
        first, second = first[None], second[None]
        z1, z2, z3 = [over_z(first, step) for step in (1, 2, 3)]
        cross = crossed(cross)
        side_a = jnp.concatenate([after(first, table, own_routes), z1], axis=0)
        side_b = jnp.concatenate([z2, z3], axis=0)
        next_a, next_b = over_y(side_a), over_x(side_b)
        later_z1, later_z3 = [over_z(after(second, z1), step) for step in (1, 3)]
        later_z2 = over_z(later_z1, 1)
        side_a = jnp.concatenate([side_a, after(next_a, later_z1, later_z3)], axis=0)
        side_b = jnp.concatenate([side_b, after(next_b, later_z1, later_z3)], axis=0)
        far_a, far_b = over_x(side_a), over_y(side_b)
        first_pieces = [side_a, after(far_a, later_z2), side_b, after(far_b, later_z2)]
        first_pieces = first_pieces + [over_core(v) for v in first_pieces]
        later_a = jnp.concatenate([after(second, far_a), later_z1], axis=0)
        later_b = jnp.concatenate([after(later_z2, far_b), later_z3], axis=0)
        next_a, next_b = over_y(later_a), over_x(later_b)
    else:
        first_pieces, second_pieces = general_pieces(
            w_query, w_out, w_up, w_down, w_key, w_value, w_router, vectors_in, b_up
        )
        cross = crossed(jnp.concatenate([tokens[HALF:], cotangent[HALF:]], axis=0))
    normed, pair, gates, small, vectors, up_bias = first_stage(
        table, tokens, cross, own_routes, first_pieces
    )
    pair_y = over_y(pair)
    pairs = (pair, over_core(pair), pair_y, over_core(pair_y))
    if tuned:
        normed = after(normed, later_a, later_b)
    query, query_weight = query_stage(table, normed, own_routes, first_pieces)
    if tuned:
        side_a = jnp.concatenate([later_a, after(next_a, query, pair_y)], axis=0)
        side_b = jnp.concatenate([later_b, after(next_b, query, pair_y)], axis=0)
        far_a, far_b = over_x(side_a), over_y(side_b)
    heads, totals = attend_stage(table, query, pairs, seq)
    if tuned:
        second_pieces = [side_a, after(far_a, heads), side_b, after(far_b, heads)]
        second_pieces = second_pieces + [over_core(v) for v in second_pieces]
    output, grad_mid, back, sums, bias_grad, *later_blocks = middle_stage(
        table, tokens, cotangent, cross, heads, gates, own_routes, vectors, up_bias, second_pieces
    )
    if tuned:
        keep_a, keep_b, send_a, send_b = later_blocks
        got_a, got_b = over_core(send_a), over_core(send_b)
    output_high = crossed(output[HALF:])
    grad_heads, inner, grad_gate = select_stage(table, back, heads, gates, own_routes)
    if tuned:
        part_a, part_b = add_low(keep_a[1], after(got_a, inner)[1]), add_low(keep_b[1], after(got_b, inner)[1])
        next_a, next_b = over_y(part_a), over_x(part_b)
        grad_heads = after(grad_heads, part_a, part_b, output_high)
    grad_query, part0, part1, part2, part3 = attend_back_stage(
        table, query, grad_heads, totals, inner, pairs, seq
    )
    pair_parts = (part0, over_core(part1), over_y(part2), crossed(part3))
    if tuned:
        next_a, next_b = after(next_a, *pair_parts), after(next_b, *pair_parts)
        part_a = add_low(keep_a[0, 1], got_a[0, 1], next_a[1])
        part_b = add_low(keep_b[0, 1], got_b[0, 1], next_b[1])
        last_a, last_b = over_x(part_a), over_y(part_b)
        grad_query = after(grad_query, part_a, part_b)
    low_rows, high_rows, *first_blocks = last_stage(
        table, tokens, cross, grad_mid, grad_query, normed, own_routes, gates, grad_gate,
        query_weight, small, vectors, sums, bias_grad, pair_parts,
    )
    if tuned:
        last_a, last_b = after(last_a, low_rows), after(last_b, low_rows)
        done_a = add_low(keep_a[0, 0], got_a[0, 0], next_a[0], last_a)
        done_b = add_low(keep_b[0, 0], got_b[0, 0], next_b[0], last_b)
        later = (done_a, over_z(done_a[1], 1), over_z(done_b[0], 2), over_z(done_b[1], 3))
        out_grad, up_grad, down_grad = unpack_second(*later, experts, hidden)
        down_grad = down_grad.T

        keep_a, keep_b, send_a, send_b = first_blocks
        got_a, got_b = over_core(send_a), over_core(send_b)
        got_a, got_b = after(got_a, done_a), after(got_b, done_b)
        next_a = over_y(add_low(keep_a[1], got_a[1]))
        next_b = over_x(add_low(keep_b[1], got_b[1]))
        last_a = over_x(add_low(keep_a[0, 1], got_a[0, 1], next_a[1]))
        last_b = over_y(add_low(keep_b[0, 1], got_b[0, 1], next_b[1]))
        last_a = after(last_a, *later[1:])
        high_rows = after(high_rows, last_a)
        done_a = add_low(keep_a[0, 0], got_a[0, 0], next_a[0], last_a)
        done_b = add_low(keep_b[0, 0], got_b[0, 0], next_b[0], last_b)
        early = (done_a, over_z(done_a[1], 1), over_z(done_b[0], 2), over_z(done_b[1], 3))
        query_grad, key_grad, value_grad, router_grad, small_grads, up_bias_grad = unpack_first(
            *early, experts, routed
        )
    else:
        (
            query_grad, key_grad, value_grad, router_grad, small_grads, up_bias_grad,
            out_grad, up_grad, down_grad,
        ) = general_grads(first_blocks, later_blocks, experts, hidden, routed)
    result = jnp.concatenate([output[:HALF], output_high], axis=0)
    grad_tokens = jnp.concatenate([low_rows, crossed(high_rows).astype(F32)], axis=0)
    return (
        result,
        grad_tokens,
        small_grads[0],
        small_grads[1],
        key_grad,
        value_grad,
        router_grad,
        query_grad,
        out_grad,
        small_grads[2],
        small_grads[3],
        up_grad,
        up_bias_grad,
        down_grad,
        small_grads[4],
    )


def solution(mesh):
    rows = P(("dp", "tensor"), None)
    vector = P(("dp", "tensor"))
    in_specs = (
        rows,
        P("dp", None),
        rows,
        vector,
        vector,
        rows,
        rows,
        rows,
        P("tensor", "dp", None),
        P("tensor", None, "dp"),
        vector,
        vector,
        P("dp", "tensor"),
        vector,
        P("tensor", "dp"),
        vector,
    )
    out_specs = (
        rows,
        rows,
        vector,
        vector,
        rows,
        rows,
        rows,
        P("tensor", "dp", None),
        P("tensor", None, "dp"),
        vector,
        vector,
        P("dp", "tensor"),
        vector,
        P("tensor", "dp"),
        vector,
    )
    return jax.shard_map(
        per_device, mesh=mesh, in_specs=in_specs, out_specs=out_specs, check_vma=False
    )
```

```python
import jax
import jax.numpy as jnp
from jax import lax
from jax.experimental import pallas as pl
from jax.experimental.pallas import tpu as pltpu
from jax.sharding import PartitionSpec as P

F32 = jnp.float32
BF16 = jnp.bfloat16
HEAD = 64
LANES = 128
HALF = 256
ROWS = 64
TINY = 16
CHUNK = 32

PLACES_A = ((0, 0, 0), (0, 0, 1), (1, 0, 0), (1, 0, 1))
PLACES_XA = tuple((y, 1, s) for y, _, s in PLACES_A)
PLACES_B = ((0, 0, 2), (0, 0, 3), (0, 1, 2), (0, 1, 3))
PLACES_YB = tuple((1, x, s) for _, x, s in PLACES_B)
LAYOUT = tuple(
    tuple((2 * y + core, 2 * s + x) for y, x, s in places)
    for core in (0, 1)
    for places in (PLACES_A, PLACES_XA, PLACES_B, PLACES_YB)
)
SLOT_AT, IN_AT, OUT_AT, POS_AT = 0, 4, 12, 20


def nn(left, right):
    return lax.dot_general(left, right, (((1,), (0,)), ((), ())), preferred_element_type=F32)


def nt(left, right):
    return lax.dot_general(left, right, (((1,), (1,)), ((), ())), preferred_element_type=F32)


def norm_parts(rows):
    average = jnp.mean(rows, axis=-1, keepdims=True)
    centered = rows - average
    inverse = lax.rsqrt(jnp.mean(centered * centered, axis=-1, keepdims=True) + 1e-05)
    return centered * inverse, inverse


def norm_backward(incoming, scaled, inverse, gain):
    weighted = incoming * gain
    return inverse * (
        weighted
        - jnp.mean(weighted, axis=-1, keepdims=True)
        - scaled * jnp.mean(weighted * scaled, axis=-1, keepdims=True)
    )


def smem_spec():
    return pl.BlockSpec(memory_space=pltpu.SMEM)


def params(mebibytes):
    return pltpu.CompilerParams(vmem_limit_bytes=mebibytes * 1024 * 1024)


def cost(microseconds):
    return pl.CostEstimate(flops=0, bytes_accessed=int(microseconds * 3.69e6), transcendentals=0)


def after(value, *earlier):
    return lax.optimization_barrier((value, *earlier))[0]


def together(*values):
    return lax.optimization_barrier(values)


def shaped(shape, kind):
    return jax.ShapeDtypeStruct(shape, kind)


def pack_kernel(
    wq, wo, wup, wdown, wk, wv, wr, tok, cot, g1, b1, g2, b2, bdown, bup, first_ref, second_ref, cross_ref, wide, square
):
    cross_ref[0:HALF, :] = tok[HALF:, :]
    cross_ref[HALF:, :] = cot[HALF:, :]
    experts = wq.shape[0]
    group = experts * HEAD
    hidden = wup.shape[1]
    first_ref[...] = jnp.zeros_like(first_ref)
    for j in range(experts):
        first_ref[0:ROWS, j * HEAD : (j + 1) * HEAD] = wq[j]
    square[...] = jnp.zeros_like(square)
    for i, vector in enumerate((g1, b1, g2, b2, bdown)):
        square[24 + i : 25 + i, 0:TINY] = vector[...].astype(F32)
    columns = square[...].T
    first_ref[ROWS : ROWS + TINY, 0:HEAD] = wk[...]
    first_ref[ROWS : ROWS + TINY, HEAD : 2 * HEAD] = wv[...]
    first_ref[ROWS : ROWS + TINY, LANES : 2 * LANES] = columns[0:TINY, :].astype(BF16)
    first_ref[ROWS : ROWS + TINY, LANES : LANES + wr.shape[1]] = wr[...]
    first_ref[ROWS : ROWS + 1, 2 * LANES : 2 * LANES + HEAD] = bup[...]
    wide[...] = jnp.zeros_like(wide)
    for j in range(experts):
        wide[j * HEAD : (j + 1) * HEAD, 0:ROWS] = wo[j].astype(F32)
    second_ref[:, 0:group] = wide[...].T[0:ROWS].astype(BF16)
    second_ref[:, group : group + hidden] = wup[...]
    second_ref[:, group + hidden :] = wdown[...]


def pack(wq, wo, wup, wdown, wk, wv, wr, tok, cot, vectors, bup):
    group, hidden = wq.shape[0] * HEAD, wup.shape[1]
    return pl.pallas_call(
        pack_kernel,
        cost_estimate=cost(0.2),
        out_shape=(
            shaped((ROWS + TINY, group), BF16),
            shaped((ROWS, group + 2 * hidden), BF16),
            shaped(tok.shape, BF16),
        ),
        scratch_shapes=[
            pltpu.VMEM((group, LANES), F32),
            pltpu.VMEM((LANES, LANES), F32),
        ],
        compiler_params=params(60),
    )(wq, wo, wup, wdown, wk, wv, wr, tok, cot, *[v.reshape(1, -1) for v in vectors], bup.reshape(1, -1))


def sum_four(kept, one, two, three):
    return kept.astype(F32) + one.astype(F32) + two.astype(F32) + three.astype(F32)


def unpack_first_kernel(kept, one, two, three, gq, gk, gv, gr, *refs):
    vectors, (gb, total) = refs[:5], refs[5:]
    total[...] = sum_four(kept[...], one[...], two[...], three[...])
    for j in range(gq.shape[0]):
        gq[j] = total[0:ROWS, j * HEAD : (j + 1) * HEAD]
    small = total[ROWS:, :]
    gk[...] = small[:, 0:HEAD]
    gv[...] = small[:, HEAD : 2 * HEAD]
    gr[...] = small[:, LANES : LANES + gr.shape[1]]
    square = jnp.concatenate(
        [small[:, LANES : 2 * LANES], jnp.zeros((LANES - TINY, LANES), F32)], axis=0
    ).T
    for i, out in enumerate(vectors):
        out[...] = square[24 + i : 25 + i, 0:TINY]
    gb[...] = small[0:1, 2 * LANES : 2 * LANES + HEAD]


def unpack_first(parts, experts, routed):
    outs = pl.pallas_call(
        unpack_first_kernel,
        cost_estimate=cost(2),
        out_shape=(
            shaped((experts, ROWS, HEAD), F32),
            shaped((TINY, HEAD), F32),
            shaped((TINY, HEAD), F32),
            shaped((TINY, routed), F32),
            *[shaped((1, TINY), F32) for _ in range(5)],
            shaped((1, HEAD), F32),
        ),
        scratch_shapes=[pltpu.VMEM(parts[0].shape, F32)],
        compiler_params=params(8),
    )(*parts)
    return outs[0], outs[1], outs[2], outs[3], [v.reshape(-1) for v in outs[4:9]], outs[9].reshape(-1)


def unpack_second_kernel(kept, one, two, three, go, gup, gdown, total, wide):
    experts = go.shape[0]
    group, hidden = experts * HEAD, gup.shape[1]
    total[...] = sum_four(kept[...], one[...], two[...], three[...])
    gup[...] = total[:, group : group + hidden]
    wide[...] = jnp.zeros_like(wide)
    wide[0:ROWS, :] = total[:, 0:group]
    turned = wide[...].T
    for j in range(experts):
        go[j] = turned[j * HEAD : (j + 1) * HEAD, 0:ROWS]
    gdown[...] = total[:, group + hidden :]


def unpack_second(kept, one, two, three, experts, hidden):
    group = experts * HEAD
    return pl.pallas_call(
        unpack_second_kernel,
        cost_estimate=cost(2),
        out_shape=(
            shaped((experts, HEAD, ROWS), F32),
            shaped((ROWS, hidden), F32),
            shaped((ROWS, hidden), F32),
        ),
        scratch_shapes=[
            pltpu.VMEM(kept.shape, F32),
            pltpu.VMEM((LANES, group), F32),
        ],
        compiler_params=params(8),
    )(kept, one, two, three)


def axis_moves(dp):
    turns = [
        [(d, (d + 2 * step) % dp) for d in range(dp)] for step in range(1, dp // 2)
    ]
    return turns, [(d, d ^ 1) for d in range(dp)]


CORE = [(0, 1), (1, 0), (2, 3), (3, 2)]
ACROSS = [(0, 2), (2, 0), (1, 3), (3, 1)]
CROSSED = [(0, 3), (3, 0), (1, 2), (2, 1)]


def over_core(x):
    return lax.ppermute(x, "tensor", CORE)


def over_y(x):
    return lax.ppermute(x, "tensor", ACROSS)


def crossed(x):
    return lax.ppermute(x, "tensor", CROSSED)


def add_blocks(name, *sums):
    terms = [term for parts in sums for term in parts]
    shapes = [parts[0][0].shape[len(parts[0][1]) :] for parts in sums]
    count = len(terms)

    def kernel(*refs):
        ins, outs = refs[:count], refs[count:]
        at = 0
        for out, parts in zip(outs, sums):
            total = None
            for ref, (_, index) in zip(ins[at : at + len(parts)], parts):
                value = ref[index].astype(F32) if index else ref[...].astype(F32)
                total = value if total is None else total + value
            out[...] = total.astype(BF16)
            at += len(parts)

    kernel.__name__ = name
    size = 0
    for shape, parts in zip(shapes, sums):
        block = 2 * (len(parts) + 1)
        for n in shape:
            block *= n
        size += block
    return pl.pallas_call(
        kernel,
        cost_estimate=pl.CostEstimate(flops=0, bytes_accessed=size, transcendentals=0),
        out_shape=tuple(shaped(shape, BF16) for shape in shapes),
        compiler_params=params(16),
    )(*[array for array, _ in terms])


def add_ends(side_a, side_b, tiny):
    arrays = [*side_a, *side_b, *tiny]

    def kernel(*refs):
        ins, outs = refs[:12], refs[12:]

        def total(terms, s):
            kept, got, near, last = terms
            return sum_four(kept[0, 0, s], got[0, 0, s], near[0, s], last[s]).astype(BF16)

        for s, out in enumerate(outs):
            out[0:ROWS, :] = total(ins[0:4] if s < 2 else ins[4:8], s % 2)
            out[ROWS:, :] = total(ins[8:12], s)

    shape = (ROWS + TINY, side_a[0].shape[-1])
    return pl.pallas_call(
        kernel,
        cost_estimate=cost(1.5),
        out_shape=(shaped(shape, BF16),) * 4,
        compiler_params=params(16),
    )(*arrays)


def place_blocks(table, pieces, row_from, rows, put):
    for piece, places in zip(pieces, LAYOUT):
        for i, (slot, place) in enumerate(places):
            put(slot, table[IN_AT + place], piece[i, row_from : row_from + rows, :])


def rows_at(index, rows):
    return pl.ds(pl.multiple_of(index * rows, rows), rows)


def place_weights(table, pieces, weight):
    def put(slot, block, value):
        weight[slot, rows_at(block, ROWS), :] = value

    place_blocks(table, pieces, 0, ROWS, put)


def first_kernel(table, low_tok, cross, routes, *refs):
    pieces, (normed_ref, kv_ref, gates_ref, small, vectors, up_bias) = refs[:8], refs[8:]

    def put(slot, block, value):
        small[rows_at(block * 4 + table[SLOT_AT + slot], TINY), :] = value

    place_blocks(table, pieces, ROWS, TINY, put)
    tokens = jnp.concatenate([low_tok[0:HALF, :], cross[0:HALF, :]], axis=0).astype(F32)
    scaled, _ = norm_parts(tokens)
    turned = small[:, LANES : 2 * LANES].astype(F32).T
    vectors[...] = turned[24:32, :]
    for i in range(32):
        up_bias[i // 8 : i // 8 + 1, (i % 8) * HEAD : (i % 8 + 1) * HEAD] = small[
            TINY * i : TINY * i + 1, 2 * LANES : 2 * LANES + HEAD
        ].astype(F32)
    normed = (scaled * vectors[0:1, :] + vectors[1:2, :]).astype(BF16)
    normed_ref[...] = normed
    kv_ref[...] = nn(normed, small[:, 0:LANES]).astype(BF16)
    logits = nn(normed, small[:, LANES : 2 * LANES])
    lane = lax.broadcasted_iota(jnp.int32, logits.shape, 1)
    ways = routes.shape[1]
    chosen = [lane == routes[:, k : k + 1] for k in range(ways)]
    member = chosen[0]
    for k in range(1, ways):
        member = member | chosen[k]
    logits = jnp.where(member, logits, -jnp.inf)
    exponent = jnp.exp(logits - jnp.max(logits, axis=-1, keepdims=True))
    shares = exponent / jnp.sum(exponent, axis=-1, keepdims=True)
    gates = jnp.zeros_like(shares)
    for k in range(ways):
        gate = jnp.sum(jnp.where(chosen[k], shares, 0.0), axis=-1, keepdims=True)
        gates = jnp.where(lane == k, gate, gates)
    gates_ref[...] = gates


def first_stage(table, tokens, cross, routes, pieces):
    rows, width = tokens.shape
    return pl.pallas_call(
        first_kernel,
        cost_estimate=cost(0.5),
        in_specs=[smem_spec()] + [pl.BlockSpec(memory_space=pltpu.VMEM)] * 11,
        out_shape=(
            shaped((rows, width), BF16),
            shaped((rows, LANES), BF16),
            shaped((rows, LANES), F32),
            shaped((width, pieces[0].shape[2]), BF16),
            shaped((8, width), F32),
            shaped((8, width), F32),
        ),
        compiler_params=params(14),
    )(table, tokens, cross, routes, *pieces)


def wanted_pairs(routes, at, ways):
    half = (lax.broadcasted_iota(jnp.int32, (CHUNK, LANES), 1) >= HEAD).astype(jnp.int32)
    return [
        (jnp.broadcast_to(routes[at, k : k + 1], half.shape) - half).astype(jnp.int16)
        for k in range(ways)
    ]


def pairs_of(table, experts):
    for slot in range(4):
        for pair in range(experts // 2):
            base = experts * table[SLOT_AT + slot] + 2 * pair
            yield slot, pair, jnp.full((CHUNK, LANES), base, jnp.int32).astype(jnp.int16)


def select_pairs(table, routes, at, ways, source):
    wanted = wanted_pairs(routes, at, ways)
    picked = [jnp.zeros((CHUNK, LANES), BF16)] * ways
    for slot, pair, base in pairs_of(table, source.shape[2] // HEAD):
        value = source[slot, at, pair * LANES : (pair + 1) * LANES]
        for k in range(ways):
            picked[k] = jnp.where(wanted[k] == base, value, picked[k])
    return picked


def spread_pairs(table, routes, at, held, target):
    wanted = wanted_pairs(routes, at, len(held))
    for slot, pair, base in pairs_of(table, target.shape[2] // HEAD):
        value = jnp.zeros((CHUNK, LANES), BF16)
        for k, row in enumerate(held):
            value = jnp.where(wanted[k] == base, row, value)
        target[slot, at, pair * LANES : (pair + 1) * LANES] = value


def over_chunks(rows, step):
    def body(c, _):
        step(pl.ds(pl.multiple_of(c * CHUNK, CHUNK), CHUNK))
        return 0

    lax.fori_loop(0, rows // CHUNK, body, 0)


def query_kernel(table, normed, routes, *refs):
    pieces, (chosen, weight, queries) = refs[:8], refs[8:]
    place_weights(table, pieces, weight)
    for slot in range(4):
        queries[slot] = nn(normed[...], weight[slot]).astype(BF16)
    ways = routes.shape[1]

    def step(at):
        for k, value in enumerate(select_pairs(table, routes, at, ways, queries)):
            chosen[k, at, :] = value

    over_chunks(normed.shape[0], step)


def query_stage(table, normed, routes, pieces):
    rows, width = normed.shape
    group = pieces[0].shape[2]
    return pl.pallas_call(
        query_kernel,
        cost_estimate=cost(0.8),
        in_specs=[smem_spec()] + [pl.BlockSpec(memory_space=pltpu.VMEM)] * 10,
        out_shape=(
            shaped((routes.shape[1], rows, LANES), BF16),
            shaped((4, width, group), BF16),
        ),
        scratch_shapes=[pltpu.VMEM((4, rows, group), BF16)],
        compiler_params=params(16),
    )(table, normed, routes, *pieces)


def place_pair(table, pieces, key_scr, value_scr, ones):
    lower = lax.broadcasted_iota(jnp.int32, (HALF, LANES), 1) < HEAD
    for p, piece in enumerate(pieces):
        for h in range(2):
            both = piece[h * HALF : (h + 1) * HALF, :].astype(F32)
            turned = pltpu.roll(both, HEAD, 1)
            at = pl.ds(pl.multiple_of(table[POS_AT + 2 * p + h] * HALF, HALF), HALF)
            key_scr[at, :] = (jnp.where(lower, both, turned) * 0.125).astype(BF16)
            value_scr[at, 0:LANES] = jnp.where(lower, turned, both).astype(BF16)
            if ones:
                value_scr[at, LANES : 2 * LANES] = jnp.ones((HALF, LANES), BF16)


def causal_mask():
    shape = (HALF, HALF)
    return lax.broadcasted_iota(jnp.int32, shape, 1) <= lax.broadcasted_iota(jnp.int32, shape, 0)


def attend_kernel(table, query, kv0, kv1, kv2, kv3, out_ref, total_ref, keys, values, scores, tops, sums):
    block = pl.program_id(0)
    ways = query.shape[0]

    @pl.when(block == 0)
    def _():
        place_pair(table, (kv0, kv1, kv2, kv3), keys, values, True)

    last = table[POS_AT + block]
    tops[...] = jnp.full_like(tops, -jnp.inf)

    def score(at, masked):
        rows = pl.ds(pl.multiple_of(at * HALF, HALF), HALF)
        keys_here = keys[rows, :]
        for k in range(ways):
            here = nt(query[k], keys_here)
            if masked:
                here = jnp.where(causal_mask(), here, -1e30)
            scores[at, k] = here
            tops[k] = jnp.maximum(tops[k], jnp.maximum(here[:, 0:LANES], here[:, LANES:]))

    lax.fori_loop(0, last, lambda at, _: (score(at, False), 0)[1], 0)
    score(last, True)
    for k in range(ways):
        tops[k] = jnp.broadcast_to(jnp.max(tops[k], axis=-1, keepdims=True), (HALF, LANES))
    sums[...] = jnp.zeros_like(sums)

    def weigh(at, _):
        rows = pl.ds(pl.multiple_of(at * HALF, HALF), HALF)
        values_here = values[rows, :]
        for k in range(ways):
            top = tops[k]
            here = scores[at, k]
            weights = jnp.concatenate(
                [jnp.exp(here[:, 0:LANES] - top), jnp.exp(here[:, LANES:] - top)], axis=1
            ).astype(BF16)
            sums[k] += nn(weights, values_here)
        return 0

    lax.fori_loop(0, last + 1, weigh, 0)
    lane = lax.broadcasted_iota(jnp.int32, (HALF, LANES), 1)
    total = jnp.zeros((HALF, LANES), F32)
    for k in range(ways):
        whole = sums[k]
        out_ref[k] = (whole[:, 0:LANES] / whole[:, LANES:]).astype(BF16)
        total = jnp.where(lane == k, tops[k] + jnp.log(whole[:, LANES:]), total)
    total_ref[...] = total


def attend_stage(table, query, pairs, seq):
    ways, rows, _ = query.shape
    kv_spec = pl.BlockSpec((rows, LANES), lambda b: (0, 0))
    spec = pl.BlockSpec((ways, HALF, LANES), lambda b: (0, b, 0))
    return pl.pallas_call(
        attend_kernel,
        cost_estimate=cost(1.2),
        grid=(rows // HALF,),
        in_specs=[smem_spec(), spec] + [kv_spec] * 4,
        out_specs=(spec, pl.BlockSpec((HALF, LANES), lambda b: (b, 0))),
        out_shape=(shaped((ways, rows, LANES), BF16), shaped((rows, LANES), F32)),
        scratch_shapes=[
            pltpu.VMEM((seq, LANES), BF16),
            pltpu.VMEM((seq, 2 * LANES), BF16),
            pltpu.VMEM((seq // HALF, ways, HALF, HALF), F32),
            pltpu.VMEM((ways, HALF, LANES), F32),
            pltpu.VMEM((ways, HALF, 2 * LANES), F32),
        ],
        compiler_params=params(28),
    )(table, query, *pairs)


def attend_back_kernel(
    table, query, grad, all_totals, gates, gate_grads, kv0, kv1, kv2, kv3, grad_query, *refs
):
    outs, (keys, values, key_sum, value_sum, query_sum, query_t, grad_t, probs, scored, totals, inner) = refs[:4], refs[4:]
    block = pl.program_id(0)
    ways = query.shape[0]

    @pl.when(block == 0)
    def _():
        place_pair(table, (kv0, kv1, kv2, kv3), keys, values, False)
        key_sum[...] = jnp.zeros_like(key_sum)
        value_sum[...] = jnp.zeros_like(value_sum)

    last = table[POS_AT + block]
    query_sum[...] = jnp.zeros_like(query_sum)
    for k in range(ways):
        query_t[:, k * HALF : (k + 1) * HALF] = query[k].T
        grad_t[:, k * HALF : (k + 1) * HALF] = grad[k].T
        totals[k] = jnp.broadcast_to(all_totals[:, k : k + 1], (HALF, LANES))
        inner[k] = jnp.broadcast_to(gates[:, k : k + 1] * gate_grads[:, k : k + 1], (HALF, LANES))

    def step(at, masked):
        rows = pl.ds(pl.multiple_of(at * HALF, HALF), HALF)
        keys_here = keys[rows, :]
        values_here = values[rows, :]
        for k in range(ways):
            score = nt(query[k], keys_here)
            total, mean = totals[k], inner[k]
            prob = jnp.concatenate(
                [jnp.exp(score[:, 0:LANES] - total), jnp.exp(score[:, LANES:] - total)], axis=1
            )
            if masked:
                prob = jnp.where(causal_mask(), prob, 0.0)
            grad_prob = nt(grad[k], values_here)
            grad_score = prob * (grad_prob - jnp.concatenate([mean, mean], axis=1))
            probs[k * HALF : (k + 1) * HALF, :] = prob.astype(BF16)
            scored[k * HALF : (k + 1) * HALF, :] = grad_score.astype(BF16)
        query_sum[...] += nn(scored[...], keys_here)
        key_sum[at] += nn(query_t[...], scored[...])
        value_sum[at] += nn(grad_t[...], probs[...])

    lax.fori_loop(0, last, lambda at, _: (step(at, False), 0)[1], 0)
    step(last, True)
    for k in range(ways):
        grad_query[k] = query_sum[k * HALF : (k + 1) * HALF, :].astype(BF16)

    @pl.when(block == pl.num_programs(0) - 1)
    def _():
        for p, out in enumerate(outs):
            for h in range(2):
                at = table[POS_AT + 2 * p + h]
                key_part, value_part = key_sum[at], value_sum[at]
                out[h, 0:HEAD, :] = ((key_part[0:HEAD] + key_part[HEAD:]) * 0.125).astype(BF16)
                out[h, HEAD:, :] = (value_part[0:HEAD] + value_part[HEAD:]).astype(BF16)


def attend_back_stage(table, query, grad, totals, gates, gate_grads, pairs, seq):
    ways, rows, _ = query.shape
    kv_spec = pl.BlockSpec((rows, LANES), lambda b: (0, 0))
    spec = pl.BlockSpec((ways, HALF, LANES), lambda b: (0, b, 0))
    pair_spec = pl.BlockSpec((2, LANES, HALF), lambda b: (0, 0, 0))
    return pl.pallas_call(
        attend_back_kernel,
        cost_estimate=cost(16),
        grid=(rows // HALF,),
        in_specs=[smem_spec()] + [spec] * 2 + [pl.BlockSpec((HALF, LANES), lambda b: (b, 0))] * 3 + [kv_spec] * 4,
        out_specs=(spec,) + (pair_spec,) * 4,
        out_shape=(shaped((ways, rows, LANES), BF16),) + (shaped((2, LANES, HALF), BF16),) * 4,
        scratch_shapes=[
            pltpu.VMEM((seq, LANES), BF16),
            pltpu.VMEM((seq, LANES), BF16),
            pltpu.VMEM((seq // HALF, LANES, HALF), F32),
            pltpu.VMEM((seq // HALF, LANES, HALF), F32),
            pltpu.VMEM((ways * HALF, LANES), F32),
            pltpu.VMEM((LANES, ways * HALF), BF16),
            pltpu.VMEM((LANES, ways * HALF), BF16),
            pltpu.VMEM((ways * HALF, HALF), BF16),
            pltpu.VMEM((ways * HALF, HALF), BF16),
            pltpu.VMEM((ways, HALF, LANES), F32),
            pltpu.VMEM((ways, HALF, LANES), F32),
        ],
        compiler_params=params(20),
    )(table, query, grad, totals, gates, gate_grads, *pairs)


def in_order(table, turned, target):
    for place in range(8):
        target[place * ROWS : (place + 1) * ROWS, :] = turned[rows_at(table[OUT_AT + place], ROWS), :]


def put_blocks(grads, outs, slot, column_to):
    keep_a, keep_b, send_a, send_b = outs
    y, core = slot // 2, slot % 2
    wide = grads.shape[1]
    for s in range(4):
        for x in range(2):
            block = grads[(2 * s + x) * ROWS : (2 * s + x + 1) * ROWS, :].astype(BF16)
            if s < 2:
                out, place = (send_a if core else keep_a), (y, x, s)
            else:
                out, place = (send_b if core else keep_b), (x, y, s - 2)
            out[place[0], place[1], place[2], :, column_to : column_to + wide] = block


def middle_kernel(table, low_tok, low_cot, cross, heads, gates, routes, vectors, up_bias, *refs):
    pieces = refs[:8]
    low_out, high_out, grad_mid, back, sums, bias_grad = refs[8:14]
    blocks = refs[14:18]
    weight, mixed, turned, ordered, hid_scr, pre_scr = refs[18:]
    ways, rows, _ = heads.shape
    width = low_tok.shape[1]
    group = mixed.shape[2]
    hidden = hid_scr.shape[2]
    place_weights(table, pieces, weight)

    def expand(at):
        held = [
            (heads[k, at, :].astype(F32) * gates[at, k : k + 1]).astype(BF16) for k in range(ways)
        ]
        spread_pairs(table, routes, at, held, mixed)

    over_chunks(rows, expand)
    middle = jnp.concatenate([low_tok[0:HALF, :], cross[0:HALF, :]], axis=0).astype(F32)
    for slot in range(4):
        middle = middle + nt(mixed[slot], weight[slot, :, 0:group])
    scaled, inverse = norm_parts(middle)
    gain = vectors[2:3, :]
    normed = (scaled * gain + vectors[3:4, :]).astype(BF16)
    turned[0] = normed.T
    in_order(table, turned.at[0], ordered.at[0])
    cot = jnp.concatenate([low_cot[0:HALF, :], cross[HALF:, :]], axis=0)
    turned[1] = cot.T
    in_order(table, turned.at[1], ordered.at[1])
    result = middle + vectors[4:5, :]
    grad_normed = jnp.zeros((rows, width), F32)
    up_at, down_at = group, group + hidden
    for slot in range(4):
        bias = up_bias[pl.ds(table[SLOT_AT + slot], 1), :]
        preact = nn(normed, weight[slot, :, up_at:down_at]) + bias
        share = jax.nn.sigmoid(preact)
        active = (preact * share).astype(BF16)
        hid_scr[slot] = active
        slope = share * (1.0 + preact * (1.0 - share))
        grad_pre = (nn(cot, weight[slot, :, down_at:]) * slope).astype(BF16)
        pre_scr[slot] = grad_pre
        bias_grad[pl.ds(table[SLOT_AT + slot], 1), :] = jnp.sum(
            grad_pre.astype(F32), axis=0, keepdims=True
        )
        result = result + nt(hid_scr[slot], weight[slot, :, down_at:])
        grad_normed = grad_normed + nt(pre_scr[slot], weight[slot, :, up_at:down_at])
        put_blocks(nn(ordered[0], pre_scr[slot]), blocks, slot, up_at)
        put_blocks(nn(ordered[1], hid_scr[slot]), blocks, slot, down_at)
    low_out[...] = result[0:HALF].astype(BF16)
    high_out[...] = result[HALF:].astype(BF16)
    cot_wide = cot.astype(F32)
    sums[...] = jnp.zeros_like(sums)
    sums[2:3, :] = jnp.sum(grad_normed * scaled, axis=0, keepdims=True)
    sums[3:4, :] = jnp.sum(grad_normed, axis=0, keepdims=True)
    sums[4:5, :] = jnp.sum(cot_wide, axis=0, keepdims=True)
    grad_middle = cot_wide + norm_backward(grad_normed, scaled, inverse, gain)
    grad_mid[...] = grad_middle
    grad_attn = grad_middle.astype(BF16)
    turned[2] = grad_attn.T
    in_order(table, turned.at[2], ordered.at[2])
    for slot in range(4):
        put_blocks(nn(ordered[2], mixed[slot]), blocks, slot, 0)
        back[slot] = nn(grad_attn, weight[slot, :, 0:group]).astype(BF16)


def select_kernel(table, back, heads, gates, routes, grad_ref, grad_gate):
    ways, rows, _ = heads.shape
    lane = lax.broadcasted_iota(jnp.int32, (CHUNK, LANES), 1)
    ones = jnp.ones((LANES, LANES), BF16)

    def step(at):
        gate_grads = jnp.zeros((CHUNK, LANES), F32)
        for k, value in enumerate(select_pairs(table, routes, at, ways, back)):
            gate_grads = jnp.where(lane == k, nn(value * heads[k, at, :], ones), gate_grads)
            grad_ref[k, at, :] = (value.astype(F32) * gates[at, k : k + 1]).astype(BF16)
        grad_gate[at, :] = gate_grads

    over_chunks(rows, step)


def select_stage(table, back, heads, gates, routes):
    ways, rows, _ = heads.shape
    vmem = pl.BlockSpec(memory_space=pltpu.VMEM)
    return pl.pallas_call(
        select_kernel,
        cost_estimate=cost(8),
        in_specs=[smem_spec()] + [vmem] * 4,
        out_shape=(
            shaped((ways, rows, LANES), BF16),
            shaped((rows, LANES), F32),
        ),
        compiler_params=params(16),
    )(table, back, heads, gates, routes)


def middle_stage(table, tokens, cot, cross, heads, gates, routes, vectors, up_bias, pieces):
    rows, width = tokens.shape
    packed = pieces[0].shape[2]
    hidden = up_bias.shape[1]
    group = packed - 2 * hidden
    block = shaped((2, 2, 2, ROWS, packed), BF16)
    vmem = pl.BlockSpec(memory_space=pltpu.VMEM)
    return pl.pallas_call(
        middle_kernel,
        cost_estimate=cost(36),
        in_specs=[smem_spec()] + [vmem] * 16,
        out_shape=(
            shaped((HALF, width), BF16),
            shaped((rows - HALF, width), BF16),
            shaped((rows, width), F32),
            shaped((4, rows, group), BF16),
            shaped((8, width), F32),
            shaped((8, hidden), F32),
            block,
            block,
            block,
            block,
        ),
        scratch_shapes=[
            pltpu.VMEM((4, width, packed), BF16),
            pltpu.VMEM((4, rows, group), BF16),
            pltpu.VMEM((3, width, rows), BF16),
            pltpu.VMEM((3, width, rows), BF16),
            pltpu.VMEM((4, rows, hidden), BF16),
            pltpu.VMEM((4, rows, hidden), BF16),
        ],
        compiler_params=params(40),
    )(table, tokens, cot, cross, heads, gates, routes, vectors, up_bias, *pieces)


def spread_kernel(table, grad_query, normed, routes, spread, *refs):
    blocks, (turned, normed_t) = refs[:4], refs[4:]
    ways, rows, _ = grad_query.shape

    def expand(at):
        spread_pairs(table, routes, at, [grad_query[k, at, :] for k in range(ways)], spread)

    over_chunks(rows, expand)
    turned[...] = normed[...].T
    in_order(table, turned, normed_t)
    for slot in range(4):
        put_blocks(nn(normed_t[...], spread[slot]), blocks, slot, 0)


def spread_stage(table, grad_query, normed, routes, group):
    rows, width = normed.shape
    block = shaped((2, 2, 2, ROWS, group), BF16)
    vmem = pl.BlockSpec(memory_space=pltpu.VMEM)
    return pl.pallas_call(
        spread_kernel,
        cost_estimate=cost(6),
        in_specs=[smem_spec()] + [vmem] * 3,
        out_shape=(shaped((4, rows, group), BF16), block, block, block, block),
        scratch_shapes=[pltpu.VMEM((width, rows), BF16), pltpu.VMEM((width, rows), BF16)],
        compiler_params=params(16),
    )(table, grad_query, normed, routes)


def last_kernel(
    table, low_tok, cross, grad_mid, spread, normed, routes, gates, grad_gate, weight, small,
    vectors, sums, bias_grad, p0, p1, p2, p3, low_out, high_out, keep, send, pair_grad, tiny, wide, extra
):
    rows = normed.shape[0]
    ways = routes.shape[1]
    for h in range(2):
        total = sum_four(p0[h], p1[h], p2[h], p3[h])
        pair_grad[h * HALF : (h + 1) * HALF, :] = total.T.astype(BF16)
    gate = gates[...]
    gate_grad = grad_gate[...]
    chosen_grad = gate * (gate_grad - jnp.sum(gate * gate_grad, axis=-1, keepdims=True))
    lane = lax.broadcasted_iota(jnp.int32, (rows, LANES), 1)
    logit_grad = jnp.zeros((rows, LANES), F32)
    for k in range(ways):
        logit_grad = jnp.where(lane == routes[:, k : k + 1], chosen_grad[:, k : k + 1], logit_grad)
    logit_low = logit_grad.astype(BF16)
    normed_t = normed[...].T
    grad_normed = nt(pair_grad[...], small[:, 0:LANES]) + nt(logit_low, small[:, LANES : 2 * LANES])
    for slot in range(4):
        grad_normed = grad_normed + nt(spread[slot], weight[slot])
    tokens = jnp.concatenate([low_tok[0:HALF, :], cross[0:HALF, :]], axis=0).astype(F32)
    scaled, inverse = norm_parts(tokens)
    back = grad_mid[...] + norm_backward(grad_normed, scaled, inverse, vectors[0:1, :])
    low_out[...] = back[0:HALF]
    high_out[...] = back[HALF:].astype(BF16)
    wide[...] = jnp.zeros_like(wide)
    wide[24:32, :] = sums[...]
    wide[24:25, :] = jnp.sum(grad_normed * scaled, axis=0, keepdims=True)
    wide[25:26, :] = jnp.sum(grad_normed, axis=0, keepdims=True)
    tiny[:, 0:LANES] = nn(normed_t, pair_grad[...]).astype(BF16)
    tiny[:, LANES : 2 * LANES] = (nn(normed_t, logit_low) + wide[...].T).astype(BF16)
    extra[...] = jnp.zeros_like(extra)
    for i in range(32):
        extra[TINY * i : TINY * i + 1, 0:HEAD] = bias_grad[i // 8 : i // 8 + 1, (i % 8) * HEAD : (i % 8 + 1) * HEAD]
    tiny[:, 2 * LANES : 3 * LANES] = extra[...].astype(BF16)
    for slot in range(4):
        out = send if slot % 2 else keep
        for s in range(4):
            for x in range(2):
                row = (table[OUT_AT + 2 * s + x] * 4 + table[SLOT_AT + slot]) * TINY
                out[slot // 2, x, s] = tiny[pl.ds(pl.multiple_of(row, TINY), TINY), :]


def last_stage(
    table, tokens, cross, grad_mid, spread, normed, routes, gates, grad_gate, weight, small,
    vectors, sums, bias_grad, pair_parts
):
    rows, width = tokens.shape
    block = shaped((2, 2, 4, TINY, 3 * LANES), BF16)
    vmem = pl.BlockSpec(memory_space=pltpu.VMEM)
    return pl.pallas_call(
        last_kernel,
        cost_estimate=cost(7),
        in_specs=[smem_spec()] + [vmem] * 17,
        out_shape=(shaped((HALF, width), F32), shaped((rows - HALF, width), BF16), block, block),
        scratch_shapes=[
            pltpu.VMEM((rows, LANES), BF16),
            pltpu.VMEM((width, 3 * LANES), BF16),
            pltpu.VMEM((LANES, width), F32),
            pltpu.VMEM((width, LANES), F32),
        ],
        compiler_params=params(24),
    )(
        table, tokens, cross, grad_mid, spread, normed, routes, gates, grad_gate, weight, small,
        vectors, sums, bias_grad, *pair_parts
    )


def gather_plain(x, axis, dim):
    return lax.all_gather(x, axis, axis=dim, tiled=True)


def general_pieces(wq, wo, wup, wdown, wk, wv, wr, vectors, bup):
    every = ("dp", "tensor")
    width = wup.shape[0] * lax.axis_size("dp")
    group = wq.shape[0] * HEAD

    def whole(rows):
        return lax.all_gather(gather_plain(rows, "dp", 0), "tensor", axis=0)

    queries = whole(wq.transpose(1, 0, 2).reshape(-1, group))
    second = whole(
        jnp.concatenate([wo.transpose(2, 0, 1).reshape(-1, group), wup, wdown.T], axis=1)
    )
    wide = [gather_plain(w, every, 0) for w in (wk, wv, wr)]
    columns = [gather_plain(v, every, 0)[:, None] for v in vectors]
    bias = jnp.pad(gather_plain(bup, every, 0).reshape(-1, 1, HEAD), ((0, 0), (0, TINY - 1), (0, 0)))
    left = jnp.concatenate(wide + columns, axis=1)
    small = jnp.concatenate(
        [jnp.pad(left, ((0, 0), (0, 2 * LANES - left.shape[1]))), bias.reshape(width, HEAD)], axis=1
    )
    small = jnp.pad(small, ((0, 0), (0, group - small.shape[1])))

    def block_one(slot, place):
        row = (4 * place + slot) * TINY
        return jnp.concatenate([queries[slot, place * ROWS : (place + 1) * ROWS], small[row : row + TINY]])

    first = [jnp.stack([block_one(*at) for at in places]) for places in LAYOUT]
    later = [
        jnp.stack([second[slot, place * ROWS : (place + 1) * ROWS] for slot, place in places])
        for places in LAYOUT
    ]
    return first, later


def general_sum(blocks):
    keep_a, keep_b, send_a, send_b = blocks
    slots = []
    for slot in range(4):
        y, core = slot // 2, slot % 2
        part_a, part_b = (send_a, send_b) if core else (keep_a, keep_b)
        slots.append(
            jnp.stack(
                [(part_a[y, x, s] if s < 2 else part_b[x, y, s - 2]) for s in range(4) for x in range(2)]
            )
        )
    return lax.psum(jnp.stack(slots), ("dp", "tensor")).astype(F32)


def general_grads(first, tiny, later, experts, hidden, routed):
    group = experts * HEAD
    d, t = lax.axis_index("dp"), lax.axis_index("tensor")
    dp = lax.axis_size("dp")
    width = 8 * ROWS
    first, later = general_sum(first), general_sum(later)
    tiny = jnp.stack([tiny[slot % 2][slot // 2].swapaxes(0, 1) for slot in range(4)])
    small = lax.psum(tiny, ("dp", "tensor")).astype(F32).reshape(4, 8, TINY, 3 * LANES)
    small = small.transpose(1, 0, 2, 3).reshape(width, 3 * LANES)
    mine = lax.dynamic_index_in_dim(first.reshape(4, width, group), t, 0, False)
    rest = lax.dynamic_index_in_dim(later.reshape(4, width, -1), t, 0, False)
    rows = width // dp

    def own(x, length, index):
        return lax.dynamic_slice_in_dim(x, index * length, length, 0)

    query = own(mine, rows, d).reshape(rows, experts, HEAD).transpose(1, 0, 2)
    rest = own(rest, rows, d)
    index = d * 4 + t
    tiny = own(small, rows // 4, index)
    bias = small.reshape(32, TINY, 3 * LANES)[:, 0, 2 * LANES : 2 * LANES + HEAD].reshape(-1)
    return (
        query,
        tiny[:, 0:HEAD],
        tiny[:, HEAD : 2 * HEAD],
        tiny[:, LANES : LANES + routed],
        [tiny[:, LANES + 24 + i] for i in range(5)],
        own(bias, bias.shape[0] // (4 * dp), index),
        rest[:, 0:group].reshape(rows, experts, HEAD).transpose(1, 2, 0),
        rest[:, group : group + hidden],
        rest[:, group + hidden :].T,
    )


def per_device(
    tokens,
    routes,
    cotangent,
    ln1_gain,
    ln1_bias,
    w_key,
    w_value,
    w_router,
    w_query,
    w_out,
    ln2_gain,
    ln2_bias,
    w_up,
    b_up,
    w_down,
    b_down,
):
    dp = lax.axis_size("dp")
    tuned = dp == 8
    d, t = lax.axis_index("dp"), lax.axis_index("tensor")
    seq = routes.shape[0]
    blocks = seq // HALF
    slots = [(t ^ s) if tuned else jnp.int32(s) for s in range(4)]
    z, x = d // 2, d % 2
    if tuned:
        into = [((z + 4 - s) % 4) * 2 + (x ^ o) for s in range(4) for o in range(2)]
        out = [((z + s) % 4) * 2 + (x ^ o) for s in range(4) for o in range(2)]
    else:
        into = out = [jnp.int32(place) for place in range(8)]
    ranks = [t, t ^ 1, t ^ 2, t ^ 3]
    positions = [p for r in ranks for p in (2 * r, blocks - 1 - 2 * r)]
    table = jnp.stack([v.astype(jnp.int32) for v in slots + into + out + positions])
    own_routes = jnp.concatenate(
        [lax.dynamic_slice_in_dim(routes, p * HALF, HALF, 0) for p in positions[0:2]], axis=0
    )
    vectors_in = (ln1_gain, ln1_bias, ln2_gain, ln2_bias, b_down)

    experts, hidden, routed = w_query.shape[0], w_up.shape[1], w_router.shape[1]
    turns, swap = axis_moves(dp)

    def over_x(x):
        return lax.ppermute(x, "dp", swap)

    def over_z(x, step):
        return lax.ppermute(x, "dp", turns[step - 1])

    def over_zx(x, step):
        return lax.ppermute(x, "dp", [(source, target ^ 1) for source, target in turns[step - 1]])

    if tuned:
        first, second, cross = pack(
            w_query, w_out, w_up, w_down.T, w_key, w_value, w_router, tokens, cotangent, vectors_in, b_up
        )
        first, second = first[None], second[None]
        z1, z2, z3 = [over_z(first, step) for step in (1, 2, 3)]
        cross = crossed(cross)
        side_a = jnp.concatenate([after(first, table, own_routes), z1], axis=0)
        side_b = jnp.concatenate([z2, z3], axis=0)
        next_a, next_b = over_y(side_a), over_x(side_b)
        later_z1, later_z3 = [over_z(after(second, z1), step) for step in (1, 3)]
        later_z2 = over_z(later_z1, 1)
        side_a = jnp.concatenate([side_a, after(next_a, later_z1, later_z3, cross)], axis=0)
        side_b = jnp.concatenate([side_b, after(next_b, later_z1, later_z3, cross)], axis=0)
        far_a, far_b = over_x(side_a), over_y(side_b)
        far_a, far_b = after(far_a, later_z2), after(far_b, later_z2)
        first_pieces = [side_a, far_a, side_b, far_b]
        first_pieces = first_pieces + [over_core(v) for v in first_pieces]
    else:
        first_pieces, second_pieces = general_pieces(
            w_query, w_out, w_up, w_down, w_key, w_value, w_router, vectors_in, b_up
        )
        cross = crossed(jnp.concatenate([tokens[HALF:], cotangent[HALF:]], axis=0))
    normed, pair, gates, small, vectors, up_bias = first_stage(
        table, tokens, cross, own_routes, first_pieces
    )
    pair_y = over_y(pair)
    if tuned:
        later_a = jnp.concatenate([after(second, pair), later_z1], axis=0)
        later_b = jnp.concatenate([after(later_z2, pair), later_z3], axis=0)
        next_a, next_b = over_y(later_a), over_x(later_b)
    pairs = (pair, over_core(pair), pair_y, over_core(pair_y))
    if tuned:
        normed = after(normed, later_a, later_b)
    query, query_weight = query_stage(table, normed, own_routes, first_pieces)
    if tuned:
        side_a = jnp.concatenate([later_a, after(next_a, query)], axis=0)
        side_b = jnp.concatenate([later_b, after(next_b, query, pair_y)], axis=0)
        far_a, far_b = over_x(side_a), over_y(side_b)
    heads, totals = attend_stage(table, query, pairs, seq)
    if tuned:
        heads, far_a, far_b, core_a, core_b = together(heads, far_a, far_b, over_core(side_a), over_core(side_b))
        second_pieces = [side_a, far_a, side_b, far_b, core_a, over_core(far_a), core_b, over_core(far_b)]
    output, output_high, grad_mid, back, sums, bias_grad, *later_blocks = middle_stage(
        table, tokens, cotangent, cross, heads, gates, own_routes, vectors, up_bias, second_pieces
    )
    if tuned:
        keep_a, keep_b, send_a, send_b = later_blocks
        got_a, got_b = over_core(send_a), over_core(send_b)
    grad_heads, grad_gate = select_stage(table, back, heads, gates, own_routes)
    if tuned:
        got_a, got_b = after(got_a, grad_gate), after(got_b, grad_gate)
        part_a, part_b = add_blocks(
            "add_near", [(keep_a, (1,)), (got_a, (1,))], [(keep_b, (1,)), (got_b, (1,))]
        )
        next_a, next_b = over_y(part_a), over_x(part_b)
        grad_heads = after(grad_heads, part_a, part_b)
    grad_query, part0, part1, part2, part3 = attend_back_stage(
        table, query, grad_heads, totals, gates, grad_gate, pairs, seq
    )
    pair_parts = (part0, over_core(part1), over_y(part2), crossed(part3))
    if tuned:
        next_a, next_b = after(next_a, part0), after(next_b, part0)
        part_a, part_b = add_blocks(
            "add_far",
            [(keep_a, (0, 1)), (got_a, (0, 1)), (next_a, (1,))],
            [(keep_b, (0, 1)), (got_b, (0, 1)), (next_b, (1,))],
        )
        last_a, last_b = over_x(part_a), over_y(part_b)
        grad_query = after(grad_query, part_a, part_b)
    spread, *first_blocks = spread_stage(table, grad_query, normed, own_routes, query_weight.shape[2])
    if tuned:
        last_a, last_b, spread, *rest = together(last_a, last_b, spread, *pair_parts, *first_blocks)
        pair_parts, first_blocks = rest[0:4], rest[4:8]

        def final(name, keep_a, keep_b, got_a, got_b, next_a, next_b, last_a, last_b):
            return add_blocks(
                name,
                *[
                    [(keep, (0, 0, s)), (got, (0, 0, s)), (near, (0, s)), (last, (s,))]
                    for keep, got, near, last in (
                        (keep_a, got_a, next_a, last_a),
                        (keep_b, got_b, next_b, last_b),
                    )
                    for s in (0, 1)
                ],
            )

        done = final("add_last", keep_a, keep_b, got_a, got_b, next_a, next_b, last_a, last_b)
        later = (done[0], *[over_z(done[step], step) for step in (1, 2, 3)])
        keep_a, keep_b, send_a, send_b = first_blocks
        got_a, got_b = over_core(send_a), over_core(send_b)
        got_a, got_b = after(got_a, *done), after(got_b, *done)
        part_a, part_b = add_blocks(
            "add_near", [(keep_a, (1,)), (got_a, (1,))], [(keep_b, (1,)), (got_b, (1,))]
        )
        next_a, next_b = over_y(part_a), over_x(part_b)
        spread = after(spread, part_a, part_b)
        output_high = after(output_high, part_a)
    output_high = crossed(output_high)
    low_rows, high_rows, *tiny_blocks = last_stage(
        table, tokens, cross, grad_mid, spread, normed, own_routes, gates, grad_gate,
        query_weight, small, vectors, sums, bias_grad, pair_parts,
    )
    if tuned:
        kept, one, two, three = later
        low_rows, high_rows, keep, send, next_a, next_b, one, three, output_high = together(
            low_rows, high_rows, *tiny_blocks, next_a, next_b, one, three, output_high
        )
        got = over_core(send)
        part_a, part_b = add_blocks(
            "add_far",
            [(keep_a, (0, 1)), (got_a, (0, 1)), (next_a, (1,))],
            [(keep_b, (0, 1)), (got_b, (0, 1)), (next_b, (1,))],
        )
        last_a, last_b = over_x(part_a), over_y(part_b)
        (part,) = add_blocks("add_tiny", [(keep, (1,)), (got, (1,))])
        next_tiny = over_y(part)
        high_rows = after(high_rows, part)
        out_grad, up_grad, down_grad = unpack_second(kept, one, two, three, experts, hidden)
        down_grad = down_grad.T
        (part,) = add_blocks("add_tiny", [(keep, (0, 1)), (got, (0, 1)), (next_tiny, (1,))])
        last_tiny = over_x(part)
        done = add_ends(
            (keep_a, got_a, next_a, last_a), (keep_b, got_b, next_b, last_b), (keep, got, next_tiny, last_tiny)
        )
        one, two, three = [over_z(done[step], step) for step in (1, 2, 3)]
        result = jnp.concatenate([output, output_high], axis=0)
        grad_tokens = jnp.concatenate([low_rows, crossed(high_rows).astype(F32)], axis=0)
        one = after(one, out_grad, result, grad_tokens)
        parts = (done[0], one, two, three)
        query_grad, key_grad, value_grad, router_grad, small_grads, up_bias_grad = unpack_first(
            parts, experts, routed
        )
    else:
        (
            query_grad, key_grad, value_grad, router_grad, small_grads, up_bias_grad,
            out_grad, up_grad, down_grad,
        ) = general_grads(first_blocks, tiny_blocks, later_blocks, experts, hidden, routed)
        result = jnp.concatenate([output, output_high], axis=0)
        grad_tokens = jnp.concatenate([low_rows, crossed(high_rows).astype(F32)], axis=0)
    return (
        result,
        grad_tokens,
        small_grads[0],
        small_grads[1],
        key_grad,
        value_grad,
        router_grad,
        query_grad,
        out_grad,
        small_grads[2],
        small_grads[3],
        up_grad,
        up_bias_grad,
        down_grad,
        small_grads[4],
    )


def solution(mesh):
    rows = P(("dp", "tensor"), None)
    vector = P(("dp", "tensor"))
    in_specs = (
        rows,
        P("dp", None),
        rows,
        vector,
        vector,
        rows,
        rows,
        rows,
        P("tensor", "dp", None),
        P("tensor", None, "dp"),
        vector,
        vector,
        P("dp", "tensor"),
        vector,
        P("tensor", "dp"),
        vector,
    )
    out_specs = (
        rows,
        rows,
        vector,
        vector,
        rows,
        rows,
        rows,
        P("tensor", "dp", None),
        P("tensor", None, "dp"),
        vector,
        vector,
        P("dp", "tensor"),
        vector,
        P("tensor", "dp"),
        vector,
    )
    return jax.shard_map(
        per_device, mesh=mesh, in_specs=in_specs, out_specs=out_specs, check_vma=False
    )
```

```python
import jax
import jax.numpy as jnp
from jax import lax
from jax.experimental import pallas as pl
from jax.experimental.pallas import tpu as pltpu
from jax.sharding import PartitionSpec as P

F32 = jnp.float32
BF16 = jnp.bfloat16
HEAD = 64
LANES = 128
HALF = 256
ROWS = 64
TINY = 16
CHUNK = 32

PLACES_A = ((0, 0, 0), (0, 0, 1), (1, 0, 0), (1, 0, 1))
PLACES_XA = tuple((y, 1, s) for y, _, s in PLACES_A)
PLACES_B = ((0, 0, 2), (0, 0, 3), (0, 1, 2), (0, 1, 3))
PLACES_YB = tuple((1, x, s) for _, x, s in PLACES_B)
LAYOUT = tuple(
    tuple((2 * y + core, 2 * s + x) for y, x, s in places)
    for core in (0, 1)
    for places in (PLACES_A, PLACES_XA, PLACES_B, PLACES_YB)
)
SLOT_AT, IN_AT, OUT_AT, POS_AT = 0, 4, 12, 20


def nn(left, right):
    return lax.dot_general(left, right, (((1,), (0,)), ((), ())), preferred_element_type=F32)


def nt(left, right):
    return lax.dot_general(left, right, (((1,), (1,)), ((), ())), preferred_element_type=F32)


def norm_parts(rows):
    average = jnp.mean(rows, axis=-1, keepdims=True)
    centered = rows - average
    inverse = lax.rsqrt(jnp.mean(centered * centered, axis=-1, keepdims=True) + 1e-05)
    return centered * inverse, inverse


def norm_backward(incoming, scaled, inverse, gain):
    weighted = incoming * gain
    return inverse * (
        weighted
        - jnp.mean(weighted, axis=-1, keepdims=True)
        - scaled * jnp.mean(weighted * scaled, axis=-1, keepdims=True)
    )


def smem_spec():
    return pl.BlockSpec(memory_space=pltpu.SMEM)


def params(mebibytes):
    return pltpu.CompilerParams(vmem_limit_bytes=mebibytes * 1024 * 1024)


def cost(microseconds):
    return pl.CostEstimate(flops=0, bytes_accessed=int(microseconds * 3.69e6), transcendentals=0)


def after(value, *earlier):
    return lax.optimization_barrier((value, *earlier))[0]


def together(*values):
    return lax.optimization_barrier(values)


def shaped(shape, kind):
    return jax.ShapeDtypeStruct(shape, kind)


def pack_kernel(
    wq, wo, wup, wdown, wk, wv, wr, tok, cot, g1, b1, g2, b2, bdown, bup, first_ref, second_ref, cross_ref, wide, square
):
    cross_ref[0:HALF, :] = tok[HALF:, :]
    cross_ref[HALF:, :] = cot[HALF:, :]
    experts = wq.shape[0]
    group = experts * HEAD
    hidden = wup.shape[1]
    first_ref[...] = jnp.zeros_like(first_ref)
    for j in range(experts):
        first_ref[0:ROWS, j * HEAD : (j + 1) * HEAD] = wq[j]
    square[...] = jnp.zeros_like(square)
    for i, vector in enumerate((g1, b1, g2, b2, bdown)):
        square[24 + i : 25 + i, 0:TINY] = vector[...].astype(F32)
    columns = square[...].T
    first_ref[ROWS : ROWS + TINY, 0:HEAD] = wk[...]
    first_ref[ROWS : ROWS + TINY, HEAD : 2 * HEAD] = wv[...]
    first_ref[ROWS : ROWS + TINY, LANES : 2 * LANES] = columns[0:TINY, :].astype(BF16)
    first_ref[ROWS : ROWS + TINY, LANES : LANES + wr.shape[1]] = wr[...]
    first_ref[ROWS : ROWS + 1, 2 * LANES : 2 * LANES + HEAD] = bup[...]
    wide[...] = jnp.zeros_like(wide)
    for j in range(experts):
        wide[j * HEAD : (j + 1) * HEAD, 0:ROWS] = wo[j].astype(F32)
    second_ref[:, 0:group] = wide[...].T[0:ROWS].astype(BF16)
    second_ref[:, group : group + hidden] = wup[...]
    second_ref[:, group + hidden :] = wdown[...]


def pack(wq, wo, wup, wdown, wk, wv, wr, tok, cot, vectors, bup):
    group, hidden = wq.shape[0] * HEAD, wup.shape[1]
    return pl.pallas_call(
        pack_kernel,
        cost_estimate=cost(0.2),
        out_shape=(
            shaped((ROWS + TINY, group), BF16),
            shaped((ROWS, group + 2 * hidden), BF16),
            shaped(tok.shape, BF16),
        ),
        scratch_shapes=[
            pltpu.VMEM((group, LANES), F32),
            pltpu.VMEM((LANES, LANES), F32),
        ],
        compiler_params=params(60),
    )(wq, wo, wup, wdown, wk, wv, wr, tok, cot, *[v.reshape(1, -1) for v in vectors], bup.reshape(1, -1))


def sum_four(kept, one, two, three):
    return kept.astype(F32) + one.astype(F32) + two.astype(F32) + three.astype(F32)


def unpack_first_kernel(kept, one, two, three, gq, gk, gv, gr, *refs):
    vectors, (gb, total) = refs[:5], refs[5:]
    total[...] = sum_four(kept[...], one[...], two[...], three[...])
    for j in range(gq.shape[0]):
        gq[j] = total[0:ROWS, j * HEAD : (j + 1) * HEAD]
    small = total[ROWS:, :]
    gk[...] = small[:, 0:HEAD]
    gv[...] = small[:, HEAD : 2 * HEAD]
    gr[...] = small[:, LANES : LANES + gr.shape[1]]
    square = jnp.concatenate(
        [small[:, LANES : 2 * LANES], jnp.zeros((LANES - TINY, LANES), F32)], axis=0
    ).T
    for i, out in enumerate(vectors):
        out[...] = square[24 + i : 25 + i, 0:TINY]
    gb[...] = small[0:1, 2 * LANES : 2 * LANES + HEAD]


def unpack_first(parts, experts, routed):
    outs = pl.pallas_call(
        unpack_first_kernel,
        cost_estimate=cost(2),
        out_shape=(
            shaped((experts, ROWS, HEAD), F32),
            shaped((TINY, HEAD), F32),
            shaped((TINY, HEAD), F32),
            shaped((TINY, routed), F32),
            *[shaped((1, TINY), F32) for _ in range(5)],
            shaped((1, HEAD), F32),
        ),
        scratch_shapes=[pltpu.VMEM(parts[0].shape, F32)],
        compiler_params=params(8),
    )(*parts)
    return outs[0], outs[1], outs[2], outs[3], [v.reshape(-1) for v in outs[4:9]], outs[9].reshape(-1)


def unpack_second_kernel(kept, one, three, go, gup, gdown, total, wide):
    experts = go.shape[0]
    group, hidden = experts * HEAD, gup.shape[1]
    total[...] = kept[...].astype(F32) + one[...].astype(F32) + three[...].astype(F32)
    gup[...] = total[:, group : group + hidden]
    wide[...] = jnp.zeros_like(wide)
    wide[0:ROWS, :] = total[:, 0:group]
    turned = wide[...].T
    for j in range(experts):
        go[j] = turned[j * HEAD : (j + 1) * HEAD, 0:ROWS]
    gdown[...] = total[:, group + hidden :]


def unpack_second(kept, one, three, experts, hidden):
    group = experts * HEAD
    return pl.pallas_call(
        unpack_second_kernel,
        cost_estimate=cost(2),
        out_shape=(
            shaped((experts, HEAD, ROWS), F32),
            shaped((ROWS, hidden), F32),
            shaped((ROWS, hidden), F32),
        ),
        scratch_shapes=[
            pltpu.VMEM(kept.shape, F32),
            pltpu.VMEM((LANES, group), F32),
        ],
        compiler_params=params(8),
    )(kept, one, three)


def axis_moves(dp):
    turns = [
        [(d, (d + 2 * step) % dp) for d in range(dp)] for step in range(1, dp // 2)
    ]
    return turns, [(d, d ^ 1) for d in range(dp)]


CORE = [(0, 1), (1, 0), (2, 3), (3, 2)]
ACROSS = [(0, 2), (2, 0), (1, 3), (3, 1)]
CROSSED = [(0, 3), (3, 0), (1, 2), (2, 1)]


def over_core(x):
    return lax.ppermute(x, "tensor", CORE)


def over_y(x):
    return lax.ppermute(x, "tensor", ACROSS)


def crossed(x):
    return lax.ppermute(x, "tensor", CROSSED)


def add_blocks(name, *sums):
    terms = [term for parts in sums for term in parts]
    shapes = [parts[0][0].shape[len(parts[0][1]) :] for parts in sums]
    count = len(terms)

    def kernel(*refs):
        ins, outs = refs[:count], refs[count:]
        at = 0
        for out, parts in zip(outs, sums):
            total = None
            for ref, (_, index) in zip(ins[at : at + len(parts)], parts):
                value = ref[index].astype(F32) if index else ref[...].astype(F32)
                total = value if total is None else total + value
            out[...] = total.astype(BF16)
            at += len(parts)

    kernel.__name__ = name
    size = 0
    for shape, parts in zip(shapes, sums):
        block = 2 * (len(parts) + 1)
        for n in shape:
            block *= n
        size += block
    return pl.pallas_call(
        kernel,
        cost_estimate=pl.CostEstimate(flops=0, bytes_accessed=size, transcendentals=0),
        out_shape=tuple(shaped(shape, BF16) for shape in shapes),
        compiler_params=params(16),
    )(*[array for array, _ in terms])


def place_blocks(table, pieces, row_from, rows, put):
    for piece, places in zip(pieces, LAYOUT):
        for i, (slot, place) in enumerate(places):
            put(slot, table[IN_AT + place], piece[i, row_from : row_from + rows, :])


def rows_at(index, rows):
    return pl.ds(pl.multiple_of(index * rows, rows), rows)


def place_weights(table, pieces, weight):
    def put(slot, block, value):
        weight[slot, rows_at(block, ROWS), :] = value

    place_blocks(table, pieces, 0, ROWS, put)


def first_kernel(table, low_tok, cross, routes, *refs):
    pieces, (normed_ref, kv_ref, gates_ref, small, vectors, up_bias) = refs[:8], refs[8:]

    def put(slot, block, value):
        small[rows_at(block * 4 + table[SLOT_AT + slot], TINY), :] = value

    place_blocks(table, pieces, ROWS, TINY, put)
    tokens = jnp.concatenate([low_tok[0:HALF, :], cross[0:HALF, :]], axis=0).astype(F32)
    scaled, _ = norm_parts(tokens)
    turned = small[:, LANES : 2 * LANES].astype(F32).T
    vectors[...] = turned[24:32, :]
    for i in range(32):
        up_bias[i // 8 : i // 8 + 1, (i % 8) * HEAD : (i % 8 + 1) * HEAD] = small[
            TINY * i : TINY * i + 1, 2 * LANES : 2 * LANES + HEAD
        ].astype(F32)
    normed = (scaled * vectors[0:1, :] + vectors[1:2, :]).astype(BF16)
    normed_ref[...] = normed
    kv_ref[...] = nn(normed, small[:, 0:LANES]).astype(BF16)
    logits = nn(normed, small[:, LANES : 2 * LANES])
    lane = lax.broadcasted_iota(jnp.int32, logits.shape, 1)
    ways = routes.shape[1]
    chosen = [lane == routes[:, k : k + 1] for k in range(ways)]
    member = chosen[0]
    for k in range(1, ways):
        member = member | chosen[k]
    logits = jnp.where(member, logits, -jnp.inf)
    exponent = jnp.exp(logits - jnp.max(logits, axis=-1, keepdims=True))
    shares = exponent / jnp.sum(exponent, axis=-1, keepdims=True)
    gates = jnp.zeros_like(shares)
    for k in range(ways):
        gate = jnp.sum(jnp.where(chosen[k], shares, 0.0), axis=-1, keepdims=True)
        gates = jnp.where(lane == k, gate, gates)
    gates_ref[...] = gates


def first_stage(table, tokens, cross, routes, pieces):
    rows, width = tokens.shape
    return pl.pallas_call(
        first_kernel,
        cost_estimate=cost(0.5),
        in_specs=[smem_spec()] + [pl.BlockSpec(memory_space=pltpu.VMEM)] * 11,
        out_shape=(
            shaped((rows, width), BF16),
            shaped((rows, LANES), BF16),
            shaped((rows, LANES), F32),
            shaped((width, pieces[0].shape[2]), BF16),
            shaped((8, width), F32),
            shaped((8, width), F32),
        ),
        compiler_params=params(14),
    )(table, tokens, cross, routes, *pieces)


def wanted_pairs(routes, at, ways):
    half = (lax.broadcasted_iota(jnp.int32, (CHUNK, LANES), 1) >= HEAD).astype(jnp.int32)
    return [
        (jnp.broadcast_to(routes[at, k : k + 1], half.shape) - half).astype(jnp.int16)
        for k in range(ways)
    ]


def pairs_of(table, experts):
    for slot in range(4):
        for pair in range(experts // 2):
            base = experts * table[SLOT_AT + slot] + 2 * pair
            yield slot, pair, jnp.full((CHUNK, LANES), base, jnp.int32).astype(jnp.int16)


def select_pairs(table, routes, at, ways, source):
    wanted = wanted_pairs(routes, at, ways)
    picked = [jnp.zeros((CHUNK, LANES), BF16)] * ways
    for slot, pair, base in pairs_of(table, source.shape[2] // HEAD):
        value = source[slot, at, pair * LANES : (pair + 1) * LANES]
        for k in range(ways):
            picked[k] = jnp.where(wanted[k] == base, value, picked[k])
    return picked


def spread_pairs(table, routes, at, held, target):
    wanted = wanted_pairs(routes, at, len(held))
    for slot, pair, base in pairs_of(table, target.shape[2] // HEAD):
        value = jnp.zeros((CHUNK, LANES), BF16)
        for k, row in enumerate(held):
            value = jnp.where(wanted[k] == base, row, value)
        target[slot, at, pair * LANES : (pair + 1) * LANES] = value


def over_chunks(rows, step):
    def body(c, _):
        step(pl.ds(pl.multiple_of(c * CHUNK, CHUNK), CHUNK))
        return 0

    lax.fori_loop(0, rows // CHUNK, body, 0)


def query_kernel(table, normed, routes, *refs):
    pieces, (chosen, weight, queries) = refs[:8], refs[8:]
    place_weights(table, pieces, weight)
    for slot in range(4):
        queries[slot] = nn(normed[...], weight[slot]).astype(BF16)
    ways = routes.shape[1]

    def step(at):
        for k, value in enumerate(select_pairs(table, routes, at, ways, queries)):
            chosen[k, at, :] = value

    over_chunks(normed.shape[0], step)


def query_stage(table, normed, routes, pieces):
    rows, width = normed.shape
    group = pieces[0].shape[2]
    return pl.pallas_call(
        query_kernel,
        cost_estimate=cost(0.8),
        in_specs=[smem_spec()] + [pl.BlockSpec(memory_space=pltpu.VMEM)] * 10,
        out_shape=(
            shaped((routes.shape[1], rows, LANES), BF16),
            shaped((4, width, group), BF16),
        ),
        scratch_shapes=[pltpu.VMEM((4, rows, group), BF16)],
        compiler_params=params(16),
    )(table, normed, routes, *pieces)


def place_pair(table, pieces, key_scr, value_scr, ones):
    lower = lax.broadcasted_iota(jnp.int32, (HALF, LANES), 1) < HEAD
    for p, piece in enumerate(pieces):
        for h in range(2):
            both = piece[h * HALF : (h + 1) * HALF, :].astype(F32)
            turned = pltpu.roll(both, HEAD, 1)
            at = pl.ds(pl.multiple_of(table[POS_AT + 2 * p + h] * HALF, HALF), HALF)
            key_scr[at, :] = (jnp.where(lower, both, turned) * 0.125).astype(BF16)
            value_scr[at, 0:LANES] = jnp.where(lower, turned, both).astype(BF16)
            if ones:
                value_scr[at, LANES : 2 * LANES] = jnp.ones((HALF, LANES), BF16)


def causal_mask():
    shape = (HALF, HALF)
    return lax.broadcasted_iota(jnp.int32, shape, 1) <= lax.broadcasted_iota(jnp.int32, shape, 0)


def attend_kernel(table, query, kv0, kv1, kv2, kv3, out_ref, total_ref, keys, values, scores, tops, sums):
    block = pl.program_id(0)
    ways = query.shape[0]

    @pl.when(block == 0)
    def _():
        place_pair(table, (kv0, kv1, kv2, kv3), keys, values, True)

    last = table[POS_AT + block]
    tops[...] = jnp.full_like(tops, -jnp.inf)

    def score(at, masked):
        rows = pl.ds(pl.multiple_of(at * HALF, HALF), HALF)
        keys_here = keys[rows, :]
        for k in range(ways):
            here = nt(query[k], keys_here)
            if masked:
                here = jnp.where(causal_mask(), here, -1e30)
            scores[at, k] = here
            tops[k] = jnp.maximum(tops[k], jnp.maximum(here[:, 0:LANES], here[:, LANES:]))

    lax.fori_loop(0, last, lambda at, _: (score(at, False), 0)[1], 0)
    score(last, True)
    for k in range(ways):
        tops[k] = jnp.broadcast_to(jnp.max(tops[k], axis=-1, keepdims=True), (HALF, LANES))
    sums[...] = jnp.zeros_like(sums)

    def weigh(at, _):
        rows = pl.ds(pl.multiple_of(at * HALF, HALF), HALF)
        values_here = values[rows, :]
        for k in range(ways):
            top = tops[k]
            here = scores[at, k]
            weights = jnp.concatenate(
                [jnp.exp(here[:, 0:LANES] - top), jnp.exp(here[:, LANES:] - top)], axis=1
            ).astype(BF16)
            sums[k] += nn(weights, values_here)
        return 0

    lax.fori_loop(0, last + 1, weigh, 0)
    lane = lax.broadcasted_iota(jnp.int32, (HALF, LANES), 1)
    total = jnp.zeros((HALF, LANES), F32)
    for k in range(ways):
        whole = sums[k]
        out_ref[k] = (whole[:, 0:LANES] / whole[:, LANES:]).astype(BF16)
        total = jnp.where(lane == k, tops[k] + jnp.log(whole[:, LANES:]), total)
    total_ref[...] = total


def attend_stage(table, query, pairs, seq):
    ways, rows, _ = query.shape
    kv_spec = pl.BlockSpec((rows, LANES), lambda b: (0, 0))
    spec = pl.BlockSpec((ways, HALF, LANES), lambda b: (0, b, 0))
    return pl.pallas_call(
        attend_kernel,
        cost_estimate=cost(1.2),
        grid=(rows // HALF,),
        in_specs=[smem_spec(), spec] + [kv_spec] * 4,
        out_specs=(spec, pl.BlockSpec((HALF, LANES), lambda b: (b, 0))),
        out_shape=(shaped((ways, rows, LANES), BF16), shaped((rows, LANES), F32)),
        scratch_shapes=[
            pltpu.VMEM((seq, LANES), BF16),
            pltpu.VMEM((seq, 2 * LANES), BF16),
            pltpu.VMEM((seq // HALF, ways, HALF, HALF), F32),
            pltpu.VMEM((ways, HALF, LANES), F32),
            pltpu.VMEM((ways, HALF, 2 * LANES), F32),
        ],
        compiler_params=params(28),
    )(table, query, *pairs)


def attend_back_kernel(
    table, query, grad, all_totals, gates, gate_grads, kv0, kv1, kv2, kv3, grad_query, *refs
):
    pair_outs, (keys, values, key_sum, value_sum, query_sum, query_t, grad_t, probs, scored, totals, inner) = refs[:2], refs[2:]
    block = pl.program_id(0)
    ways = query.shape[0]

    @pl.when(block == 0)
    def _():
        place_pair(table, (kv0, kv1, kv2, kv3), keys, values, False)
        key_sum[...] = jnp.zeros_like(key_sum)
        value_sum[...] = jnp.zeros_like(value_sum)

    last = table[POS_AT + block]
    query_sum[...] = jnp.zeros_like(query_sum)
    for k in range(ways):
        query_t[:, k * HALF : (k + 1) * HALF] = query[k].T
        grad_t[:, k * HALF : (k + 1) * HALF] = grad[k].T
        totals[k] = jnp.broadcast_to(all_totals[:, k : k + 1], (HALF, LANES))
        inner[k] = jnp.broadcast_to(gates[:, k : k + 1] * gate_grads[:, k : k + 1], (HALF, LANES))

    def step(at, masked):
        rows = pl.ds(pl.multiple_of(at * HALF, HALF), HALF)
        keys_here = keys[rows, :]
        values_here = values[rows, :]
        for k in range(ways):
            score = nt(query[k], keys_here)
            total, mean = totals[k], inner[k]
            prob = jnp.concatenate(
                [jnp.exp(score[:, 0:LANES] - total), jnp.exp(score[:, LANES:] - total)], axis=1
            )
            if masked:
                prob = jnp.where(causal_mask(), prob, 0.0)
            grad_prob = nt(grad[k], values_here)
            grad_score = prob * (grad_prob - jnp.concatenate([mean, mean], axis=1))
            probs[k * HALF : (k + 1) * HALF, :] = prob.astype(BF16)
            scored[k * HALF : (k + 1) * HALF, :] = grad_score.astype(BF16)
        query_sum[...] += nn(scored[...], keys_here)
        key_sum[at] += nn(query_t[...], scored[...])
        value_sum[at] += nn(grad_t[...], probs[...])

    lax.fori_loop(0, last, lambda at, _: (step(at, False), 0)[1], 0)
    step(last, True)
    for k in range(ways):
        grad_query[k] = query_sum[k * HALF : (k + 1) * HALF, :].astype(BF16)

    @pl.when(block == pl.num_programs(0) - 1)
    def _():
        for p in range(4):
            out = pair_outs[p % 2]
            for h in range(2):
                at = table[POS_AT + 2 * p + h]
                key_part, value_part = key_sum[at], value_sum[at]
                out[p // 2, h, 0:HEAD, :] = ((key_part[0:HEAD] + key_part[HEAD:]) * 0.125).astype(BF16)
                out[p // 2, h, HEAD:, :] = (value_part[0:HEAD] + value_part[HEAD:]).astype(BF16)


def attend_back_stage(table, query, grad, totals, gates, gate_grads, pairs, seq):
    ways, rows, _ = query.shape
    kv_spec = pl.BlockSpec((rows, LANES), lambda b: (0, 0))
    spec = pl.BlockSpec((ways, HALF, LANES), lambda b: (0, b, 0))
    pair_spec = pl.BlockSpec((2, 2, LANES, HALF), lambda b: (0, 0, 0, 0))
    return pl.pallas_call(
        attend_back_kernel,
        cost_estimate=cost(16),
        grid=(rows // HALF,),
        in_specs=[smem_spec()] + [spec] * 2 + [pl.BlockSpec((HALF, LANES), lambda b: (b, 0))] * 3 + [kv_spec] * 4,
        out_specs=(spec,) + (pair_spec,) * 2,
        out_shape=(shaped((ways, rows, LANES), BF16),) + (shaped((2, 2, LANES, HALF), BF16),) * 2,
        scratch_shapes=[
            pltpu.VMEM((seq, LANES), BF16),
            pltpu.VMEM((seq, LANES), BF16),
            pltpu.VMEM((seq // HALF, LANES, HALF), F32),
            pltpu.VMEM((seq // HALF, LANES, HALF), F32),
            pltpu.VMEM((ways * HALF, LANES), F32),
            pltpu.VMEM((LANES, ways * HALF), BF16),
            pltpu.VMEM((LANES, ways * HALF), BF16),
            pltpu.VMEM((ways * HALF, HALF), BF16),
            pltpu.VMEM((ways * HALF, HALF), BF16),
            pltpu.VMEM((ways, HALF, LANES), F32),
            pltpu.VMEM((ways, HALF, LANES), F32),
        ],
        compiler_params=params(20),
    )(table, query, grad, totals, gates, gate_grads, *pairs)


def in_order(table, turned, target):
    for place in range(8):
        target[place * ROWS : (place + 1) * ROWS, :] = turned[rows_at(table[OUT_AT + place], ROWS), :]


def put_blocks(grads, outs, slot, column_to):
    keep_a, keep_b, send_a, send_b = outs
    y, core = slot // 2, slot % 2
    wide = grads.shape[1]
    for s in range(4):
        for x in range(2):
            block = grads[(2 * s + x) * ROWS : (2 * s + x + 1) * ROWS, :].astype(BF16)
            if s in (1, 2):
                out, place = (send_a if core else keep_a), (y, x, s - 1)
            else:
                out, place = (send_b if core else keep_b), (x, y, s // 2)
            out[place[0], place[1], place[2], 0:ROWS, column_to : column_to + wide] = block


def middle_kernel(table, low_tok, low_cot, cross, heads, gates, routes, vectors, up_bias, *refs):
    pieces = refs[:8]
    low_out, high_out, grad_mid, back, sums, bias_grad = refs[8:14]
    blocks = refs[14:18]
    weight, mixed, turned, ordered, hid_scr, pre_scr = refs[18:]
    ways, rows, _ = heads.shape
    width = low_tok.shape[1]
    group = mixed.shape[2]
    hidden = hid_scr.shape[2]
    place_weights(table, pieces, weight)

    def expand(at):
        held = [
            (heads[k, at, :].astype(F32) * gates[at, k : k + 1]).astype(BF16) for k in range(ways)
        ]
        spread_pairs(table, routes, at, held, mixed)

    over_chunks(rows, expand)
    middle = jnp.concatenate([low_tok[0:HALF, :], cross[0:HALF, :]], axis=0).astype(F32)
    for slot in range(4):
        middle = middle + nt(mixed[slot], weight[slot, :, 0:group])
    scaled, inverse = norm_parts(middle)
    gain = vectors[2:3, :]
    normed = (scaled * gain + vectors[3:4, :]).astype(BF16)
    turned[0] = normed.T
    in_order(table, turned.at[0], ordered.at[0])
    cot = jnp.concatenate([low_cot[0:HALF, :], cross[HALF:, :]], axis=0)
    turned[1] = cot.T
    in_order(table, turned.at[1], ordered.at[1])
    result = middle + vectors[4:5, :]
    grad_normed = jnp.zeros((rows, width), F32)
    up_at, down_at = group, group + hidden
    for slot in range(4):
        bias = up_bias[pl.ds(table[SLOT_AT + slot], 1), :]
        preact = nn(normed, weight[slot, :, up_at:down_at]) + bias
        share = jax.nn.sigmoid(preact)
        active = (preact * share).astype(BF16)
        hid_scr[slot] = active
        slope = share * (1.0 + preact * (1.0 - share))
        grad_pre = (nn(cot, weight[slot, :, down_at:]) * slope).astype(BF16)
        pre_scr[slot] = grad_pre
        bias_grad[pl.ds(table[SLOT_AT + slot], 1), :] = jnp.sum(
            grad_pre.astype(F32), axis=0, keepdims=True
        )
        result = result + nt(hid_scr[slot], weight[slot, :, down_at:])
        grad_normed = grad_normed + nt(pre_scr[slot], weight[slot, :, up_at:down_at])
        put_blocks(nn(ordered[0], pre_scr[slot]), blocks, slot, up_at)
        put_blocks(nn(ordered[1], hid_scr[slot]), blocks, slot, down_at)
    low_out[...] = result[0:HALF].astype(BF16)
    high_out[...] = result[HALF:].astype(BF16)
    cot_wide = cot.astype(F32)
    sums[...] = jnp.zeros_like(sums)
    sums[2:3, :] = jnp.sum(grad_normed * scaled, axis=0, keepdims=True)
    sums[3:4, :] = jnp.sum(grad_normed, axis=0, keepdims=True)
    sums[4:5, :] = jnp.sum(cot_wide, axis=0, keepdims=True)
    grad_middle = cot_wide + norm_backward(grad_normed, scaled, inverse, gain)
    grad_mid[...] = grad_middle
    grad_attn = grad_middle.astype(BF16)
    turned[2] = grad_attn.T
    in_order(table, turned.at[2], ordered.at[2])
    for slot in range(4):
        put_blocks(nn(ordered[2], mixed[slot]), blocks, slot, 0)
        back[slot] = nn(grad_attn, weight[slot, :, 0:group]).astype(BF16)


def select_kernel(table, back, heads, gates, routes, grad_ref, grad_gate):
    ways, rows, _ = heads.shape
    lane = lax.broadcasted_iota(jnp.int32, (CHUNK, LANES), 1)
    ones = jnp.ones((LANES, LANES), BF16)

    def step(at):
        gate_grads = jnp.zeros((CHUNK, LANES), F32)
        for k, value in enumerate(select_pairs(table, routes, at, ways, back)):
            gate_grads = jnp.where(lane == k, nn(value * heads[k, at, :], ones), gate_grads)
            grad_ref[k, at, :] = (value.astype(F32) * gates[at, k : k + 1]).astype(BF16)
        grad_gate[at, :] = gate_grads

    over_chunks(rows, step)


def select_stage(table, back, heads, gates, routes):
    ways, rows, _ = heads.shape
    vmem = pl.BlockSpec(memory_space=pltpu.VMEM)
    return pl.pallas_call(
        select_kernel,
        cost_estimate=cost(8),
        in_specs=[smem_spec()] + [vmem] * 4,
        out_shape=(
            shaped((ways, rows, LANES), BF16),
            shaped((rows, LANES), F32),
        ),
        compiler_params=params(16),
    )(table, back, heads, gates, routes)


def middle_stage(table, tokens, cot, cross, heads, gates, routes, vectors, up_bias, pieces):
    rows, width = tokens.shape
    packed = pieces[0].shape[2]
    hidden = up_bias.shape[1]
    group = packed - 2 * hidden
    block = shaped((2, 2, 2, ROWS, packed), BF16)
    vmem = pl.BlockSpec(memory_space=pltpu.VMEM)
    return pl.pallas_call(
        middle_kernel,
        cost_estimate=cost(36),
        in_specs=[smem_spec()] + [vmem] * 16,
        out_shape=(
            shaped((HALF, width), BF16),
            shaped((rows - HALF, width), BF16),
            shaped((rows, width), F32),
            shaped((4, rows, group), BF16),
            shaped((8, width), F32),
            shaped((8, hidden), F32),
            block,
            block,
            block,
            block,
        ),
        scratch_shapes=[
            pltpu.VMEM((4, width, packed), BF16),
            pltpu.VMEM((4, rows, group), BF16),
            pltpu.VMEM((3, width, rows), BF16),
            pltpu.VMEM((3, width, rows), BF16),
            pltpu.VMEM((4, rows, hidden), BF16),
            pltpu.VMEM((4, rows, hidden), BF16),
        ],
        compiler_params=params(40),
    )(table, tokens, cot, cross, heads, gates, routes, vectors, up_bias, *pieces)


def spread_kernel(table, grad_query, normed, routes, spread, grads, turned, normed_t):
    ways, rows, _ = grad_query.shape

    def expand(at):
        spread_pairs(table, routes, at, [grad_query[k, at, :] for k in range(ways)], spread)

    over_chunks(rows, expand)
    turned[...] = normed[...].T
    in_order(table, turned, normed_t)
    for slot in range(4):
        grads[slot] = nn(normed_t[...], spread[slot]).astype(BF16)


def spread_stage(table, grad_query, normed, routes, group):
    rows, width = normed.shape
    vmem = pl.BlockSpec(memory_space=pltpu.VMEM)
    return pl.pallas_call(
        spread_kernel,
        cost_estimate=cost(6),
        in_specs=[smem_spec()] + [vmem] * 3,
        out_shape=(shaped((4, rows, group), BF16), shaped((4, width, group), BF16)),
        scratch_shapes=[pltpu.VMEM((width, rows), BF16), pltpu.VMEM((width, rows), BF16)],
        compiler_params=params(16),
    )(table, grad_query, normed, routes)


def last_kernel(
    table, low_tok, cross, grad_mid, spread, normed, routes, gates, grad_gate, weight, small,
    vectors, sums, bias_grad, pair_keep, pair_got, pair_far, grads, low_out, high_out, *refs
):
    blocks, (pair_grad, tiny, wide, extra) = refs[:4], refs[4:]
    keep_a, keep_b, send_a, send_b = blocks
    rows = normed.shape[0]
    ways = routes.shape[1]
    for h in range(2):
        total = pair_keep[0, h].astype(F32) + pair_got[0, h].astype(F32) + pair_far[h].astype(F32)
        pair_grad[h * HALF : (h + 1) * HALF, :] = total.T.astype(BF16)
    gate = gates[...]
    gate_grad = grad_gate[...]
    chosen_grad = gate * (gate_grad - jnp.sum(gate * gate_grad, axis=-1, keepdims=True))
    lane = lax.broadcasted_iota(jnp.int32, (rows, LANES), 1)
    logit_grad = jnp.zeros((rows, LANES), F32)
    for k in range(ways):
        logit_grad = jnp.where(lane == routes[:, k : k + 1], chosen_grad[:, k : k + 1], logit_grad)
    logit_low = logit_grad.astype(BF16)
    normed_t = normed[...].T
    grad_normed = nt(pair_grad[...], small[:, 0:LANES]) + nt(logit_low, small[:, LANES : 2 * LANES])
    for slot in range(4):
        grad_normed = grad_normed + nt(spread[slot], weight[slot])
    tokens = jnp.concatenate([low_tok[0:HALF, :], cross[0:HALF, :]], axis=0).astype(F32)
    scaled, inverse = norm_parts(tokens)
    back = grad_mid[...] + norm_backward(grad_normed, scaled, inverse, vectors[0:1, :])
    low_out[...] = back[0:HALF]
    high_out[...] = back[HALF:].astype(BF16)
    wide[...] = jnp.zeros_like(wide)
    wide[24:32, :] = sums[...]
    wide[24:25, :] = jnp.sum(grad_normed * scaled, axis=0, keepdims=True)
    wide[25:26, :] = jnp.sum(grad_normed, axis=0, keepdims=True)
    tiny[:, 0:LANES] = nn(normed_t, pair_grad[...]).astype(BF16)
    tiny[:, LANES : 2 * LANES] = (nn(normed_t, logit_low) + wide[...].T).astype(BF16)
    extra[...] = jnp.zeros_like(extra)
    for i in range(32):
        extra[TINY * i : TINY * i + 1, 0:HEAD] = bias_grad[i // 8 : i // 8 + 1, (i % 8) * HEAD : (i % 8 + 1) * HEAD]
    tiny[:, 2 * LANES : 3 * LANES] = extra[...].astype(BF16)
    for slot in range(4):
        y, core = slot // 2, slot % 2
        put_blocks(grads[slot], blocks, slot, 0)
        for s in range(4):
            for x in range(2):
                row = table[OUT_AT + 2 * s + x] * 4 + table[SLOT_AT + slot]
                if s in (1, 2):
                    out, place = (send_a if core else keep_a), (y, x, s - 1)
                else:
                    out, place = (send_b if core else keep_b), (x, y, s // 2)
                out[place[0], place[1], place[2], ROWS:, :] = tiny[rows_at(row, TINY), :]


def last_stage(
    table, tokens, cross, grad_mid, spread, normed, routes, gates, grad_gate, weight, small,
    vectors, sums, bias_grad, pair_parts, grads
):
    rows, width = tokens.shape
    block = shaped((2, 2, 2, ROWS + TINY, 3 * LANES), BF16)
    vmem = pl.BlockSpec(memory_space=pltpu.VMEM)
    return pl.pallas_call(
        last_kernel,
        cost_estimate=cost(7),
        in_specs=[smem_spec()] + [vmem] * 17,
        out_shape=(shaped((HALF, width), F32), shaped((rows - HALF, width), BF16), block, block, block, block),
        scratch_shapes=[
            pltpu.VMEM((rows, LANES), BF16),
            pltpu.VMEM((width, 3 * LANES), BF16),
            pltpu.VMEM((LANES, width), F32),
            pltpu.VMEM((width, LANES), F32),
        ],
        compiler_params=params(24),
    )(
        table, tokens, cross, grad_mid, spread, normed, routes, gates, grad_gate, weight, small,
        vectors, sums, bias_grad, *pair_parts, grads
    )


def gather_plain(x, axis, dim):
    return lax.all_gather(x, axis, axis=dim, tiled=True)


def general_pieces(wq, wo, wup, wdown, wk, wv, wr, vectors, bup):
    every = ("dp", "tensor")
    width = wup.shape[0] * lax.axis_size("dp")
    group = wq.shape[0] * HEAD

    def whole(rows):
        return lax.all_gather(gather_plain(rows, "dp", 0), "tensor", axis=0)

    queries = whole(wq.transpose(1, 0, 2).reshape(-1, group))
    second = whole(
        jnp.concatenate([wo.transpose(2, 0, 1).reshape(-1, group), wup, wdown.T], axis=1)
    )
    wide = [gather_plain(w, every, 0) for w in (wk, wv, wr)]
    columns = [gather_plain(v, every, 0)[:, None] for v in vectors]
    bias = jnp.pad(gather_plain(bup, every, 0).reshape(-1, 1, HEAD), ((0, 0), (0, TINY - 1), (0, 0)))
    left = jnp.concatenate(wide + columns, axis=1)
    small = jnp.concatenate(
        [jnp.pad(left, ((0, 0), (0, 2 * LANES - left.shape[1]))), bias.reshape(width, HEAD)], axis=1
    )
    small = jnp.pad(small, ((0, 0), (0, group - small.shape[1])))

    def block_one(slot, place):
        row = (4 * place + slot) * TINY
        return jnp.concatenate([queries[slot, place * ROWS : (place + 1) * ROWS], small[row : row + TINY]])

    first = [jnp.stack([block_one(*at) for at in places]) for places in LAYOUT]
    later = [
        jnp.stack([second[slot, place * ROWS : (place + 1) * ROWS] for slot, place in places])
        for places in LAYOUT
    ]
    return first, later


def general_sum(blocks):
    keep_a, keep_b, send_a, send_b = blocks
    slots = []
    for slot in range(4):
        y, core = slot // 2, slot % 2
        part_a, part_b = (send_a, send_b) if core else (keep_a, keep_b)
        slots.append(
            jnp.stack(
                [
                    (part_a[y, x, s - 1] if s in (1, 2) else part_b[x, y, s // 2])
                    for s in range(4)
                    for x in range(2)
                ]
            )
        )
    return lax.psum(jnp.stack(slots), ("dp", "tensor")).astype(F32)


def general_grads(first, later, experts, hidden, routed):
    group = experts * HEAD
    d, t = lax.axis_index("dp"), lax.axis_index("tensor")
    dp = lax.axis_size("dp")
    width = 8 * ROWS
    first, later = general_sum(first), general_sum(later)
    small = first[:, :, ROWS:].transpose(1, 0, 2, 3).reshape(width, group)
    mine = lax.dynamic_index_in_dim(first[:, :, :ROWS].reshape(4, width, group), t, 0, False)
    rest = lax.dynamic_index_in_dim(later.reshape(4, width, -1), t, 0, False)
    rows = width // dp

    def own(x, length, index):
        return lax.dynamic_slice_in_dim(x, index * length, length, 0)

    query = own(mine, rows, d).reshape(rows, experts, HEAD).transpose(1, 0, 2)
    rest = own(rest, rows, d)
    index = d * 4 + t
    tiny = own(small, rows // 4, index)
    bias = small.reshape(32, TINY, group)[:, 0, 2 * LANES : 2 * LANES + HEAD].reshape(-1)
    return (
        query,
        tiny[:, 0:HEAD],
        tiny[:, HEAD : 2 * HEAD],
        tiny[:, LANES : LANES + routed],
        [tiny[:, LANES + 24 + i] for i in range(5)],
        own(bias, bias.shape[0] // (4 * dp), index),
        rest[:, 0:group].reshape(rows, experts, HEAD).transpose(1, 2, 0),
        rest[:, group : group + hidden],
        rest[:, group + hidden :].T,
    )


def per_device(
    tokens,
    routes,
    cotangent,
    ln1_gain,
    ln1_bias,
    w_key,
    w_value,
    w_router,
    w_query,
    w_out,
    ln2_gain,
    ln2_bias,
    w_up,
    b_up,
    w_down,
    b_down,
):
    dp = lax.axis_size("dp")
    tuned = dp == 8
    d, t = lax.axis_index("dp"), lax.axis_index("tensor")
    seq = routes.shape[0]
    blocks = seq // HALF
    slots = [(t ^ s) if tuned else jnp.int32(s) for s in range(4)]
    z, x = d // 2, d % 2
    if tuned:
        into = [((z + 4 - s) % 4) * 2 + (x ^ o) for s in range(4) for o in range(2)]
        out = [((z + s) % 4) * 2 + (x ^ o) for s in range(4) for o in range(2)]
    else:
        into = out = [jnp.int32(place) for place in range(8)]
    ranks = [t, t ^ 1, t ^ 2, t ^ 3]
    positions = [p for r in ranks for p in (2 * r, blocks - 1 - 2 * r)]
    table = jnp.stack([v.astype(jnp.int32) for v in slots + into + out + positions])
    own_routes = jnp.concatenate(
        [lax.dynamic_slice_in_dim(routes, p * HALF, HALF, 0) for p in positions[0:2]], axis=0
    )
    vectors_in = (ln1_gain, ln1_bias, ln2_gain, ln2_bias, b_down)

    experts, hidden, routed = w_query.shape[0], w_up.shape[1], w_router.shape[1]
    turns, swap = axis_moves(dp)

    def over_x(x):
        return lax.ppermute(x, "dp", swap)

    def over_z(x, step):
        return lax.ppermute(x, "dp", turns[step - 1])

    def over_zx(x, step):
        return lax.ppermute(x, "dp", [(source, target ^ 1) for source, target in turns[step - 1]])

    if tuned:
        first, second, cross = pack(
            w_query, w_out, w_up, w_down.T, w_key, w_value, w_router, tokens, cotangent, vectors_in, b_up
        )
        first, second = first[None], second[None]
        z1, z2, z3 = [over_z(first, step) for step in (1, 2, 3)]
        cross = crossed(cross)
        side_a = jnp.concatenate([after(first, table, own_routes), z1], axis=0)
        side_b = jnp.concatenate([z2, z3], axis=0)
        next_a, next_b = over_y(side_a), over_x(side_b)
        later_z1, later_z3 = [over_z(after(second, z1), step) for step in (1, 3)]
        later_z2 = over_z(later_z1, 1)
        side_a = jnp.concatenate([side_a, after(next_a, later_z1, later_z3, cross)], axis=0)
        side_b = jnp.concatenate([side_b, after(next_b, later_z1, later_z3, cross)], axis=0)
        far_a, far_b = over_x(side_a), over_y(side_b)
        far_a, far_b, later_z2 = together(far_a, far_b, later_z2)
        later_a = jnp.concatenate([after(second, far_a), later_z1], axis=0)
        later_b = jnp.concatenate([later_z2, later_z3], axis=0)
        next_a, next_b = over_y(later_a), over_x(later_b)
        first_pieces = [side_a, far_a, side_b, far_b]
        first_pieces = first_pieces + [over_core(v) for v in first_pieces]
    else:
        first_pieces, second_pieces = general_pieces(
            w_query, w_out, w_up, w_down, w_key, w_value, w_router, vectors_in, b_up
        )
        cross = crossed(jnp.concatenate([tokens[HALF:], cotangent[HALF:]], axis=0))
    normed, pair, gates, small, vectors, up_bias = first_stage(
        table, tokens, cross, own_routes, first_pieces
    )
    pair_y = over_y(pair)
    pairs = (pair, over_core(pair), pair_y, over_core(pair_y))
    if tuned:
        normed, later_a, later_b = together(normed, later_a, later_b)
    query, query_weight = query_stage(table, normed, own_routes, first_pieces)
    if tuned:
        side_a = jnp.concatenate([later_a, after(next_a, query)], axis=0)
        side_b = jnp.concatenate([later_b, after(next_b, query, pair_y)], axis=0)
        far_a, far_b = over_x(side_a), over_y(side_b)
    heads, totals = attend_stage(table, query, pairs, seq)
    if tuned:
        heads, far_a, far_b, core_a, core_b = together(heads, far_a, far_b, over_core(side_a), over_core(side_b))
        second_pieces = [side_a, far_a, side_b, far_b, core_a, over_core(far_a), core_b, over_core(far_b)]
    output, output_high, grad_mid, back, sums, bias_grad, *later_blocks = middle_stage(
        table, tokens, cotangent, cross, heads, gates, own_routes, vectors, up_bias, second_pieces
    )
    if tuned:
        keep_a, keep_b, send_a, send_b = later_blocks
        got_a, got_b = over_core(send_a), over_core(send_b)
    grad_heads, grad_gate = select_stage(table, back, heads, gates, own_routes)
    if tuned:
        grad_heads, grad_gate, output_high, got_a, got_b = together(
            grad_heads, grad_gate, crossed(output_high), got_a, got_b
        )
        part_a, part_b = add_blocks(
            "add_near", [(keep_a, (1,)), (got_a, (1,))], [(keep_b, (1,)), (got_b, (1,))]
        )
        next_a, next_b = over_y(part_a), over_x(part_b)
        grad_heads = after(grad_heads, part_a, part_b)
    grad_query, pair_keep, pair_send = attend_back_stage(
        table, query, grad_heads, totals, gates, grad_gate, pairs, seq
    )
    pair_got = over_core(pair_send)
    (pair_next,) = add_blocks("add_pairs", [(pair_keep, (1,)), (pair_got, (1,))])
    pair_parts = (pair_keep, pair_got, over_y(pair_next))
    if tuned:
        next_a, next_b = after(next_a, pair_next), after(next_b, pair_next)
        part_a, part_b = add_blocks(
            "add_far",
            [(keep_a, (0, 1)), (got_a, (0, 1)), (next_a, (1,))],
            [(keep_b, (0, 1)), (got_b, (0, 1)), (next_b, (1,))],
        )
        last_a = over_x(part_a)
        grad_query = after(grad_query, part_a, part_b)
    else:
        output_high = crossed(output_high)
    spread, query_grads = spread_stage(table, grad_query, normed, own_routes, query_weight.shape[2])
    if tuned:
        spread, pair_far, last_a = together(spread, pair_parts[2], last_a)
        pair_parts = (*pair_parts[0:2], pair_far)
        last_b = over_y(after(part_b, pair_far, spread))

        def final(name, *sides):
            return add_blocks(
                name,
                *[
                    [(keep, (0, 0, s)), (got, (0, 0, s)), (near, (0, s)), (last, (s,))]
                    for keep, got, near, last in sides
                    for s in (0, 1)
                ],
            )

        ahead, beyond = final("add_last", (keep_a, got_a, next_a, last_a))
        beyond = over_z(beyond, 1)
    low_rows, high_rows, *first_blocks = last_stage(
        table, tokens, cross, grad_mid, spread, normed, own_routes, gates, grad_gate,
        query_weight, small, vectors, sums, bias_grad, pair_parts, query_grads,
    )
    if tuned:
        low_rows, high_rows, last_b, beyond, *first_blocks = together(
            low_rows, high_rows, last_b, beyond, *first_blocks
        )
        first_got = over_core(first_blocks[2]), over_core(first_blocks[3])
        kept, back = final("add_last", (keep_b, got_b, next_b, last_b))
        (ahead,) = add_blocks("add_ahead", [(ahead, ()), (beyond, ())])
        one, three = over_z(ahead, 1), over_z(back, 3)
        keep_a, keep_b = first_blocks[0:2]
        got_a, got_b = first_got
        got_a, got_b = after(got_a, ahead, back), after(got_b, ahead, back)
        part_a, part_b = add_blocks(
            "add_near", [(keep_a, (1,)), (got_a, (1,))], [(keep_b, (1,)), (got_b, (1,))]
        )
        next_a, next_b = over_y(part_a), over_x(part_b)
        next_a, next_b = together(next_a, next_b)
        part_a, part_b = add_blocks(
            "add_far",
            [(keep_a, (0, 1)), (got_a, (0, 1)), (next_a, (1,))],
            [(keep_b, (0, 1)), (got_b, (0, 1)), (next_b, (1,))],
        )
        last_a, last_b = over_x(part_a), over_y(part_b)
        last_a, last_b, one, three = together(last_a, last_b, one, three)
        high_rows = after(high_rows, last_b)
        out_grad, up_grad, down_grad = unpack_second(kept, one, three, experts, hidden)
        down_grad = down_grad.T
        done = final("add_last", (keep_a, got_a, next_a, last_a), (keep_b, got_b, next_b, last_b))
        done = (done[2], done[0], done[1], done[3])
        one, two, three = [over_z(done[step], step) for step in (1, 2, 3)]
        result = jnp.concatenate([output, output_high], axis=0)
        grad_tokens = jnp.concatenate([low_rows, crossed(high_rows).astype(F32)], axis=0)
        one = after(one, out_grad, result, grad_tokens)
        parts = (done[0], one, two, three)
        query_grad, key_grad, value_grad, router_grad, small_grads, up_bias_grad = unpack_first(
            parts, experts, routed
        )
    else:
        (
            query_grad, key_grad, value_grad, router_grad, small_grads, up_bias_grad,
            out_grad, up_grad, down_grad,
        ) = general_grads(first_blocks, later_blocks, experts, hidden, routed)
        result = jnp.concatenate([output, output_high], axis=0)
        grad_tokens = jnp.concatenate([low_rows, crossed(high_rows).astype(F32)], axis=0)
    return (
        result,
        grad_tokens,
        small_grads[0],
        small_grads[1],
        key_grad,
        value_grad,
        router_grad,
        query_grad,
        out_grad,
        small_grads[2],
        small_grads[3],
        up_grad,
        up_bias_grad,
        down_grad,
        small_grads[4],
    )


def solution(mesh):
    rows = P(("dp", "tensor"), None)
    vector = P(("dp", "tensor"))
    in_specs = (
        rows,
        P("dp", None),
        rows,
        vector,
        vector,
        rows,
        rows,
        rows,
        P("tensor", "dp", None),
        P("tensor", None, "dp"),
        vector,
        vector,
        P("dp", "tensor"),
        vector,
        P("tensor", "dp"),
        vector,
    )
    out_specs = (
        rows,
        rows,
        vector,
        vector,
        rows,
        rows,
        rows,
        P("tensor", "dp", None),
        P("tensor", None, "dp"),
        vector,
        vector,
        P("dp", "tensor"),
        vector,
        P("tensor", "dp"),
        vector,
    )
    return jax.shard_map(
        per_device, mesh=mesh, in_specs=in_specs, out_specs=out_specs, check_vma=False
    )
```

```python
import jax
import jax.numpy as jnp
from jax import lax
from jax.experimental import pallas as pl
from jax.experimental.pallas import tpu as pltpu
from jax.sharding import PartitionSpec as P

F32 = jnp.float32
BF16 = jnp.bfloat16
HEAD = 64
LANES = 128
HALF = 256
ROWS = 64
TINY = 16
CHUNK = 32

PLACES_A = ((0, 0, 0), (0, 0, 1), (1, 0, 0), (1, 0, 1))
PLACES_XA = tuple((y, 1, s) for y, _, s in PLACES_A)
PLACES_B = ((0, 0, 2), (0, 0, 3), (0, 1, 2), (0, 1, 3))
PLACES_YB = tuple((1, x, s) for _, x, s in PLACES_B)
LAYOUT = tuple(
    tuple((2 * y + core, 2 * s + x) for y, x, s in places)
    for core in (0, 1)
    for places in (PLACES_A, PLACES_XA, PLACES_B, PLACES_YB)
)
SLOT_AT, IN_AT, OUT_AT, POS_AT = 0, 4, 12, 20


def nn(left, right):
    return lax.dot_general(left, right, (((1,), (0,)), ((), ())), preferred_element_type=F32)


def nt(left, right):
    return lax.dot_general(left, right, (((1,), (1,)), ((), ())), preferred_element_type=F32)


def norm_parts(rows):
    average = jnp.mean(rows, axis=-1, keepdims=True)
    centered = rows - average
    inverse = lax.rsqrt(jnp.mean(centered * centered, axis=-1, keepdims=True) + 1e-05)
    return centered * inverse, inverse


def norm_backward(incoming, scaled, inverse, gain):
    weighted = incoming * gain
    return inverse * (
        weighted
        - jnp.mean(weighted, axis=-1, keepdims=True)
        - scaled * jnp.mean(weighted * scaled, axis=-1, keepdims=True)
    )


def smem_spec():
    return pl.BlockSpec(memory_space=pltpu.SMEM)


def params(mebibytes):
    return pltpu.CompilerParams(vmem_limit_bytes=mebibytes * 1024 * 1024)


def cost(microseconds):
    return pl.CostEstimate(flops=0, bytes_accessed=int(microseconds * 3.69e6), transcendentals=0)


def after(value, *earlier):
    return lax.optimization_barrier((value, *earlier))[0]


def together(*values):
    return lax.optimization_barrier(values)


def shaped(shape, kind):
    return jax.ShapeDtypeStruct(shape, kind)


def pack_kernel(
    wq, wo, wup, wdown, wk, wv, wr, tok, cot, g1, b1, g2, b2, bdown, bup, first_ref, second_ref, cross_ref, wide, square
):
    cross_ref[0:HALF, :] = tok[HALF:, :]
    cross_ref[HALF:, :] = cot[HALF:, :]
    experts = wq.shape[0]
    group = experts * HEAD
    hidden = wup.shape[1]
    first_ref[...] = jnp.zeros_like(first_ref)
    for j in range(experts):
        first_ref[0:ROWS, j * HEAD : (j + 1) * HEAD] = wq[j]
    square[...] = jnp.zeros_like(square)
    for i, vector in enumerate((g1, b1, g2, b2, bdown)):
        square[24 + i : 25 + i, 0:TINY] = vector[...].astype(F32)
    columns = square[...].T
    first_ref[ROWS : ROWS + TINY, 0:HEAD] = wk[...]
    first_ref[ROWS : ROWS + TINY, HEAD : 2 * HEAD] = wv[...]
    first_ref[ROWS : ROWS + TINY, LANES : 2 * LANES] = columns[0:TINY, :].astype(BF16)
    first_ref[ROWS : ROWS + TINY, LANES : LANES + wr.shape[1]] = wr[...]
    first_ref[ROWS : ROWS + 1, 2 * LANES : 2 * LANES + HEAD] = bup[...]
    wide[...] = jnp.zeros_like(wide)
    for j in range(experts):
        wide[j * HEAD : (j + 1) * HEAD, 0:ROWS] = wo[j].astype(F32)
    second_ref[:, 0:group] = wide[...].T[0:ROWS].astype(BF16)
    second_ref[:, group : group + hidden] = wup[...]
    second_ref[:, group + hidden :] = wdown[...]


def pack(wq, wo, wup, wdown, wk, wv, wr, tok, cot, vectors, bup):
    group, hidden = wq.shape[0] * HEAD, wup.shape[1]
    return pl.pallas_call(
        pack_kernel,
        cost_estimate=cost(0.2),
        out_shape=(
            shaped((ROWS + TINY, group), BF16),
            shaped((ROWS, group + 2 * hidden), BF16),
            shaped(tok.shape, BF16),
        ),
        scratch_shapes=[
            pltpu.VMEM((group, LANES), F32),
            pltpu.VMEM((LANES, LANES), F32),
        ],
        compiler_params=params(60),
    )(wq, wo, wup, wdown, wk, wv, wr, tok, cot, *[v.reshape(1, -1) for v in vectors], bup.reshape(1, -1))


def sum_four(kept, one, two, three):
    return kept.astype(F32) + one.astype(F32) + two.astype(F32) + three.astype(F32)


def unpack_first_kernel(kept, one, two, three, low, high, gq, gk, gv, gr, *refs):
    vectors, (gb, tokens, total) = refs[:5], refs[5:]
    tokens[0:HALF, :] = low[...]
    tokens[HALF:, :] = high[...].astype(F32)
    total[...] = sum_four(kept[...], one[...], two[...], three[...])
    for j in range(gq.shape[0]):
        gq[j] = total[0:ROWS, j * HEAD : (j + 1) * HEAD]
    small = total[ROWS:, :]
    gk[...] = small[:, 0:HEAD]
    gv[...] = small[:, HEAD : 2 * HEAD]
    gr[...] = small[:, LANES : LANES + gr.shape[1]]
    square = jnp.concatenate(
        [small[:, LANES : 2 * LANES], jnp.zeros((LANES - TINY, LANES), F32)], axis=0
    ).T
    for i, out in enumerate(vectors):
        out[...] = square[24 + i : 25 + i, 0:TINY]
    gb[...] = small[0:1, 2 * LANES : 2 * LANES + HEAD]


def unpack_first(parts, low, high, experts, routed):
    outs = pl.pallas_call(
        unpack_first_kernel,
        cost_estimate=cost(2),
        out_shape=(
            shaped((experts, ROWS, HEAD), F32),
            shaped((TINY, HEAD), F32),
            shaped((TINY, HEAD), F32),
            shaped((TINY, routed), F32),
            *[shaped((1, TINY), F32) for _ in range(5)],
            shaped((1, HEAD), F32),
            shaped((low.shape[0] + high.shape[0], low.shape[1]), F32),
        ),
        scratch_shapes=[pltpu.VMEM(parts[0].shape, F32)],
        compiler_params=params(8),
    )(*parts, low, high)
    return *outs[0:4], [v.reshape(-1) for v in outs[4:9]], outs[9].reshape(-1), outs[10]


def unpack_second_kernel(kept, one, three, low, high, go, gup, gdown, rows, total, wide):
    rows[0:HALF, :] = low[...]
    rows[HALF:, :] = high[...]
    experts = go.shape[0]
    group, hidden = experts * HEAD, gup.shape[1]
    total[...] = kept[...].astype(F32) + one[...].astype(F32) + three[...].astype(F32)
    gup[...] = total[:, group : group + hidden]
    wide[...] = jnp.zeros_like(wide)
    wide[0:ROWS, :] = total[:, 0:group]
    turned = wide[...].T
    for j in range(experts):
        go[j] = turned[j * HEAD : (j + 1) * HEAD, 0:ROWS]
    gdown[...] = total[:, group + hidden :]


def unpack_second(kept, one, three, low, high, experts, hidden):
    group = experts * HEAD
    return pl.pallas_call(
        unpack_second_kernel,
        cost_estimate=cost(2),
        out_shape=(
            shaped((experts, HEAD, ROWS), F32),
            shaped((ROWS, hidden), F32),
            shaped((ROWS, hidden), F32),
            shaped((low.shape[0] + high.shape[0], low.shape[1]), BF16),
        ),
        scratch_shapes=[
            pltpu.VMEM(kept.shape, F32),
            pltpu.VMEM((LANES, group), F32),
        ],
        compiler_params=params(8),
    )(kept, one, three, low, high)


def axis_moves(dp):
    turns = [
        [(d, (d + 2 * step) % dp) for d in range(dp)] for step in range(1, dp // 2)
    ]
    return turns, [(d, d ^ 1) for d in range(dp)]


CORE = [(0, 1), (1, 0), (2, 3), (3, 2)]
ACROSS = [(0, 2), (2, 0), (1, 3), (3, 1)]
CROSSED = [(0, 3), (3, 0), (1, 2), (2, 1)]


def over_core(x):
    return lax.ppermute(x, "tensor", CORE)


def over_y(x):
    return lax.ppermute(x, "tensor", ACROSS)


def crossed(x):
    return lax.ppermute(x, "tensor", CROSSED)


def add_blocks(name, *sums):
    terms = [term for parts in sums for term in parts]
    shapes = [parts[0][0].shape[len(parts[0][1]) :] for parts in sums]
    count = len(terms)

    def kernel(*refs):
        ins, outs = refs[:count], refs[count:]
        at = 0
        for out, parts in zip(outs, sums):
            total = None
            for ref, (_, index) in zip(ins[at : at + len(parts)], parts):
                value = ref[index].astype(F32) if index else ref[...].astype(F32)
                total = value if total is None else total + value
            out[...] = total.astype(BF16)
            at += len(parts)

    kernel.__name__ = name
    size = 0
    for shape, parts in zip(shapes, sums):
        block = 2 * (len(parts) + 1)
        for n in shape:
            block *= n
        size += block
    return pl.pallas_call(
        kernel,
        cost_estimate=pl.CostEstimate(flops=0, bytes_accessed=size, transcendentals=0),
        out_shape=tuple(shaped(shape, BF16) for shape in shapes),
        compiler_params=params(16),
    )(*[array for array, _ in terms])


def place_blocks(table, pieces, row_from, rows, put):
    for piece, places in zip(pieces, LAYOUT):
        for i, (slot, place) in enumerate(places):
            put(slot, table[IN_AT + place], piece[i, row_from : row_from + rows, :])


def rows_at(index, rows):
    return pl.ds(pl.multiple_of(index * rows, rows), rows)


def place_weights(table, pieces, weight):
    def put(slot, block, value):
        weight[slot, rows_at(block, ROWS), :] = value

    place_blocks(table, pieces, 0, ROWS, put)


def first_kernel(table, low_tok, cross, routes, *refs):
    pieces, (normed_ref, kv_ref, gates_ref, small, vectors, up_bias) = refs[:8], refs[8:]

    def put(slot, block, value):
        small[rows_at(block * 4 + table[SLOT_AT + slot], TINY), :] = value

    place_blocks(table, pieces, ROWS, TINY, put)
    tokens = jnp.concatenate([low_tok[0:HALF, :], cross[0:HALF, :]], axis=0).astype(F32)
    scaled, _ = norm_parts(tokens)
    turned = small[:, LANES : 2 * LANES].astype(F32).T
    vectors[...] = turned[24:32, :]
    for i in range(32):
        up_bias[i // 8 : i // 8 + 1, (i % 8) * HEAD : (i % 8 + 1) * HEAD] = small[
            TINY * i : TINY * i + 1, 2 * LANES : 2 * LANES + HEAD
        ].astype(F32)
    normed = (scaled * vectors[0:1, :] + vectors[1:2, :]).astype(BF16)
    normed_ref[...] = normed
    kv_ref[...] = nn(normed, small[:, 0:LANES]).astype(BF16)
    logits = nn(normed, small[:, LANES : 2 * LANES])
    lane = lax.broadcasted_iota(jnp.int32, logits.shape, 1)
    ways = routes.shape[1]
    chosen = [lane == routes[:, k : k + 1] for k in range(ways)]
    member = chosen[0]
    for k in range(1, ways):
        member = member | chosen[k]
    logits = jnp.where(member, logits, -jnp.inf)
    exponent = jnp.exp(logits - jnp.max(logits, axis=-1, keepdims=True))
    shares = exponent / jnp.sum(exponent, axis=-1, keepdims=True)
    gates = jnp.zeros_like(shares)
    for k in range(ways):
        gate = jnp.sum(jnp.where(chosen[k], shares, 0.0), axis=-1, keepdims=True)
        gates = jnp.where(lane == k, gate, gates)
    gates_ref[...] = gates


def first_stage(table, tokens, cross, routes, pieces):
    rows, width = tokens.shape
    return pl.pallas_call(
        first_kernel,
        cost_estimate=cost(0.5),
        in_specs=[smem_spec()] + [pl.BlockSpec(memory_space=pltpu.VMEM)] * 11,
        out_shape=(
            shaped((rows, width), BF16),
            shaped((rows, LANES), BF16),
            shaped((rows, LANES), F32),
            shaped((width, pieces[0].shape[2]), BF16),
            shaped((8, width), F32),
            shaped((8, width), F32),
        ),
        compiler_params=params(14),
    )(table, tokens, cross, routes, *pieces)


def wanted_pairs(routes, at, ways):
    half = (lax.broadcasted_iota(jnp.int32, (CHUNK, LANES), 1) >= HEAD).astype(jnp.int32)
    return [
        (jnp.broadcast_to(routes[at, k : k + 1], half.shape) - half).astype(jnp.int16)
        for k in range(ways)
    ]


def pairs_of(table, experts):
    for slot in range(4):
        for pair in range(experts // 2):
            base = experts * table[SLOT_AT + slot] + 2 * pair
            yield slot, pair, jnp.full((CHUNK, LANES), base, jnp.int32).astype(jnp.int16)


def select_pairs(table, routes, at, ways, source):
    wanted = wanted_pairs(routes, at, ways)
    picked = [jnp.zeros((CHUNK, LANES), BF16)] * ways
    for slot, pair, base in pairs_of(table, source.shape[2] // HEAD):
        value = source[slot, at, pair * LANES : (pair + 1) * LANES]
        for k in range(ways):
            picked[k] = jnp.where(wanted[k] == base, value, picked[k])
    return picked


def spread_pairs(table, routes, at, held, target):
    wanted = wanted_pairs(routes, at, len(held))
    for slot, pair, base in pairs_of(table, target.shape[2] // HEAD):
        value = jnp.zeros((CHUNK, LANES), BF16)
        for k, row in enumerate(held):
            value = jnp.where(wanted[k] == base, row, value)
        target[slot, at, pair * LANES : (pair + 1) * LANES] = value


def over_chunks(rows, step):
    def body(c, _):
        step(pl.ds(pl.multiple_of(c * CHUNK, CHUNK), CHUNK))
        return 0

    lax.fori_loop(0, rows // CHUNK, body, 0)


def query_kernel(table, normed, routes, *refs):
    pieces, (chosen, weight, queries) = refs[:8], refs[8:]
    place_weights(table, pieces, weight)
    for slot in range(4):
        queries[slot] = nn(normed[...], weight[slot]).astype(BF16)
    ways = routes.shape[1]

    def step(at):
        for k, value in enumerate(select_pairs(table, routes, at, ways, queries)):
            chosen[k, at, :] = value

    over_chunks(normed.shape[0], step)


def query_stage(table, normed, routes, pieces):
    rows, width = normed.shape
    group = pieces[0].shape[2]
    return pl.pallas_call(
        query_kernel,
        cost_estimate=cost(0.8),
        in_specs=[smem_spec()] + [pl.BlockSpec(memory_space=pltpu.VMEM)] * 10,
        out_shape=(
            shaped((routes.shape[1], rows, LANES), BF16),
            shaped((4, width, group), BF16),
        ),
        scratch_shapes=[pltpu.VMEM((4, rows, group), BF16)],
        compiler_params=params(16),
    )(table, normed, routes, *pieces)


def place_pair(table, pieces, key_scr, value_scr, ones):
    lower = lax.broadcasted_iota(jnp.int32, (HALF, LANES), 1) < HEAD
    for p, piece in enumerate(pieces):
        for h in range(2):
            both = piece[h * HALF : (h + 1) * HALF, :].astype(F32)
            turned = pltpu.roll(both, HEAD, 1)
            at = pl.ds(pl.multiple_of(table[POS_AT + 2 * p + h] * HALF, HALF), HALF)
            key_scr[at, :] = (jnp.where(lower, both, turned) * 0.125).astype(BF16)
            value_scr[at, 0:LANES] = jnp.where(lower, turned, both).astype(BF16)
            if ones:
                value_scr[at, LANES : 2 * LANES] = jnp.ones((HALF, LANES), BF16)


def causal_mask():
    shape = (HALF, HALF)
    return lax.broadcasted_iota(jnp.int32, shape, 1) <= lax.broadcasted_iota(jnp.int32, shape, 0)


def attend_kernel(table, query, kv0, kv1, kv2, kv3, out_ref, total_ref, keys, values, scores, tops, sums):
    block = pl.program_id(0)
    ways = query.shape[0]

    @pl.when(block == 0)
    def _():
        place_pair(table, (kv0, kv1, kv2, kv3), keys, values, True)

    last = table[POS_AT + block]
    tops[...] = jnp.full_like(tops, -jnp.inf)

    def score(at, masked):
        rows = pl.ds(pl.multiple_of(at * HALF, HALF), HALF)
        keys_here = keys[rows, :]
        for k in range(ways):
            here = nt(query[k], keys_here)
            if masked:
                here = jnp.where(causal_mask(), here, -1e30)
            scores[at, k] = here
            tops[k] = jnp.maximum(tops[k], jnp.maximum(here[:, 0:LANES], here[:, LANES:]))

    lax.fori_loop(0, last, lambda at, _: (score(at, False), 0)[1], 0)
    score(last, True)
    for k in range(ways):
        tops[k] = jnp.broadcast_to(jnp.max(tops[k], axis=-1, keepdims=True), (HALF, LANES))
    sums[...] = jnp.zeros_like(sums)

    def weigh(at, _):
        rows = pl.ds(pl.multiple_of(at * HALF, HALF), HALF)
        values_here = values[rows, :]
        for k in range(ways):
            top = tops[k]
            here = scores[at, k]
            weights = jnp.concatenate(
                [jnp.exp(here[:, 0:LANES] - top), jnp.exp(here[:, LANES:] - top)], axis=1
            ).astype(BF16)
            sums[k] += nn(weights, values_here)
        return 0

    lax.fori_loop(0, last + 1, weigh, 0)
    lane = lax.broadcasted_iota(jnp.int32, (HALF, LANES), 1)
    total = jnp.zeros((HALF, LANES), F32)
    for k in range(ways):
        whole = sums[k]
        out_ref[k] = (whole[:, 0:LANES] / whole[:, LANES:]).astype(BF16)
        total = jnp.where(lane == k, tops[k] + jnp.log(whole[:, LANES:]), total)
    total_ref[...] = total


def attend_stage(table, query, pairs, seq):
    ways, rows, _ = query.shape
    kv_spec = pl.BlockSpec((rows, LANES), lambda b: (0, 0))
    spec = pl.BlockSpec((ways, HALF, LANES), lambda b: (0, b, 0))
    return pl.pallas_call(
        attend_kernel,
        cost_estimate=cost(1.2),
        grid=(rows // HALF,),
        in_specs=[smem_spec(), spec] + [kv_spec] * 4,
        out_specs=(spec, pl.BlockSpec((HALF, LANES), lambda b: (b, 0))),
        out_shape=(shaped((ways, rows, LANES), BF16), shaped((rows, LANES), F32)),
        scratch_shapes=[
            pltpu.VMEM((seq, LANES), BF16),
            pltpu.VMEM((seq, 2 * LANES), BF16),
            pltpu.VMEM((seq // HALF, ways, HALF, HALF), F32),
            pltpu.VMEM((ways, HALF, LANES), F32),
            pltpu.VMEM((ways, HALF, 2 * LANES), F32),
        ],
        compiler_params=params(28),
    )(table, query, *pairs)


def attend_back_kernel(
    table, query, grad, all_totals, gates, gate_grads, kv0, kv1, kv2, kv3, grad_query, *refs
):
    pair_outs, (keys, values, key_sum, value_sum, query_sum, query_t, grad_t, probs, scored, totals, inner) = refs[:2], refs[2:]
    block = pl.program_id(0)
    ways = query.shape[0]

    @pl.when(block == 0)
    def _():
        place_pair(table, (kv0, kv1, kv2, kv3), keys, values, False)
        key_sum[...] = jnp.zeros_like(key_sum)
        value_sum[...] = jnp.zeros_like(value_sum)

    last = table[POS_AT + block]
    query_sum[...] = jnp.zeros_like(query_sum)
    for k in range(ways):
        query_t[:, k * HALF : (k + 1) * HALF] = query[k].T
        grad_t[:, k * HALF : (k + 1) * HALF] = grad[k].T
        totals[k] = jnp.broadcast_to(all_totals[:, k : k + 1], (HALF, LANES))
        inner[k] = jnp.broadcast_to(gates[:, k : k + 1] * gate_grads[:, k : k + 1], (HALF, LANES))

    def step(at, masked):
        rows = pl.ds(pl.multiple_of(at * HALF, HALF), HALF)
        keys_here = keys[rows, :]
        values_here = values[rows, :]
        for k in range(ways):
            score = nt(query[k], keys_here)
            total, mean = totals[k], inner[k]
            prob = jnp.concatenate(
                [jnp.exp(score[:, 0:LANES] - total), jnp.exp(score[:, LANES:] - total)], axis=1
            )
            if masked:
                prob = jnp.where(causal_mask(), prob, 0.0)
            grad_prob = nt(grad[k], values_here)
            grad_score = prob * (grad_prob - jnp.concatenate([mean, mean], axis=1))
            probs[k * HALF : (k + 1) * HALF, :] = prob.astype(BF16)
            scored[k * HALF : (k + 1) * HALF, :] = grad_score.astype(BF16)
        query_sum[...] += nn(scored[...], keys_here)
        key_sum[at] += nn(query_t[...], scored[...])
        value_sum[at] += nn(grad_t[...], probs[...])

    lax.fori_loop(0, last, lambda at, _: (step(at, False), 0)[1], 0)
    step(last, True)
    for k in range(ways):
        grad_query[k] = query_sum[k * HALF : (k + 1) * HALF, :].astype(BF16)

    @pl.when(block == pl.num_programs(0) - 1)
    def _():
        for p in range(4):
            out = pair_outs[p % 2]
            for h in range(2):
                at = table[POS_AT + 2 * p + h]
                key_part, value_part = key_sum[at], value_sum[at]
                out[p // 2, h, 0:HEAD, :] = ((key_part[0:HEAD] + key_part[HEAD:]) * 0.125).astype(BF16)
                out[p // 2, h, HEAD:, :] = (value_part[0:HEAD] + value_part[HEAD:]).astype(BF16)


def attend_back_stage(table, query, grad, totals, gates, gate_grads, pairs, seq):
    ways, rows, _ = query.shape
    kv_spec = pl.BlockSpec((rows, LANES), lambda b: (0, 0))
    spec = pl.BlockSpec((ways, HALF, LANES), lambda b: (0, b, 0))
    pair_spec = pl.BlockSpec((2, 2, LANES, HALF), lambda b: (0, 0, 0, 0))
    return pl.pallas_call(
        attend_back_kernel,
        cost_estimate=cost(16),
        grid=(rows // HALF,),
        in_specs=[smem_spec()] + [spec] * 2 + [pl.BlockSpec((HALF, LANES), lambda b: (b, 0))] * 3 + [kv_spec] * 4,
        out_specs=(spec,) + (pair_spec,) * 2,
        out_shape=(shaped((ways, rows, LANES), BF16),) + (shaped((2, 2, LANES, HALF), BF16),) * 2,
        scratch_shapes=[
            pltpu.VMEM((seq, LANES), BF16),
            pltpu.VMEM((seq, LANES), BF16),
            pltpu.VMEM((seq // HALF, LANES, HALF), F32),
            pltpu.VMEM((seq // HALF, LANES, HALF), F32),
            pltpu.VMEM((ways * HALF, LANES), F32),
            pltpu.VMEM((LANES, ways * HALF), BF16),
            pltpu.VMEM((LANES, ways * HALF), BF16),
            pltpu.VMEM((ways * HALF, HALF), BF16),
            pltpu.VMEM((ways * HALF, HALF), BF16),
            pltpu.VMEM((ways, HALF, LANES), F32),
            pltpu.VMEM((ways, HALF, LANES), F32),
        ],
        compiler_params=params(20),
    )(table, query, grad, totals, gates, gate_grads, *pairs)


def in_order(table, turned, target):
    for place in range(8):
        target[place * ROWS : (place + 1) * ROWS, :] = turned[rows_at(table[OUT_AT + place], ROWS), :]


def put_blocks(grads, outs, slot, column_to):
    keep_a, keep_b, send_a, send_b = outs
    y, core = slot // 2, slot % 2
    wide = grads.shape[1]
    for s in range(4):
        for x in range(2):
            block = grads[(2 * s + x) * ROWS : (2 * s + x + 1) * ROWS, :].astype(BF16)
            if s in (1, 2):
                out, place = (send_a if core else keep_a), (y, x, s - 1)
            else:
                out, place = (send_b if core else keep_b), (x, y, s // 2)
            out[place[0], place[1], place[2], 0:ROWS, column_to : column_to + wide] = block


def prepare_kernel(table, heads, gates, routes, low_cot, cross, mixed, cot_t, turned):
    ways, rows, _ = heads.shape

    def expand(at):
        held = [
            (heads[k, at, :].astype(F32) * gates[at, k : k + 1]).astype(BF16) for k in range(ways)
        ]
        spread_pairs(table, routes, at, held, mixed)

    over_chunks(rows, expand)
    turned[...] = jnp.concatenate([low_cot[0:HALF, :], cross[HALF:, :]], axis=0).T
    in_order(table, turned, cot_t)


def prepare_stage(table, heads, gates, routes, cot, cross, group):
    rows, width = cot.shape
    return pl.pallas_call(
        prepare_kernel,
        cost_estimate=cost(0.3),
        in_specs=[smem_spec()] + [pl.BlockSpec(memory_space=pltpu.VMEM)] * 5,
        out_shape=(shaped((4, rows, group), BF16), shaped((width, rows), BF16)),
        scratch_shapes=[pltpu.VMEM((width, rows), BF16)],
        compiler_params=params(12),
    )(table, heads, gates, routes, cot, cross)


def middle_kernel(table, low_tok, low_cot, cross, mixed, cot_t, vectors, up_bias, *refs):
    pieces = refs[:8]
    low_out, high_out, grad_mid, back, sums, bias_grad = refs[8:14]
    blocks = refs[14:18]
    weight, turned, ordered, hid_scr, pre_scr = refs[18:]
    rows, width = low_tok.shape
    group = mixed.shape[2]
    hidden = hid_scr.shape[2]
    place_weights(table, pieces, weight)
    middle = jnp.concatenate([low_tok[0:HALF, :], cross[0:HALF, :]], axis=0).astype(F32)
    for slot in range(4):
        middle = middle + nt(mixed[slot], weight[slot, :, 0:group])
    scaled, inverse = norm_parts(middle)
    gain = vectors[2:3, :]
    normed = (scaled * gain + vectors[3:4, :]).astype(BF16)
    turned[0] = normed.T
    in_order(table, turned.at[0], ordered.at[0])
    cot = jnp.concatenate([low_cot[0:HALF, :], cross[HALF:, :]], axis=0)
    result = middle + vectors[4:5, :]
    grad_normed = jnp.zeros((rows, width), F32)
    up_at, down_at = group, group + hidden
    for slot in range(4):
        bias = up_bias[pl.ds(table[SLOT_AT + slot], 1), :]
        preact = nn(normed, weight[slot, :, up_at:down_at]) + bias
        share = jax.nn.sigmoid(preact)
        active = (preact * share).astype(BF16)
        hid_scr[slot] = active
        slope = share * (1.0 + preact * (1.0 - share))
        grad_pre = (nn(cot, weight[slot, :, down_at:]) * slope).astype(BF16)
        pre_scr[slot] = grad_pre
        bias_grad[pl.ds(table[SLOT_AT + slot], 1), :] = jnp.sum(
            grad_pre.astype(F32), axis=0, keepdims=True
        )
        result = result + nt(hid_scr[slot], weight[slot, :, down_at:])
        grad_normed = grad_normed + nt(pre_scr[slot], weight[slot, :, up_at:down_at])
        put_blocks(nn(ordered[0], pre_scr[slot]), blocks, slot, up_at)
        put_blocks(nn(cot_t[...], hid_scr[slot]), blocks, slot, down_at)
    low_out[...] = result[0:HALF].astype(BF16)
    high_out[...] = result[HALF:].astype(BF16)
    cot_wide = cot.astype(F32)
    sums[...] = jnp.zeros_like(sums)
    sums[2:3, :] = jnp.sum(grad_normed * scaled, axis=0, keepdims=True)
    sums[3:4, :] = jnp.sum(grad_normed, axis=0, keepdims=True)
    sums[4:5, :] = jnp.sum(cot_wide, axis=0, keepdims=True)
    grad_middle = cot_wide + norm_backward(grad_normed, scaled, inverse, gain)
    grad_mid[...] = grad_middle
    grad_attn = grad_middle.astype(BF16)
    turned[1] = grad_attn.T
    in_order(table, turned.at[1], ordered.at[1])
    for slot in range(4):
        put_blocks(nn(ordered[1], mixed[slot]), blocks, slot, 0)
        back[slot] = nn(grad_attn, weight[slot, :, 0:group]).astype(BF16)


def select_kernel(table, back, heads, gates, routes, grad_ref, grad_gate):
    ways, rows, _ = heads.shape
    lane = lax.broadcasted_iota(jnp.int32, (CHUNK, LANES), 1)
    ones = jnp.ones((LANES, LANES), BF16)

    def step(at):
        gate_grads = jnp.zeros((CHUNK, LANES), F32)
        for k, value in enumerate(select_pairs(table, routes, at, ways, back)):
            gate_grads = jnp.where(lane == k, nn(value * heads[k, at, :], ones), gate_grads)
            grad_ref[k, at, :] = (value.astype(F32) * gates[at, k : k + 1]).astype(BF16)
        grad_gate[at, :] = gate_grads

    over_chunks(rows, step)


def select_stage(table, back, heads, gates, routes):
    ways, rows, _ = heads.shape
    vmem = pl.BlockSpec(memory_space=pltpu.VMEM)
    return pl.pallas_call(
        select_kernel,
        cost_estimate=cost(8),
        in_specs=[smem_spec()] + [vmem] * 4,
        out_shape=(
            shaped((ways, rows, LANES), BF16),
            shaped((rows, LANES), F32),
        ),
        compiler_params=params(16),
    )(table, back, heads, gates, routes)


def middle_stage(table, tokens, cot, cross, mixed, cot_t, vectors, up_bias, pieces):
    rows, width = tokens.shape
    packed = pieces[0].shape[2]
    hidden = up_bias.shape[1]
    group = packed - 2 * hidden
    block = shaped((2, 2, 2, ROWS, packed), BF16)
    vmem = pl.BlockSpec(memory_space=pltpu.VMEM)
    return pl.pallas_call(
        middle_kernel,
        cost_estimate=cost(36),
        in_specs=[smem_spec()] + [vmem] * 15,
        out_shape=(
            shaped((HALF, width), BF16),
            shaped((rows - HALF, width), BF16),
            shaped((rows, width), F32),
            shaped((4, rows, group), BF16),
            shaped((8, width), F32),
            shaped((8, hidden), F32),
            block,
            block,
            block,
            block,
        ),
        scratch_shapes=[
            pltpu.VMEM((4, width, packed), BF16),
            pltpu.VMEM((2, width, rows), BF16),
            pltpu.VMEM((2, width, rows), BF16),
            pltpu.VMEM((4, rows, hidden), BF16),
            pltpu.VMEM((4, rows, hidden), BF16),
        ],
        compiler_params=params(28),
    )(table, tokens, cot, cross, mixed, cot_t, vectors, up_bias, *pieces)


def spread_kernel(table, grad_query, normed, routes, spread, grads, turned, normed_t):
    ways, rows, _ = grad_query.shape

    def expand(at):
        spread_pairs(table, routes, at, [grad_query[k, at, :] for k in range(ways)], spread)

    over_chunks(rows, expand)
    turned[...] = normed[...].T
    in_order(table, turned, normed_t)
    for slot in range(4):
        grads[slot] = nn(normed_t[...], spread[slot]).astype(BF16)


def spread_stage(table, grad_query, normed, routes, group):
    rows, width = normed.shape
    vmem = pl.BlockSpec(memory_space=pltpu.VMEM)
    return pl.pallas_call(
        spread_kernel,
        cost_estimate=cost(6),
        in_specs=[smem_spec()] + [vmem] * 3,
        out_shape=(shaped((4, rows, group), BF16), shaped((4, width, group), BF16)),
        scratch_shapes=[pltpu.VMEM((width, rows), BF16), pltpu.VMEM((width, rows), BF16)],
        compiler_params=params(16),
    )(table, grad_query, normed, routes)


def last_kernel(
    table, low_tok, cross, grad_mid, spread, normed, routes, gates, grad_gate, weight, small,
    vectors, sums, bias_grad, pair_keep, pair_got, pair_far, grads, low_out, high_out, *refs
):
    blocks, (pair_grad, tiny, wide, extra) = refs[:4], refs[4:]
    keep_a, keep_b, send_a, send_b = blocks
    rows = normed.shape[0]
    ways = routes.shape[1]
    for h in range(2):
        total = pair_keep[0, h].astype(F32) + pair_got[0, h].astype(F32) + pair_far[h].astype(F32)
        pair_grad[h * HALF : (h + 1) * HALF, :] = total.T.astype(BF16)
    gate = gates[...]
    gate_grad = grad_gate[...]
    chosen_grad = gate * (gate_grad - jnp.sum(gate * gate_grad, axis=-1, keepdims=True))
    lane = lax.broadcasted_iota(jnp.int32, (rows, LANES), 1)
    logit_grad = jnp.zeros((rows, LANES), F32)
    for k in range(ways):
        logit_grad = jnp.where(lane == routes[:, k : k + 1], chosen_grad[:, k : k + 1], logit_grad)
    logit_low = logit_grad.astype(BF16)
    normed_t = normed[...].T
    grad_normed = nt(pair_grad[...], small[:, 0:LANES]) + nt(logit_low, small[:, LANES : 2 * LANES])
    for slot in range(4):
        grad_normed = grad_normed + nt(spread[slot], weight[slot])
    tokens = jnp.concatenate([low_tok[0:HALF, :], cross[0:HALF, :]], axis=0).astype(F32)
    scaled, inverse = norm_parts(tokens)
    back = grad_mid[...] + norm_backward(grad_normed, scaled, inverse, vectors[0:1, :])
    low_out[...] = back[0:HALF]
    high_out[...] = back[HALF:].astype(BF16)
    wide[...] = jnp.zeros_like(wide)
    wide[24:32, :] = sums[...]
    wide[24:25, :] = jnp.sum(grad_normed * scaled, axis=0, keepdims=True)
    wide[25:26, :] = jnp.sum(grad_normed, axis=0, keepdims=True)
    tiny[:, 0:LANES] = nn(normed_t, pair_grad[...]).astype(BF16)
    tiny[:, LANES : 2 * LANES] = (nn(normed_t, logit_low) + wide[...].T).astype(BF16)
    extra[...] = jnp.zeros_like(extra)
    for i in range(32):
        extra[TINY * i : TINY * i + 1, 0:HEAD] = bias_grad[i // 8 : i // 8 + 1, (i % 8) * HEAD : (i % 8 + 1) * HEAD]
    tiny[:, 2 * LANES : 3 * LANES] = extra[...].astype(BF16)
    for slot in range(4):
        y, core = slot // 2, slot % 2
        put_blocks(grads[slot], blocks, slot, 0)
        for s in range(4):
            for x in range(2):
                row = table[OUT_AT + 2 * s + x] * 4 + table[SLOT_AT + slot]
                if s in (1, 2):
                    out, place = (send_a if core else keep_a), (y, x, s - 1)
                else:
                    out, place = (send_b if core else keep_b), (x, y, s // 2)
                out[place[0], place[1], place[2], ROWS:, :] = tiny[rows_at(row, TINY), :]


def last_stage(
    table, tokens, cross, grad_mid, spread, normed, routes, gates, grad_gate, weight, small,
    vectors, sums, bias_grad, pair_parts, grads
):
    rows, width = tokens.shape
    block = shaped((2, 2, 2, ROWS + TINY, 3 * LANES), BF16)
    vmem = pl.BlockSpec(memory_space=pltpu.VMEM)
    return pl.pallas_call(
        last_kernel,
        cost_estimate=cost(7),
        in_specs=[smem_spec()] + [vmem] * 17,
        out_shape=(shaped((HALF, width), F32), shaped((rows - HALF, width), BF16), block, block, block, block),
        scratch_shapes=[
            pltpu.VMEM((rows, LANES), BF16),
            pltpu.VMEM((width, 3 * LANES), BF16),
            pltpu.VMEM((LANES, width), F32),
            pltpu.VMEM((width, LANES), F32),
        ],
        compiler_params=params(24),
    )(
        table, tokens, cross, grad_mid, spread, normed, routes, gates, grad_gate, weight, small,
        vectors, sums, bias_grad, *pair_parts, grads
    )


def gather_plain(x, axis, dim):
    return lax.all_gather(x, axis, axis=dim, tiled=True)


def general_pieces(wq, wo, wup, wdown, wk, wv, wr, vectors, bup):
    every = ("dp", "tensor")
    width = wup.shape[0] * lax.axis_size("dp")
    group = wq.shape[0] * HEAD

    def whole(rows):
        return lax.all_gather(gather_plain(rows, "dp", 0), "tensor", axis=0)

    queries = whole(wq.transpose(1, 0, 2).reshape(-1, group))
    second = whole(
        jnp.concatenate([wo.transpose(2, 0, 1).reshape(-1, group), wup, wdown.T], axis=1)
    )
    wide = [gather_plain(w, every, 0) for w in (wk, wv, wr)]
    columns = [gather_plain(v, every, 0)[:, None] for v in vectors]
    bias = jnp.pad(gather_plain(bup, every, 0).reshape(-1, 1, HEAD), ((0, 0), (0, TINY - 1), (0, 0)))
    left = jnp.concatenate(wide + columns, axis=1)
    small = jnp.concatenate(
        [jnp.pad(left, ((0, 0), (0, 2 * LANES - left.shape[1]))), bias.reshape(width, HEAD)], axis=1
    )
    small = jnp.pad(small, ((0, 0), (0, group - small.shape[1])))

    def block_one(slot, place):
        row = (4 * place + slot) * TINY
        return jnp.concatenate([queries[slot, place * ROWS : (place + 1) * ROWS], small[row : row + TINY]])

    first = [jnp.stack([block_one(*at) for at in places]) for places in LAYOUT]
    later = [
        jnp.stack([second[slot, place * ROWS : (place + 1) * ROWS] for slot, place in places])
        for places in LAYOUT
    ]
    return first, later


def general_sum(blocks):
    keep_a, keep_b, send_a, send_b = blocks
    slots = []
    for slot in range(4):
        y, core = slot // 2, slot % 2
        part_a, part_b = (send_a, send_b) if core else (keep_a, keep_b)
        slots.append(
            jnp.stack(
                [
                    (part_a[y, x, s - 1] if s in (1, 2) else part_b[x, y, s // 2])
                    for s in range(4)
                    for x in range(2)
                ]
            )
        )
    return lax.psum(jnp.stack(slots), ("dp", "tensor")).astype(F32)


def general_grads(first, later, experts, hidden, routed):
    group = experts * HEAD
    d, t = lax.axis_index("dp"), lax.axis_index("tensor")
    dp = lax.axis_size("dp")
    width = 8 * ROWS
    first, later = general_sum(first), general_sum(later)
    small = first[:, :, ROWS:].transpose(1, 0, 2, 3).reshape(width, group)
    mine = lax.dynamic_index_in_dim(first[:, :, :ROWS].reshape(4, width, group), t, 0, False)
    rest = lax.dynamic_index_in_dim(later.reshape(4, width, -1), t, 0, False)
    rows = width // dp

    def own(x, length, index):
        return lax.dynamic_slice_in_dim(x, index * length, length, 0)

    query = own(mine, rows, d).reshape(rows, experts, HEAD).transpose(1, 0, 2)
    rest = own(rest, rows, d)
    index = d * 4 + t
    tiny = own(small, rows // 4, index)
    bias = small.reshape(32, TINY, group)[:, 0, 2 * LANES : 2 * LANES + HEAD].reshape(-1)
    return (
        query,
        tiny[:, 0:HEAD],
        tiny[:, HEAD : 2 * HEAD],
        tiny[:, LANES : LANES + routed],
        [tiny[:, LANES + 24 + i] for i in range(5)],
        own(bias, bias.shape[0] // (4 * dp), index),
        rest[:, 0:group].reshape(rows, experts, HEAD).transpose(1, 2, 0),
        rest[:, group : group + hidden],
        rest[:, group + hidden :].T,
    )


def per_device(
    tokens,
    routes,
    cotangent,
    ln1_gain,
    ln1_bias,
    w_key,
    w_value,
    w_router,
    w_query,
    w_out,
    ln2_gain,
    ln2_bias,
    w_up,
    b_up,
    w_down,
    b_down,
):
    dp = lax.axis_size("dp")
    tuned = dp == 8
    d, t = lax.axis_index("dp"), lax.axis_index("tensor")
    seq = routes.shape[0]
    blocks = seq // HALF
    slots = [(t ^ s) if tuned else jnp.int32(s) for s in range(4)]
    z, x = d // 2, d % 2
    if tuned:
        into = [((z + 4 - s) % 4) * 2 + (x ^ o) for s in range(4) for o in range(2)]
        out = [((z + s) % 4) * 2 + (x ^ o) for s in range(4) for o in range(2)]
    else:
        into = out = [jnp.int32(place) for place in range(8)]
    ranks = [t, t ^ 1, t ^ 2, t ^ 3]
    positions = [p for r in ranks for p in (2 * r, blocks - 1 - 2 * r)]
    table = jnp.stack([v.astype(jnp.int32) for v in slots + into + out + positions])
    own_routes = jnp.concatenate(
        [lax.dynamic_slice_in_dim(routes, p * HALF, HALF, 0) for p in positions[0:2]], axis=0
    )
    vectors_in = (ln1_gain, ln1_bias, ln2_gain, ln2_bias, b_down)

    experts, hidden, routed = w_query.shape[0], w_up.shape[1], w_router.shape[1]
    turns, swap = axis_moves(dp)

    def over_x(x):
        return lax.ppermute(x, "dp", swap)

    def over_z(x, step):
        return lax.ppermute(x, "dp", turns[step - 1])

    def over_zx(x, step):
        return lax.ppermute(x, "dp", [(source, target ^ 1) for source, target in turns[step - 1]])

    if tuned:
        first, second, cross = pack(
            w_query, w_out, w_up, w_down.T, w_key, w_value, w_router, tokens, cotangent, vectors_in, b_up
        )
        first, second = first[None], second[None]
        z1, z2, z3 = [over_z(first, step) for step in (1, 2, 3)]
        cross = crossed(cross)
        side_a = jnp.concatenate([after(first, table, own_routes), z1], axis=0)
        side_b = jnp.concatenate([z2, z3], axis=0)
        next_a, next_b = over_y(side_a), over_x(side_b)
        later_z1, later_z3 = [over_z(after(second, z1), step) for step in (1, 3)]
        later_z2 = over_z(later_z1, 1)
        side_a = jnp.concatenate([side_a, after(next_a, later_z1, later_z3, cross)], axis=0)
        side_b = jnp.concatenate([side_b, after(next_b, later_z1, later_z3, cross)], axis=0)
        far_a, far_b = over_x(side_a), over_y(side_b)
        later_a = jnp.concatenate([second, later_z1], axis=0)
        later_b = jnp.concatenate([later_z2, later_z3], axis=0)
        far_a, far_b, later_a, later_b = together(far_a, far_b, later_a, later_b)
        next_a, next_b = over_y(later_a), over_x(later_b)
        first_pieces = [side_a, far_a, side_b, far_b]
        first_pieces = first_pieces + [over_core(v) for v in first_pieces]
    else:
        first_pieces, second_pieces = general_pieces(
            w_query, w_out, w_up, w_down, w_key, w_value, w_router, vectors_in, b_up
        )
        cross = crossed(jnp.concatenate([tokens[HALF:], cotangent[HALF:]], axis=0))
    normed, pair, gates, small, vectors, up_bias = first_stage(
        table, tokens, cross, own_routes, first_pieces
    )
    pair_y = over_y(pair)
    pairs = (pair, over_core(pair), pair_y, over_core(pair_y))
    if tuned:
        normed, later_a, later_b = together(normed, later_a, later_b)
    query, query_weight = query_stage(table, normed, own_routes, first_pieces)
    if tuned:
        side_a = jnp.concatenate([later_a, after(next_a, query)], axis=0)
        side_b = jnp.concatenate([later_b, after(next_b, query, pair_y)], axis=0)
        far_a, far_b = over_x(side_a), over_y(side_b)
    heads, totals = attend_stage(table, query, pairs, seq)
    mixed, cot_t = prepare_stage(table, heads, gates, own_routes, cotangent, cross, query_weight.shape[2])
    if tuned:
        mixed, far_a, far_b, core_a, core_b = together(mixed, far_a, far_b, over_core(side_a), over_core(side_b))
        second_pieces = [side_a, far_a, side_b, far_b, core_a, over_core(far_a), core_b, over_core(far_b)]
    output, output_high, grad_mid, back, sums, bias_grad, *later_blocks = middle_stage(
        table, tokens, cotangent, cross, mixed, cot_t, vectors, up_bias, second_pieces
    )
    if tuned:
        keep_a, keep_b, send_a, send_b = later_blocks
        got_a, got_b = over_core(send_a), over_core(send_b)
    grad_heads, grad_gate = select_stage(table, back, heads, gates, own_routes)
    if tuned:
        grad_heads, grad_gate, got_a, got_b = together(grad_heads, grad_gate, got_a, got_b)
        part_a, part_b = add_blocks(
            "add_near", [(keep_a, (1,)), (got_a, (1,))], [(keep_b, (1,)), (got_b, (1,))]
        )
        next_a, next_b = over_y(part_a), over_x(part_b)
        grad_heads = after(grad_heads, part_a, part_b)
    grad_query, pair_keep, pair_send = attend_back_stage(
        table, query, grad_heads, totals, gates, grad_gate, pairs, seq
    )
    pair_got = over_core(pair_send)
    (pair_next,) = add_blocks("add_pairs", [(pair_keep, (1,)), (pair_got, (1,))])
    pair_parts = (pair_keep, pair_got, over_y(pair_next))
    if tuned:
        next_a, next_b = after(next_a, pair_next), after(next_b, pair_next)
        part_a, part_b = add_blocks(
            "add_far",
            [(keep_a, (0, 1)), (got_a, (0, 1)), (next_a, (1,))],
            [(keep_b, (0, 1)), (got_b, (0, 1)), (next_b, (1,))],
        )
        last_a = over_x(part_a)
        grad_query = after(grad_query, part_a, part_b)
    else:
        output_high = crossed(output_high)
    spread, query_grads = spread_stage(table, grad_query, normed, own_routes, query_weight.shape[2])
    if tuned:
        spread, pair_far = together(spread, pair_parts[2])
        pair_parts = (*pair_parts[0:2], pair_far)
        last_b = over_y(after(part_b, pair_far, spread))

        def final(name, *sides):
            return add_blocks(
                name,
                *[
                    [(keep, (0, 0, s)), (got, (0, 0, s)), (near, (0, s)), (last, (s,))]
                    for keep, got, near, last in sides
                    for s in (0, 1)
                ],
            )

    low_rows, high_rows, *first_blocks = last_stage(
        table, tokens, cross, grad_mid, spread, normed, own_routes, gates, grad_gate,
        query_weight, small, vectors, sums, bias_grad, pair_parts, query_grads,
    )
    if tuned:
        last_a = after(last_a, low_rows)
        ahead, beyond = final("add_last", (keep_a, got_a, next_a, last_a))
        beyond = over_z(beyond, 1)
        low_rows, high_rows, last_b, *first_blocks = together(low_rows, high_rows, last_b, *first_blocks)
        output_high = crossed(after(output_high, last_b))
        kept, back = final("add_last", (keep_b, got_b, next_b, last_b))
        keep_a, keep_b, send_a, send_b = first_blocks
        got_a, got_b, beyond, back = together(over_core(send_a), over_core(send_b), beyond, back)
        (ahead,) = add_blocks("add_ahead", [(ahead, ()), (beyond, ())])
        one, three = over_z(ahead, 1), over_z(back, 3)
        got_a, got_b = after(got_a, ahead), after(got_b, ahead)
        part_a, part_b = add_blocks(
            "add_near", [(keep_a, (1,)), (got_a, (1,))], [(keep_b, (1,)), (got_b, (1,))]
        )
        next_a, next_b = over_y(part_a), over_x(part_b)
        next_a, next_b, output_high = together(next_a, next_b, output_high)
        part_a, part_b = add_blocks(
            "add_far",
            [(keep_a, (0, 1)), (got_a, (0, 1)), (next_a, (1,))],
            [(keep_b, (0, 1)), (got_b, (0, 1)), (next_b, (1,))],
        )
        last_a, last_b = over_x(part_a), over_y(part_b)
        last_a, last_b, one, three = together(last_a, last_b, one, three)
        high_rows = after(high_rows, last_b)
        out_grad, up_grad, down_grad, result = unpack_second(
            kept, one, three, output, output_high, experts, hidden
        )
        down_grad = down_grad.T
        done = final("add_last", (keep_a, got_a, next_a, last_a), (keep_b, got_b, next_b, last_b))
        done = (done[2], done[0], done[1], done[3])
        one, two, three = [over_z(done[step], step) for step in (1, 2, 3)]
        one = after(one, out_grad)
        parts = (done[0], one, two, three)
        query_grad, key_grad, value_grad, router_grad, small_grads, up_bias_grad, grad_tokens = unpack_first(
            parts, low_rows, crossed(high_rows), experts, routed
        )
    else:
        (
            query_grad, key_grad, value_grad, router_grad, small_grads, up_bias_grad,
            out_grad, up_grad, down_grad,
        ) = general_grads(first_blocks, later_blocks, experts, hidden, routed)
        result = jnp.concatenate([output, output_high], axis=0)
        grad_tokens = jnp.concatenate([low_rows, crossed(high_rows).astype(F32)], axis=0)
    return (
        result,
        grad_tokens,
        small_grads[0],
        small_grads[1],
        key_grad,
        value_grad,
        router_grad,
        query_grad,
        out_grad,
        small_grads[2],
        small_grads[3],
        up_grad,
        up_bias_grad,
        down_grad,
        small_grads[4],
    )


def solution(mesh):
    rows = P(("dp", "tensor"), None)
    vector = P(("dp", "tensor"))
    in_specs = (
        rows,
        P("dp", None),
        rows,
        vector,
        vector,
        rows,
        rows,
        rows,
        P("tensor", "dp", None),
        P("tensor", None, "dp"),
        vector,
        vector,
        P("dp", "tensor"),
        vector,
        P("tensor", "dp"),
        vector,
    )
    out_specs = (
        rows,
        rows,
        vector,
        vector,
        rows,
        rows,
        rows,
        P("tensor", "dp", None),
        P("tensor", None, "dp"),
        vector,
        vector,
        P("dp", "tensor"),
        vector,
        P("tensor", "dp"),
        vector,
    )
    return jax.shard_map(
        per_device, mesh=mesh, in_specs=in_specs, out_specs=out_specs, check_vma=False
    )
```

```python
import jax
import jax.numpy as jnp
from jax import lax
from jax.experimental import pallas as pl
from jax.experimental.pallas import tpu as pltpu
from jax.sharding import PartitionSpec as P

F32 = jnp.float32
BF16 = jnp.bfloat16
HEAD = 64
LANES = 128
HALF = 256
ROWS = 64
TINY = 16
CHUNK = 32

PLACES_A = ((0, 0, 0), (0, 0, 1), (1, 0, 0), (1, 0, 1))
PLACES_XA = tuple((y, 1, s) for y, _, s in PLACES_A)
PLACES_B = ((0, 0, 2), (0, 0, 3), (0, 1, 2), (0, 1, 3))
PLACES_YB = tuple((1, x, s) for _, x, s in PLACES_B)
LAYOUT = tuple(
    tuple((2 * y + core, 2 * s + x) for y, x, s in places)
    for core in (0, 1)
    for places in (PLACES_A, PLACES_XA, PLACES_B, PLACES_YB)
)
SLOT_AT, IN_AT, OUT_AT, POS_AT = 0, 4, 12, 20


def nn(left, right):
    return lax.dot_general(left, right, (((1,), (0,)), ((), ())), preferred_element_type=F32)


def nt(left, right):
    return lax.dot_general(left, right, (((1,), (1,)), ((), ())), preferred_element_type=F32)


def norm_parts(rows):
    average = jnp.mean(rows, axis=-1, keepdims=True)
    centered = rows - average
    inverse = lax.rsqrt(jnp.mean(centered * centered, axis=-1, keepdims=True) + 1e-05)
    return centered * inverse, inverse


def norm_backward(incoming, scaled, inverse, gain):
    weighted = incoming * gain
    return inverse * (
        weighted
        - jnp.mean(weighted, axis=-1, keepdims=True)
        - scaled * jnp.mean(weighted * scaled, axis=-1, keepdims=True)
    )


def smem_spec():
    return pl.BlockSpec(memory_space=pltpu.SMEM)


def params(mebibytes):
    return pltpu.CompilerParams(vmem_limit_bytes=mebibytes * 1024 * 1024)


def cost(microseconds):
    return pl.CostEstimate(flops=0, bytes_accessed=int(microseconds * 3.69e6), transcendentals=0)


def after(value, *earlier):
    return lax.optimization_barrier((value, *earlier))[0]


def together(*values):
    return lax.optimization_barrier(values)


def shaped(shape, kind):
    return jax.ShapeDtypeStruct(shape, kind)


def pack_kernel(
    wq, wo, wup, wdown, wk, wv, wr, tok, cot, g1, b1, g2, b2, bdown, bup, first_ref, second_ref, cross_ref, wide, square
):
    cross_ref[0:HALF, :] = tok[HALF:, :]
    cross_ref[HALF:, :] = cot[HALF:, :]
    experts = wq.shape[0]
    group = experts * HEAD
    hidden = wup.shape[1]
    first_ref[...] = jnp.zeros_like(first_ref)
    for j in range(experts):
        first_ref[0:ROWS, j * HEAD : (j + 1) * HEAD] = wq[j]
    square[...] = jnp.zeros_like(square)
    for i, vector in enumerate((g1, b1, g2, b2, bdown)):
        square[24 + i : 25 + i, 0:TINY] = vector[...].astype(F32)
    columns = square[...].T
    first_ref[ROWS : ROWS + TINY, 0:HEAD] = wk[...]
    first_ref[ROWS : ROWS + TINY, HEAD : 2 * HEAD] = wv[...]
    first_ref[ROWS : ROWS + TINY, LANES : 2 * LANES] = columns[0:TINY, :].astype(BF16)
    first_ref[ROWS : ROWS + TINY, LANES : LANES + wr.shape[1]] = wr[...]
    first_ref[ROWS : ROWS + 1, 2 * LANES : 2 * LANES + HEAD] = bup[...]
    wide[...] = jnp.zeros_like(wide)
    for j in range(experts):
        wide[j * HEAD : (j + 1) * HEAD, 0:ROWS] = wo[j].astype(F32)
    second_ref[:, 0:group] = wide[...].T[0:ROWS].astype(BF16)
    second_ref[:, group : group + hidden] = wup[...]
    second_ref[:, group + hidden :] = wdown[...]


def pack(wq, wo, wup, wdown, wk, wv, wr, tok, cot, vectors, bup):
    group, hidden = wq.shape[0] * HEAD, wup.shape[1]
    return pl.pallas_call(
        pack_kernel,
        cost_estimate=cost(0.2),
        out_shape=(
            shaped((ROWS + TINY, group), BF16),
            shaped((ROWS, group + 2 * hidden), BF16),
            shaped(tok.shape, BF16),
        ),
        scratch_shapes=[
            pltpu.VMEM((group, LANES), F32),
            pltpu.VMEM((LANES, LANES), F32),
        ],
        compiler_params=params(60),
    )(wq, wo, wup, wdown, wk, wv, wr, tok, cot, *[v.reshape(1, -1) for v in vectors], bup.reshape(1, -1))


def sum_four(kept, one, two, three):
    return kept.astype(F32) + one.astype(F32) + two.astype(F32) + three.astype(F32)


def unpack_first_kernel(kept, one, two, three, low, high, gq, gk, gv, gr, *refs):
    vectors, (gb, tokens, total) = refs[:5], refs[5:]
    tokens[0:HALF, :] = low[...]
    tokens[HALF:, :] = high[...].astype(F32)
    total[...] = sum_four(kept[...], one[...], two[...], three[...])
    for j in range(gq.shape[0]):
        gq[j] = total[0:ROWS, j * HEAD : (j + 1) * HEAD]
    small = total[ROWS:, :]
    gk[...] = small[:, 0:HEAD]
    gv[...] = small[:, HEAD : 2 * HEAD]
    gr[...] = small[:, LANES : LANES + gr.shape[1]]
    square = jnp.concatenate(
        [small[:, LANES : 2 * LANES], jnp.zeros((LANES - TINY, LANES), F32)], axis=0
    ).T
    for i, out in enumerate(vectors):
        out[...] = square[24 + i : 25 + i, 0:TINY]
    gb[...] = small[0:1, 2 * LANES : 2 * LANES + HEAD]


def unpack_first(parts, low, high, experts, routed):
    outs = pl.pallas_call(
        unpack_first_kernel,
        cost_estimate=cost(2),
        out_shape=(
            shaped((experts, ROWS, HEAD), F32),
            shaped((TINY, HEAD), F32),
            shaped((TINY, HEAD), F32),
            shaped((TINY, routed), F32),
            *[shaped((1, TINY), F32) for _ in range(5)],
            shaped((1, HEAD), F32),
            shaped((low.shape[0] + high.shape[0], low.shape[1]), F32),
        ),
        scratch_shapes=[pltpu.VMEM(parts[0].shape, F32)],
        compiler_params=params(8),
    )(*parts, low, high)
    return *outs[0:4], [v.reshape(-1) for v in outs[4:9]], outs[9].reshape(-1), outs[10]


def unpack_second_kernel(kept, one, three, low, high, go, gup, gdown, rows, total, wide):
    rows[0:HALF, :] = low[...]
    rows[HALF:, :] = high[...]
    experts = go.shape[0]
    group, hidden = experts * HEAD, gup.shape[1]
    total[...] = kept[...].astype(F32) + one[...].astype(F32) + three[...].astype(F32)
    gup[...] = total[:, group : group + hidden]
    wide[...] = jnp.zeros_like(wide)
    wide[0:ROWS, :] = total[:, 0:group]
    turned = wide[...].T
    for j in range(experts):
        go[j] = turned[j * HEAD : (j + 1) * HEAD, 0:ROWS]
    gdown[...] = total[:, group + hidden :]


def unpack_second(kept, one, three, low, high, experts, hidden):
    group = experts * HEAD
    return pl.pallas_call(
        unpack_second_kernel,
        cost_estimate=cost(2),
        out_shape=(
            shaped((experts, HEAD, ROWS), F32),
            shaped((ROWS, hidden), F32),
            shaped((ROWS, hidden), F32),
            shaped((low.shape[0] + high.shape[0], low.shape[1]), BF16),
        ),
        scratch_shapes=[
            pltpu.VMEM(kept.shape, F32),
            pltpu.VMEM((LANES, group), F32),
        ],
        compiler_params=params(8),
    )(kept, one, three, low, high)


def axis_moves(dp):
    turns = [
        [(d, (d + 2 * step) % dp) for d in range(dp)] for step in range(1, dp // 2)
    ]
    return turns, [(d, d ^ 1) for d in range(dp)]


CORE = [(0, 1), (1, 0), (2, 3), (3, 2)]
ACROSS = [(0, 2), (2, 0), (1, 3), (3, 1)]
CROSSED = [(0, 3), (3, 0), (1, 2), (2, 1)]


def over_core(x):
    return lax.ppermute(x, "tensor", CORE)


def over_y(x):
    return lax.ppermute(x, "tensor", ACROSS)


def crossed(x):
    return lax.ppermute(x, "tensor", CROSSED)


def add_blocks(name, *sums):
    terms = [term for parts in sums for term in parts]
    shapes = [parts[0][0].shape[len(parts[0][1]) :] for parts in sums]
    count = len(terms)

    def kernel(*refs):
        ins, outs = refs[:count], refs[count:]
        at = 0
        for out, parts in zip(outs, sums):
            total = None
            for ref, (_, index) in zip(ins[at : at + len(parts)], parts):
                value = ref[index].astype(F32) if index else ref[...].astype(F32)
                total = value if total is None else total + value
            out[...] = total.astype(BF16)
            at += len(parts)

    kernel.__name__ = name
    size = 0
    for shape, parts in zip(shapes, sums):
        block = 2 * (len(parts) + 1)
        for n in shape:
            block *= n
        size += block
    return pl.pallas_call(
        kernel,
        cost_estimate=pl.CostEstimate(flops=0, bytes_accessed=size, transcendentals=0),
        out_shape=tuple(shaped(shape, BF16) for shape in shapes),
        compiler_params=params(16),
    )(*[array for array, _ in terms])


def place_blocks(table, pieces, row_from, rows, put):
    for piece, places in zip(pieces, LAYOUT):
        for i, (slot, place) in enumerate(places):
            put(slot, table[IN_AT + place], piece[i, row_from : row_from + rows, :])


def rows_at(index, rows):
    return pl.ds(pl.multiple_of(index * rows, rows), rows)


def place_weights(table, pieces, weight):
    def put(slot, block, value):
        weight[slot, rows_at(block, ROWS), :] = value

    place_blocks(table, pieces, 0, ROWS, put)


def first_kernel(table, low_tok, cross, routes, *refs):
    pieces, (normed_ref, kv_ref, gates_ref, small, vectors, up_bias) = refs[:8], refs[8:]

    def put(slot, block, value):
        small[rows_at(block * 4 + table[SLOT_AT + slot], TINY), :] = value

    place_blocks(table, pieces, ROWS, TINY, put)
    tokens = jnp.concatenate([low_tok[0:HALF, :], cross[0:HALF, :]], axis=0).astype(F32)
    scaled, _ = norm_parts(tokens)
    turned = small[:, LANES : 2 * LANES].astype(F32).T
    vectors[...] = turned[24:32, :]
    for i in range(32):
        up_bias[i // 8 : i // 8 + 1, (i % 8) * HEAD : (i % 8 + 1) * HEAD] = small[
            TINY * i : TINY * i + 1, 2 * LANES : 2 * LANES + HEAD
        ].astype(F32)
    normed = (scaled * vectors[0:1, :] + vectors[1:2, :]).astype(BF16)
    normed_ref[...] = normed
    kv_ref[...] = nn(normed, small[:, 0:LANES]).astype(BF16)
    logits = nn(normed, small[:, LANES : 2 * LANES])
    lane = lax.broadcasted_iota(jnp.int32, logits.shape, 1)
    ways = routes.shape[1]
    chosen = [lane == routes[:, k : k + 1] for k in range(ways)]
    member = chosen[0]
    for k in range(1, ways):
        member = member | chosen[k]
    logits = jnp.where(member, logits, -jnp.inf)
    exponent = jnp.exp(logits - jnp.max(logits, axis=-1, keepdims=True))
    shares = exponent / jnp.sum(exponent, axis=-1, keepdims=True)
    gates = jnp.zeros_like(shares)
    for k in range(ways):
        gate = jnp.sum(jnp.where(chosen[k], shares, 0.0), axis=-1, keepdims=True)
        gates = jnp.where(lane == k, gate, gates)
    gates_ref[...] = gates


def first_stage(table, tokens, cross, routes, pieces):
    rows, width = tokens.shape
    return pl.pallas_call(
        first_kernel,
        cost_estimate=cost(0.5),
        in_specs=[smem_spec()] + [pl.BlockSpec(memory_space=pltpu.VMEM)] * 11,
        out_shape=(
            shaped((rows, width), BF16),
            shaped((rows, LANES), BF16),
            shaped((rows, LANES), F32),
            shaped((width, pieces[0].shape[2]), BF16),
            shaped((8, width), F32),
            shaped((8, width), F32),
        ),
        compiler_params=params(14),
    )(table, tokens, cross, routes, *pieces)


def wanted_pairs(routes, at, ways):
    half = (lax.broadcasted_iota(jnp.int32, (CHUNK, LANES), 1) >= HEAD).astype(jnp.int32)
    return [
        (jnp.broadcast_to(routes[at, k : k + 1], half.shape) - half).astype(jnp.int16)
        for k in range(ways)
    ]


def pairs_of(table, experts):
    for slot in range(4):
        for pair in range(experts // 2):
            base = experts * table[SLOT_AT + slot] + 2 * pair
            yield slot, pair, jnp.full((CHUNK, LANES), base, jnp.int32).astype(jnp.int16)


def select_pairs(table, routes, at, ways, source):
    wanted = wanted_pairs(routes, at, ways)
    picked = [jnp.zeros((CHUNK, LANES), BF16)] * ways
    for slot, pair, base in pairs_of(table, source.shape[2] // HEAD):
        value = source[slot, at, pair * LANES : (pair + 1) * LANES]
        for k in range(ways):
            picked[k] = jnp.where(wanted[k] == base, value, picked[k])
    return picked


def spread_pairs(table, routes, at, held, target):
    wanted = wanted_pairs(routes, at, len(held))
    for slot, pair, base in pairs_of(table, target.shape[2] // HEAD):
        value = jnp.zeros((CHUNK, LANES), BF16)
        for k, row in enumerate(held):
            value = jnp.where(wanted[k] == base, row, value)
        target[slot, at, pair * LANES : (pair + 1) * LANES] = value


def over_chunks(rows, step):
    def body(c, _):
        step(pl.ds(pl.multiple_of(c * CHUNK, CHUNK), CHUNK))
        return 0

    lax.fori_loop(0, rows // CHUNK, body, 0)


def query_kernel(table, normed, routes, *refs):
    pieces, (chosen, weight, queries) = refs[:8], refs[8:]
    place_weights(table, pieces, weight)
    for slot in range(4):
        queries[slot] = nn(normed[...], weight[slot]).astype(BF16)
    ways = routes.shape[1]

    def step(at):
        for k, value in enumerate(select_pairs(table, routes, at, ways, queries)):
            chosen[k, at, :] = value

    over_chunks(normed.shape[0], step)


def query_stage(table, normed, routes, pieces):
    rows, width = normed.shape
    group = pieces[0].shape[2]
    return pl.pallas_call(
        query_kernel,
        cost_estimate=cost(0.8),
        in_specs=[smem_spec()] + [pl.BlockSpec(memory_space=pltpu.VMEM)] * 10,
        out_shape=(
            shaped((routes.shape[1], rows, LANES), BF16),
            shaped((4, width, group), BF16),
        ),
        scratch_shapes=[pltpu.VMEM((4, rows, group), BF16)],
        compiler_params=params(16),
    )(table, normed, routes, *pieces)


def place_pair(table, pieces, key_scr, value_scr, ones):
    lower = lax.broadcasted_iota(jnp.int32, (HALF, LANES), 1) < HEAD
    for p, piece in enumerate(pieces):
        for h in range(2):
            both = piece[h * HALF : (h + 1) * HALF, :].astype(F32)
            turned = pltpu.roll(both, HEAD, 1)
            at = pl.ds(pl.multiple_of(table[POS_AT + 2 * p + h] * HALF, HALF), HALF)
            key_scr[at, :] = (jnp.where(lower, both, turned) * 0.125).astype(BF16)
            value_scr[at, 0:LANES] = jnp.where(lower, turned, both).astype(BF16)
            if ones:
                value_scr[at, LANES : 2 * LANES] = jnp.ones((HALF, LANES), BF16)


def causal_mask():
    shape = (HALF, HALF)
    return lax.broadcasted_iota(jnp.int32, shape, 1) <= lax.broadcasted_iota(jnp.int32, shape, 0)


def attend_kernel(table, query, kv0, kv1, kv2, kv3, out_ref, total_ref, keys, values, scores, tops, sums):
    block = pl.program_id(0)
    ways = query.shape[0]

    @pl.when(block == 0)
    def _():
        place_pair(table, (kv0, kv1, kv2, kv3), keys, values, True)

    last = table[POS_AT + block]
    tops[...] = jnp.full_like(tops, -jnp.inf)

    def score(at, masked):
        rows = pl.ds(pl.multiple_of(at * HALF, HALF), HALF)
        keys_here = keys[rows, :]
        for k in range(ways):
            here = nt(query[k], keys_here)
            if masked:
                here = jnp.where(causal_mask(), here, -1e30)
            scores[at, k] = here
            tops[k] = jnp.maximum(tops[k], jnp.maximum(here[:, 0:LANES], here[:, LANES:]))

    lax.fori_loop(0, last, lambda at, _: (score(at, False), 0)[1], 0)
    score(last, True)
    for k in range(ways):
        tops[k] = jnp.broadcast_to(jnp.max(tops[k], axis=-1, keepdims=True), (HALF, LANES))
    sums[...] = jnp.zeros_like(sums)

    def weigh(at, _):
        rows = pl.ds(pl.multiple_of(at * HALF, HALF), HALF)
        values_here = values[rows, :]
        for k in range(ways):
            top = tops[k]
            here = scores[at, k]
            weights = jnp.concatenate(
                [jnp.exp(here[:, 0:LANES] - top), jnp.exp(here[:, LANES:] - top)], axis=1
            ).astype(BF16)
            sums[k] += nn(weights, values_here)
        return 0

    lax.fori_loop(0, last + 1, weigh, 0)
    lane = lax.broadcasted_iota(jnp.int32, (HALF, LANES), 1)
    total = jnp.zeros((HALF, LANES), F32)
    for k in range(ways):
        whole = sums[k]
        out_ref[k] = (whole[:, 0:LANES] / whole[:, LANES:]).astype(BF16)
        total = jnp.where(lane == k, tops[k] + jnp.log(whole[:, LANES:]), total)
    total_ref[...] = total


def attend_stage(table, query, pairs, seq):
    ways, rows, _ = query.shape
    kv_spec = pl.BlockSpec((rows, LANES), lambda b: (0, 0))
    spec = pl.BlockSpec((ways, HALF, LANES), lambda b: (0, b, 0))
    return pl.pallas_call(
        attend_kernel,
        cost_estimate=cost(1.2),
        grid=(rows // HALF,),
        in_specs=[smem_spec(), spec] + [kv_spec] * 4,
        out_specs=(spec, pl.BlockSpec((HALF, LANES), lambda b: (b, 0))),
        out_shape=(shaped((ways, rows, LANES), BF16), shaped((rows, LANES), F32)),
        scratch_shapes=[
            pltpu.VMEM((seq, LANES), BF16),
            pltpu.VMEM((seq, 2 * LANES), BF16),
            pltpu.VMEM((seq // HALF, ways, HALF, HALF), F32),
            pltpu.VMEM((ways, HALF, LANES), F32),
            pltpu.VMEM((ways, HALF, 2 * LANES), F32),
        ],
        compiler_params=params(28),
    )(table, query, *pairs)


def attend_back_kernel(
    table, query, grad, all_totals, gates, gate_grads, kv0, kv1, kv2, kv3, grad_query, *refs
):
    pair_outs, (keys, values, key_sum, value_sum, query_sum, query_t, grad_t, probs, scored, totals, inner) = refs[:2], refs[2:]
    block = pl.program_id(0)
    ways = query.shape[0]

    @pl.when(block == 0)
    def _():
        place_pair(table, (kv0, kv1, kv2, kv3), keys, values, False)
        key_sum[...] = jnp.zeros_like(key_sum)
        value_sum[...] = jnp.zeros_like(value_sum)

    last = table[POS_AT + block]
    query_sum[...] = jnp.zeros_like(query_sum)
    for k in range(ways):
        query_t[:, k * HALF : (k + 1) * HALF] = query[k].T
        grad_t[:, k * HALF : (k + 1) * HALF] = grad[k].T
        totals[k] = jnp.broadcast_to(all_totals[:, k : k + 1], (HALF, LANES))
        inner[k] = jnp.broadcast_to(gates[:, k : k + 1] * gate_grads[:, k : k + 1], (HALF, LANES))

    def step(at, masked):
        rows = pl.ds(pl.multiple_of(at * HALF, HALF), HALF)
        keys_here = keys[rows, :]
        values_here = values[rows, :]
        for k in range(ways):
            score = nt(query[k], keys_here)
            total, mean = totals[k], inner[k]
            prob = jnp.concatenate(
                [jnp.exp(score[:, 0:LANES] - total), jnp.exp(score[:, LANES:] - total)], axis=1
            )
            if masked:
                prob = jnp.where(causal_mask(), prob, 0.0)
            grad_prob = nt(grad[k], values_here)
            grad_score = prob * (grad_prob - jnp.concatenate([mean, mean], axis=1))
            probs[k * HALF : (k + 1) * HALF, :] = prob.astype(BF16)
            scored[k * HALF : (k + 1) * HALF, :] = grad_score.astype(BF16)
        query_sum[...] += nn(scored[...], keys_here)
        key_sum[at] += nn(query_t[...], scored[...])
        value_sum[at] += nn(grad_t[...], probs[...])

    lax.fori_loop(0, last, lambda at, _: (step(at, False), 0)[1], 0)
    step(last, True)
    for k in range(ways):
        grad_query[k] = query_sum[k * HALF : (k + 1) * HALF, :].astype(BF16)

    @pl.when(block == pl.num_programs(0) - 1)
    def _():
        for p in range(4):
            out = pair_outs[p % 2]
            for h in range(2):
                at = table[POS_AT + 2 * p + h]
                key_part, value_part = key_sum[at], value_sum[at]
                out[p // 2, h, 0:HEAD, :] = ((key_part[0:HEAD] + key_part[HEAD:]) * 0.125).astype(BF16)
                out[p // 2, h, HEAD:, :] = (value_part[0:HEAD] + value_part[HEAD:]).astype(BF16)


def attend_back_stage(table, query, grad, totals, gates, gate_grads, pairs, seq):
    ways, rows, _ = query.shape
    kv_spec = pl.BlockSpec((rows, LANES), lambda b: (0, 0))
    spec = pl.BlockSpec((ways, HALF, LANES), lambda b: (0, b, 0))
    pair_spec = pl.BlockSpec((2, 2, LANES, HALF), lambda b: (0, 0, 0, 0))
    return pl.pallas_call(
        attend_back_kernel,
        cost_estimate=cost(16),
        grid=(rows // HALF,),
        in_specs=[smem_spec()] + [spec] * 2 + [pl.BlockSpec((HALF, LANES), lambda b: (b, 0))] * 3 + [kv_spec] * 4,
        out_specs=(spec,) + (pair_spec,) * 2,
        out_shape=(shaped((ways, rows, LANES), BF16),) + (shaped((2, 2, LANES, HALF), BF16),) * 2,
        scratch_shapes=[
            pltpu.VMEM((seq, LANES), BF16),
            pltpu.VMEM((seq, LANES), BF16),
            pltpu.VMEM((seq // HALF, LANES, HALF), F32),
            pltpu.VMEM((seq // HALF, LANES, HALF), F32),
            pltpu.VMEM((ways * HALF, LANES), F32),
            pltpu.VMEM((LANES, ways * HALF), BF16),
            pltpu.VMEM((LANES, ways * HALF), BF16),
            pltpu.VMEM((ways * HALF, HALF), BF16),
            pltpu.VMEM((ways * HALF, HALF), BF16),
            pltpu.VMEM((ways, HALF, LANES), F32),
            pltpu.VMEM((ways, HALF, LANES), F32),
        ],
        compiler_params=params(20),
    )(table, query, grad, totals, gates, gate_grads, *pairs)


def in_order(table, turned, target):
    for place in range(8):
        target[place * ROWS : (place + 1) * ROWS, :] = turned[rows_at(table[OUT_AT + place], ROWS), :]


def put_blocks(grads, outs, slot, column_to):
    keep_a, keep_b, send_a, send_b = outs
    y, core = slot // 2, slot % 2
    wide = grads.shape[1]
    for s in range(4):
        for x in range(2):
            block = grads[(2 * s + x) * ROWS : (2 * s + x + 1) * ROWS, :].astype(BF16)
            if s in (1, 2):
                out, place = (send_a if core else keep_a), (y, x, s - 1)
            else:
                out, place = (send_b if core else keep_b), (x, y, s // 2)
            out[place[0], place[1], place[2], 0:ROWS, column_to : column_to + wide] = block


def prepare_kernel(table, heads, gates, routes, low_cot, cross, mixed, cot_t, turned):
    ways, rows, _ = heads.shape

    def expand(at):
        held = [
            (heads[k, at, :].astype(F32) * gates[at, k : k + 1]).astype(BF16) for k in range(ways)
        ]
        spread_pairs(table, routes, at, held, mixed)

    over_chunks(rows, expand)
    turned[...] = jnp.concatenate([low_cot[0:HALF, :], cross[HALF:, :]], axis=0).T
    in_order(table, turned, cot_t)


def prepare_stage(table, heads, gates, routes, cot, cross, group):
    rows, width = cot.shape
    return pl.pallas_call(
        prepare_kernel,
        cost_estimate=cost(0.3),
        in_specs=[smem_spec()] + [pl.BlockSpec(memory_space=pltpu.VMEM)] * 5,
        out_shape=(shaped((4, rows, group), BF16), shaped((width, rows), BF16)),
        scratch_shapes=[pltpu.VMEM((width, rows), BF16)],
        compiler_params=params(12),
    )(table, heads, gates, routes, cot, cross)


def middle_kernel(table, low_tok, low_cot, cross, mixed, cot_t, vectors, up_bias, *refs):
    pieces = refs[:8]
    low_out, high_out, grad_mid, back, sums, bias_grad = refs[8:14]
    blocks = refs[14:18]
    weight, turned, ordered, hid_scr, pre_scr = refs[18:]
    rows, width = low_tok.shape
    group = mixed.shape[2]
    hidden = hid_scr.shape[2]
    place_weights(table, pieces, weight)
    middle = jnp.concatenate([low_tok[0:HALF, :], cross[0:HALF, :]], axis=0).astype(F32)
    for slot in range(4):
        middle = middle + nt(mixed[slot], weight[slot, :, 0:group])
    scaled, inverse = norm_parts(middle)
    gain = vectors[2:3, :]
    normed = (scaled * gain + vectors[3:4, :]).astype(BF16)
    turned[0] = normed.T
    in_order(table, turned.at[0], ordered.at[0])
    cot = jnp.concatenate([low_cot[0:HALF, :], cross[HALF:, :]], axis=0)
    result = middle + vectors[4:5, :]
    grad_normed = jnp.zeros((rows, width), F32)
    up_at, down_at = group, group + hidden
    for slot in range(4):
        bias = up_bias[pl.ds(table[SLOT_AT + slot], 1), :]
        preact = nn(normed, weight[slot, :, up_at:down_at]) + bias
        share = jax.nn.sigmoid(preact)
        active = (preact * share).astype(BF16)
        hid_scr[slot] = active
        slope = share * (1.0 + preact * (1.0 - share))
        grad_pre = (nn(cot, weight[slot, :, down_at:]) * slope).astype(BF16)
        pre_scr[slot] = grad_pre
        bias_grad[pl.ds(table[SLOT_AT + slot], 1), :] = jnp.sum(
            grad_pre.astype(F32), axis=0, keepdims=True
        )
        result = result + nt(hid_scr[slot], weight[slot, :, down_at:])
        grad_normed = grad_normed + nt(pre_scr[slot], weight[slot, :, up_at:down_at])
        put_blocks(nn(ordered[0], pre_scr[slot]), blocks, slot, up_at)
        put_blocks(nn(cot_t[...], hid_scr[slot]), blocks, slot, down_at)
    low_out[...] = result[0:HALF].astype(BF16)
    high_out[...] = result[HALF:].astype(BF16)
    cot_wide = cot.astype(F32)
    sums[...] = jnp.zeros_like(sums)
    sums[2:3, :] = jnp.sum(grad_normed * scaled, axis=0, keepdims=True)
    sums[3:4, :] = jnp.sum(grad_normed, axis=0, keepdims=True)
    sums[4:5, :] = jnp.sum(cot_wide, axis=0, keepdims=True)
    grad_middle = cot_wide + norm_backward(grad_normed, scaled, inverse, gain)
    grad_mid[...] = grad_middle
    grad_attn = grad_middle.astype(BF16)
    turned[1] = grad_attn.T
    in_order(table, turned.at[1], ordered.at[1])
    for slot in range(4):
        put_blocks(nn(ordered[1], mixed[slot]), blocks, slot, 0)
        back[slot] = nn(grad_attn, weight[slot, :, 0:group]).astype(BF16)


def select_kernel(table, back, heads, gates, routes, grad_ref, grad_gate):
    ways, rows, _ = heads.shape
    lane = lax.broadcasted_iota(jnp.int32, (CHUNK, LANES), 1)
    ones = jnp.ones((LANES, LANES), BF16)

    def step(at):
        gate_grads = jnp.zeros((CHUNK, LANES), F32)
        for k, value in enumerate(select_pairs(table, routes, at, ways, back)):
            gate_grads = jnp.where(lane == k, nn(value * heads[k, at, :], ones), gate_grads)
            grad_ref[k, at, :] = (value.astype(F32) * gates[at, k : k + 1]).astype(BF16)
        grad_gate[at, :] = gate_grads

    over_chunks(rows, step)


def select_stage(table, back, heads, gates, routes):
    ways, rows, _ = heads.shape
    vmem = pl.BlockSpec(memory_space=pltpu.VMEM)
    return pl.pallas_call(
        select_kernel,
        cost_estimate=cost(8),
        in_specs=[smem_spec()] + [vmem] * 4,
        out_shape=(
            shaped((ways, rows, LANES), BF16),
            shaped((rows, LANES), F32),
        ),
        compiler_params=params(16),
    )(table, back, heads, gates, routes)


def middle_stage(table, tokens, cot, cross, mixed, cot_t, vectors, up_bias, pieces):
    rows, width = tokens.shape
    packed = pieces[0].shape[2]
    hidden = up_bias.shape[1]
    group = packed - 2 * hidden
    block = shaped((2, 2, 2, ROWS, packed), BF16)
    vmem = pl.BlockSpec(memory_space=pltpu.VMEM)
    return pl.pallas_call(
        middle_kernel,
        cost_estimate=cost(36),
        in_specs=[smem_spec()] + [vmem] * 15,
        out_shape=(
            shaped((HALF, width), BF16),
            shaped((rows - HALF, width), BF16),
            shaped((rows, width), F32),
            shaped((4, rows, group), BF16),
            shaped((8, width), F32),
            shaped((8, hidden), F32),
            block,
            block,
            block,
            block,
        ),
        scratch_shapes=[
            pltpu.VMEM((4, width, packed), BF16),
            pltpu.VMEM((2, width, rows), BF16),
            pltpu.VMEM((2, width, rows), BF16),
            pltpu.VMEM((4, rows, hidden), BF16),
            pltpu.VMEM((4, rows, hidden), BF16),
        ],
        compiler_params=params(28),
    )(table, tokens, cot, cross, mixed, cot_t, vectors, up_bias, *pieces)


def spread_kernel(table, grad_query, normed, routes, spread, grads, turned, normed_t):
    ways, rows, _ = grad_query.shape

    def expand(at):
        spread_pairs(table, routes, at, [grad_query[k, at, :] for k in range(ways)], spread)

    over_chunks(rows, expand)
    turned[...] = normed[...].T
    in_order(table, turned, normed_t)
    for slot in range(4):
        grads[slot] = nn(normed_t[...], spread[slot]).astype(BF16)


def last_kernel(
    table, low_tok, cross, grad_mid, grad_query, normed, routes, gates, grad_gate, weight, small,
    vectors, sums, bias_grad, pair_keep, pair_got, pair_far, low_out, high_out, *refs
):
    blocks, (pair_grad, tiny, wide, extra, spread, grads, turned, ordered) = refs[:4], refs[4:]
    spread_kernel(table, grad_query, normed, routes, spread, grads, turned, ordered)
    keep_a, keep_b, send_a, send_b = blocks
    rows = normed.shape[0]
    ways = routes.shape[1]
    for h in range(2):
        total = pair_keep[0, h].astype(F32) + pair_got[0, h].astype(F32) + pair_far[h].astype(F32)
        pair_grad[h * HALF : (h + 1) * HALF, :] = total.T.astype(BF16)
    gate = gates[...]
    gate_grad = grad_gate[...]
    chosen_grad = gate * (gate_grad - jnp.sum(gate * gate_grad, axis=-1, keepdims=True))
    lane = lax.broadcasted_iota(jnp.int32, (rows, LANES), 1)
    logit_grad = jnp.zeros((rows, LANES), F32)
    for k in range(ways):
        logit_grad = jnp.where(lane == routes[:, k : k + 1], chosen_grad[:, k : k + 1], logit_grad)
    logit_low = logit_grad.astype(BF16)
    normed_t = normed[...].T
    grad_normed = nt(pair_grad[...], small[:, 0:LANES]) + nt(logit_low, small[:, LANES : 2 * LANES])
    for slot in range(4):
        grad_normed = grad_normed + nt(spread[slot], weight[slot])
    tokens = jnp.concatenate([low_tok[0:HALF, :], cross[0:HALF, :]], axis=0).astype(F32)
    scaled, inverse = norm_parts(tokens)
    back = grad_mid[...] + norm_backward(grad_normed, scaled, inverse, vectors[0:1, :])
    low_out[...] = back[0:HALF]
    high_out[...] = back[HALF:].astype(BF16)
    wide[...] = jnp.zeros_like(wide)
    wide[24:32, :] = sums[...]
    wide[24:25, :] = jnp.sum(grad_normed * scaled, axis=0, keepdims=True)
    wide[25:26, :] = jnp.sum(grad_normed, axis=0, keepdims=True)
    tiny[:, 0:LANES] = nn(normed_t, pair_grad[...]).astype(BF16)
    tiny[:, LANES : 2 * LANES] = (nn(normed_t, logit_low) + wide[...].T).astype(BF16)
    extra[...] = jnp.zeros_like(extra)
    for i in range(32):
        extra[TINY * i : TINY * i + 1, 0:HEAD] = bias_grad[i // 8 : i // 8 + 1, (i % 8) * HEAD : (i % 8 + 1) * HEAD]
    tiny[:, 2 * LANES : 3 * LANES] = extra[...].astype(BF16)
    for slot in range(4):
        y, core = slot // 2, slot % 2
        put_blocks(grads[slot], blocks, slot, 0)
        for s in range(4):
            for x in range(2):
                row = table[OUT_AT + 2 * s + x] * 4 + table[SLOT_AT + slot]
                if s in (1, 2):
                    out, place = (send_a if core else keep_a), (y, x, s - 1)
                else:
                    out, place = (send_b if core else keep_b), (x, y, s // 2)
                out[place[0], place[1], place[2], ROWS:, :] = tiny[rows_at(row, TINY), :]


def last_stage(
    table, tokens, cross, grad_mid, grad_query, normed, routes, gates, grad_gate, weight, small,
    vectors, sums, bias_grad, pair_parts
):
    rows, width = tokens.shape
    block = shaped((2, 2, 2, ROWS + TINY, 3 * LANES), BF16)
    vmem = pl.BlockSpec(memory_space=pltpu.VMEM)
    return pl.pallas_call(
        last_kernel,
        cost_estimate=cost(7),
        in_specs=[smem_spec()] + [vmem] * 16,
        out_shape=(shaped((HALF, width), F32), shaped((rows - HALF, width), BF16), block, block, block, block),
        scratch_shapes=[
            pltpu.VMEM((rows, LANES), BF16),
            pltpu.VMEM((width, 3 * LANES), BF16),
            pltpu.VMEM((LANES, width), F32),
            pltpu.VMEM((width, LANES), F32),
            pltpu.VMEM((4, rows, weight.shape[2]), BF16),
            pltpu.VMEM((4, width, weight.shape[2]), BF16),
            pltpu.VMEM((width, rows), BF16),
            pltpu.VMEM((width, rows), BF16),
        ],
        compiler_params=params(24),
    )(
        table, tokens, cross, grad_mid, grad_query, normed, routes, gates, grad_gate, weight, small,
        vectors, sums, bias_grad, *pair_parts
    )


def gather_plain(x, axis, dim):
    return lax.all_gather(x, axis, axis=dim, tiled=True)


def general_pieces(wq, wo, wup, wdown, wk, wv, wr, vectors, bup):
    every = ("dp", "tensor")
    width = wup.shape[0] * lax.axis_size("dp")
    group = wq.shape[0] * HEAD

    def whole(rows):
        return lax.all_gather(gather_plain(rows, "dp", 0), "tensor", axis=0)

    queries = whole(wq.transpose(1, 0, 2).reshape(-1, group))
    second = whole(
        jnp.concatenate([wo.transpose(2, 0, 1).reshape(-1, group), wup, wdown.T], axis=1)
    )
    wide = [gather_plain(w, every, 0) for w in (wk, wv, wr)]
    columns = [gather_plain(v, every, 0)[:, None] for v in vectors]
    bias = jnp.pad(gather_plain(bup, every, 0).reshape(-1, 1, HEAD), ((0, 0), (0, TINY - 1), (0, 0)))
    left = jnp.concatenate(wide + columns, axis=1)
    small = jnp.concatenate(
        [jnp.pad(left, ((0, 0), (0, 2 * LANES - left.shape[1]))), bias.reshape(width, HEAD)], axis=1
    )
    small = jnp.pad(small, ((0, 0), (0, group - small.shape[1])))

    def block_one(slot, place):
        row = (4 * place + slot) * TINY
        return jnp.concatenate([queries[slot, place * ROWS : (place + 1) * ROWS], small[row : row + TINY]])

    first = [jnp.stack([block_one(*at) for at in places]) for places in LAYOUT]
    later = [
        jnp.stack([second[slot, place * ROWS : (place + 1) * ROWS] for slot, place in places])
        for places in LAYOUT
    ]
    return first, later


def general_sum(blocks):
    keep_a, keep_b, send_a, send_b = blocks
    slots = []
    for slot in range(4):
        y, core = slot // 2, slot % 2
        part_a, part_b = (send_a, send_b) if core else (keep_a, keep_b)
        slots.append(
            jnp.stack(
                [
                    (part_a[y, x, s - 1] if s in (1, 2) else part_b[x, y, s // 2])
                    for s in range(4)
                    for x in range(2)
                ]
            )
        )
    return lax.psum(jnp.stack(slots), ("dp", "tensor")).astype(F32)


def general_grads(first, later, experts, hidden, routed):
    group = experts * HEAD
    d, t = lax.axis_index("dp"), lax.axis_index("tensor")
    dp = lax.axis_size("dp")
    width = 8 * ROWS
    first, later = general_sum(first), general_sum(later)
    small = first[:, :, ROWS:].transpose(1, 0, 2, 3).reshape(width, group)
    mine = lax.dynamic_index_in_dim(first[:, :, :ROWS].reshape(4, width, group), t, 0, False)
    rest = lax.dynamic_index_in_dim(later.reshape(4, width, -1), t, 0, False)
    rows = width // dp

    def own(x, length, index):
        return lax.dynamic_slice_in_dim(x, index * length, length, 0)

    query = own(mine, rows, d).reshape(rows, experts, HEAD).transpose(1, 0, 2)
    rest = own(rest, rows, d)
    index = d * 4 + t
    tiny = own(small, rows // 4, index)
    bias = small.reshape(32, TINY, group)[:, 0, 2 * LANES : 2 * LANES + HEAD].reshape(-1)
    return (
        query,
        tiny[:, 0:HEAD],
        tiny[:, HEAD : 2 * HEAD],
        tiny[:, LANES : LANES + routed],
        [tiny[:, LANES + 24 + i] for i in range(5)],
        own(bias, bias.shape[0] // (4 * dp), index),
        rest[:, 0:group].reshape(rows, experts, HEAD).transpose(1, 2, 0),
        rest[:, group : group + hidden],
        rest[:, group + hidden :].T,
    )


def per_device(
    tokens,
    routes,
    cotangent,
    ln1_gain,
    ln1_bias,
    w_key,
    w_value,
    w_router,
    w_query,
    w_out,
    ln2_gain,
    ln2_bias,
    w_up,
    b_up,
    w_down,
    b_down,
):
    dp = lax.axis_size("dp")
    tuned = dp == 8
    d, t = lax.axis_index("dp"), lax.axis_index("tensor")
    seq = routes.shape[0]
    blocks = seq // HALF
    slots = [(t ^ s) if tuned else jnp.int32(s) for s in range(4)]
    z, x = d // 2, d % 2
    if tuned:
        into = [((z + 4 - s) % 4) * 2 + (x ^ o) for s in range(4) for o in range(2)]
        out = [((z + s) % 4) * 2 + (x ^ o) for s in range(4) for o in range(2)]
    else:
        into = out = [jnp.int32(place) for place in range(8)]
    ranks = [t, t ^ 1, t ^ 2, t ^ 3]
    positions = [p for r in ranks for p in (2 * r, blocks - 1 - 2 * r)]
    table = jnp.stack([v.astype(jnp.int32) for v in slots + into + out + positions])
    own_routes = jnp.concatenate(
        [lax.dynamic_slice_in_dim(routes, p * HALF, HALF, 0) for p in positions[0:2]], axis=0
    )
    vectors_in = (ln1_gain, ln1_bias, ln2_gain, ln2_bias, b_down)

    experts, hidden, routed = w_query.shape[0], w_up.shape[1], w_router.shape[1]
    turns, swap = axis_moves(dp)

    def over_x(x):
        return lax.ppermute(x, "dp", swap)

    def over_z(x, step):
        return lax.ppermute(x, "dp", turns[step - 1])

    def over_zx(x, step):
        return lax.ppermute(x, "dp", [(source, target ^ 1) for source, target in turns[step - 1]])

    if tuned:
        first, second, cross = pack(
            w_query, w_out, w_up, w_down.T, w_key, w_value, w_router, tokens, cotangent, vectors_in, b_up
        )
        first, second = first[None], second[None]
        z1, z2, z3 = [over_z(first, step) for step in (1, 2, 3)]
        cross = crossed(cross)
        side_a = jnp.concatenate([after(first, table, own_routes), z1], axis=0)
        side_b = jnp.concatenate([z2, z3], axis=0)
        next_a, next_b = over_y(side_a), over_x(side_b)
        later_z1, later_z3 = [over_z(after(second, z1), step) for step in (1, 3)]
        later_z2 = over_z(later_z1, 1)
        side_a = jnp.concatenate([side_a, after(next_a, later_z1, later_z3, cross)], axis=0)
        side_b = jnp.concatenate([side_b, after(next_b, later_z1, later_z3, cross)], axis=0)
        far_a, far_b = over_x(side_a), over_y(side_b)
        later_a = jnp.concatenate([second, later_z1], axis=0)
        later_b = jnp.concatenate([later_z2, later_z3], axis=0)
        far_a, far_b, later_a, later_b = together(far_a, far_b, later_a, later_b)
        next_a, next_b = over_y(later_a), over_x(later_b)
        first_pieces = [side_a, far_a, side_b, far_b]
        first_pieces = first_pieces + [over_core(v) for v in first_pieces]
    else:
        first_pieces, second_pieces = general_pieces(
            w_query, w_out, w_up, w_down, w_key, w_value, w_router, vectors_in, b_up
        )
        cross = crossed(jnp.concatenate([tokens[HALF:], cotangent[HALF:]], axis=0))
    normed, pair, gates, small, vectors, up_bias = first_stage(
        table, tokens, cross, own_routes, first_pieces
    )
    pair_y = over_y(pair)
    pairs = (pair, over_core(pair), pair_y, over_core(pair_y))
    if tuned:
        normed, later_a, later_b = together(normed, later_a, later_b)
    query, query_weight = query_stage(table, normed, own_routes, first_pieces)
    if tuned:
        side_a = jnp.concatenate([later_a, after(next_a, query)], axis=0)
        side_b = jnp.concatenate([later_b, after(next_b, query, pair_y)], axis=0)
        far_a, far_b = over_x(side_a), over_y(side_b)
    heads, totals = attend_stage(table, query, pairs, seq)
    mixed, cot_t = prepare_stage(table, heads, gates, own_routes, cotangent, cross, query_weight.shape[2])
    if tuned:
        mixed, far_a, far_b, core_a, core_b = together(mixed, far_a, far_b, over_core(side_a), over_core(side_b))
        second_pieces = [side_a, far_a, side_b, far_b, core_a, over_core(far_a), core_b, over_core(far_b)]
    output, output_high, grad_mid, back, sums, bias_grad, *later_blocks = middle_stage(
        table, tokens, cotangent, cross, mixed, cot_t, vectors, up_bias, second_pieces
    )
    if tuned:
        keep_a, keep_b, send_a, send_b = later_blocks
        got_a, got_b = over_core(send_a), over_core(send_b)
    grad_heads, grad_gate = select_stage(table, back, heads, gates, own_routes)
    if tuned:
        grad_heads, grad_gate, got_a, got_b = together(grad_heads, grad_gate, got_a, got_b)
        part_a, part_b = add_blocks(
            "add_near", [(keep_a, (1,)), (got_a, (1,))], [(keep_b, (1,)), (got_b, (1,))]
        )
        next_a, next_b = over_y(part_a), over_x(part_b)
        grad_heads = after(grad_heads, part_a, part_b)
    grad_query, pair_keep, pair_send = attend_back_stage(
        table, query, grad_heads, totals, gates, grad_gate, pairs, seq
    )
    pair_got = over_core(pair_send)
    (pair_next,) = add_blocks("add_pairs", [(pair_keep, (1,)), (pair_got, (1,))])
    pair_parts = (pair_keep, pair_got, over_y(pair_next))
    if tuned:
        next_a, next_b = after(next_a, pair_next), after(next_b, pair_next)
        part_a, part_b = add_blocks(
            "add_far",
            [(keep_a, (0, 1)), (got_a, (0, 1)), (next_a, (1,))],
            [(keep_b, (0, 1)), (got_b, (0, 1)), (next_b, (1,))],
        )
        last_a = over_x(part_a)
        grad_query = after(grad_query, part_a, part_b)
    else:
        output_high = crossed(output_high)
    if tuned:
        grad_query, pair_far = together(grad_query, pair_parts[2])
        pair_parts = (*pair_parts[0:2], pair_far)
        last_b = over_y(after(part_b, pair_far))

        def final(name, *sides):
            return add_blocks(
                name,
                *[
                    [(keep, (0, 0, s)), (got, (0, 0, s)), (near, (0, s)), (last, (s,))]
                    for keep, got, near, last in sides
                    for s in (0, 1)
                ],
            )

    low_rows, high_rows, *first_blocks = last_stage(
        table, tokens, cross, grad_mid, grad_query, normed, own_routes, gates, grad_gate,
        query_weight, small, vectors, sums, bias_grad, pair_parts,
    )
    if tuned:
        last_a = after(last_a, low_rows)
        ahead, beyond = final("add_last", (keep_a, got_a, next_a, last_a))
        beyond = over_z(beyond, 1)
        low_rows, high_rows, last_b, *first_blocks = together(low_rows, high_rows, last_b, *first_blocks)
        output_high = crossed(after(output_high, last_b))
        kept, back = final("add_last", (keep_b, got_b, next_b, last_b))
        keep_a, keep_b, send_a, send_b = first_blocks
        got_a, got_b, beyond, back = together(over_core(send_a), over_core(send_b), beyond, back)
        (ahead,) = add_blocks("add_ahead", [(ahead, ()), (beyond, ())])
        one, three = over_z(ahead, 1), over_z(back, 3)
        got_a, got_b = after(got_a, ahead), after(got_b, ahead)
        part_a, part_b = add_blocks(
            "add_near", [(keep_a, (1,)), (got_a, (1,))], [(keep_b, (1,)), (got_b, (1,))]
        )
        next_a, next_b = over_y(part_a), over_x(part_b)
        next_a, next_b, output_high = together(next_a, next_b, output_high)
        part_a, part_b = add_blocks(
            "add_far",
            [(keep_a, (0, 1)), (got_a, (0, 1)), (next_a, (1,))],
            [(keep_b, (0, 1)), (got_b, (0, 1)), (next_b, (1,))],
        )
        last_a, last_b = over_x(part_a), over_y(part_b)
        last_a, last_b, one, three = together(last_a, last_b, one, three)
        high_rows = after(high_rows, last_b)
        out_grad, up_grad, down_grad, result = unpack_second(
            kept, one, three, output, output_high, experts, hidden
        )
        down_grad = down_grad.T
        done = final("add_last", (keep_a, got_a, next_a, last_a), (keep_b, got_b, next_b, last_b))
        done = (done[2], done[0], done[1], done[3])
        one, two, three = [over_z(done[step], step) for step in (1, 2, 3)]
        one = after(one, out_grad)
        parts = (done[0], one, two, three)
        query_grad, key_grad, value_grad, router_grad, small_grads, up_bias_grad, grad_tokens = unpack_first(
            parts, low_rows, crossed(high_rows), experts, routed
        )
    else:
        (
            query_grad, key_grad, value_grad, router_grad, small_grads, up_bias_grad,
            out_grad, up_grad, down_grad,
        ) = general_grads(first_blocks, later_blocks, experts, hidden, routed)
        result = jnp.concatenate([output, output_high], axis=0)
        grad_tokens = jnp.concatenate([low_rows, crossed(high_rows).astype(F32)], axis=0)
    return (
        result,
        grad_tokens,
        small_grads[0],
        small_grads[1],
        key_grad,
        value_grad,
        router_grad,
        query_grad,
        out_grad,
        small_grads[2],
        small_grads[3],
        up_grad,
        up_bias_grad,
        down_grad,
        small_grads[4],
    )


def solution(mesh):
    rows = P(("dp", "tensor"), None)
    vector = P(("dp", "tensor"))
    in_specs = (
        rows,
        P("dp", None),
        rows,
        vector,
        vector,
        rows,
        rows,
        rows,
        P("tensor", "dp", None),
        P("tensor", None, "dp"),
        vector,
        vector,
        P("dp", "tensor"),
        vector,
        P("tensor", "dp"),
        vector,
    )
    out_specs = (
        rows,
        rows,
        vector,
        vector,
        rows,
        rows,
        rows,
        P("tensor", "dp", None),
        P("tensor", None, "dp"),
        vector,
        vector,
        P("dp", "tensor"),
        vector,
        P("tensor", "dp"),
        vector,
    )
    return jax.shard_map(
        per_device, mesh=mesh, in_specs=in_specs, out_specs=out_specs, check_vma=False
    )
```
